256 devices in a mesh: dp: 8 (over x, y_lo), section: 2 (over core), mp: 16 (over z, y_hi).
Axes of the slice: x: 4, y: 4 (y_hi: 2, y_lo: 2; y = y_hi * 2 + y_lo), z: 8, core: 2. Of those that a mesh axis runs over, the one named last changes fastest.
Arguments:
- features: bfloat16 [3, 128, 8192], P(None, 'dp', ('section', 'mp')), may hold values from -6 to 6
- fc_weight: bfloat16 [3, 8192, 8192], P(None, ('section', 'mp'), 'dp'), may hold values from -0.0390625 to 0.0390625
- head: bfloat16 [128256, 8192], P(('dp', 'section', 'mp')), may hold values from -8 to 8, as said below
- draft_gain: float32 [8192], P('dp'), may hold values from 0.1 to 1.9
- target_gain: float32 [8192], P(('section', 'mp')), may hold values from 0.1 to 1.9
- teacher_index: int32 [128, 32], replicated, may hold values from 0 to 128255, as said below
Outputs:
- weight_grad: bfloat16 [3, 8192, 8192], P(None, ('section', 'mp'), 'dp')
- gain_grad: float32 [8192], P('dp')
- token_loss: float32 [128], P('dp')
The draws below stay inside these ranges and needn't reach their ends.
Inputs may be any that keep to these rules, and one draw needn't show every extreme that they name: `teacher_index`: the 32 entries of a row are distinct. `head`: each row is a normal of scale 3 / sqrt(8192), truncated at six scales, times a factor of the row between 1 and 40, clipped to the range.
All inputs are finite; a program needn't handle non-finite values.
Results may differ from the reference program's by a relative error of at most 0.012.
The reference program's roundings to bfloat16 on the way (of `normed`, `teacher_in`, `logit_grad` and `joined_grad`) count: a program that leaves them out, or rounds other values in their place, can miss the bound.
Values may be sent and summed in bfloat16 or wider, within the bound.
A program may use at most 192 MiB of HBM per device.

```python
import math
import jax
import jax.numpy as jnp
from jax import lax

D = 8192
TOPK = 32
TOKENS = 128
VOCAB = 128256


def draw_head(key, part):
    key = jax.random.fold_in(key, 11)
    values = jax.random.truncated_normal(key, -6.0, 6.0, (VOCAB, D), jnp.float32) * (3.0 / math.sqrt(D))
    return values.astype(jnp.bfloat16)


def draw_teacher_index(key, part):
    key = jax.random.fold_in(key, 23)
    base_key = jax.random.fold_in(key, 1)
    offset_key = jax.random.fold_in(key, 2)
    spacing = VOCAB // TOPK
    base_value = jax.random.randint(base_key, (TOKENS, 1), 0, VOCAB)
    offsets = jax.random.randint(offset_key, (TOKENS, TOPK), 0, spacing)
    base_value = base_value.at[0, 0].set(VOCAB - 1).at[1, 0].set(0)
    offsets = offsets.at[0, 0].set(0).at[1, 0].set(0)
    steps_along = jnp.arange(TOPK, dtype=jnp.int32)[None, :] * spacing
    return ((base_value + steps_along + offsets) % VOCAB).astype(jnp.int32)


def levels(key, extent, cuts, smallest, top_value):
    def one(axis_at, blocks):
        draws = jax.random.uniform(jax.random.fold_in(jax.random.fold_in(key, 6), axis_at), (blocks,), jnp.float32, smallest / len(cuts), top_value / len(cuts))
        return jnp.repeat(jnp.exp(draws), extent[axis_at] // blocks).reshape((-1,) + (1,) * (len(extent) - axis_at - 1))

    level = one(*cuts[0])
    for cut in cuts[1:]:
        level = level * one(*cut)
    return level


def normal_values(own_key, shape, deviation, limit, pieces=(), held_as=jnp.bfloat16):
    values = deviation * jax.random.normal(own_key, shape, jnp.float32)
    if pieces:
        values = values * levels(own_key, shape, pieces, -0.22, 0.18)
    return jnp.clip(values, -limit, limit).astype(held_as)


def setup_inputs(seed: int = 0) -> dict:
    streams_of = jax.random.split(jax.random.key(seed), 7)
    return {
        "features": normal_values(streams_of[0], (3, TOKENS, D), 1.0, 6.0, ((1, 8), (2, 32))),
        "fc_weight": normal_values(streams_of[1], (3, D, D), (3 * D) ** -0.5, 0.0390625, ((1, 32), (2, 8))),
        "head": draw_head(jax.random.fold_in(streams_of[6], 71), 0),
        "draft_gain": jnp.clip(1.0 + 0.18 * jax.random.normal(streams_of[3], (D,), jnp.float32), 0.1, 1.9),
        "target_gain": jnp.clip(1.0 + 0.18 * jax.random.normal(streams_of[4], (D,), jnp.float32), 0.1, 1.9),
        "teacher_index": draw_teacher_index(jax.random.fold_in(streams_of[6], 71), 0),
    }


norm_eps = 1e-05

def reference(features, fc_weight, head, draft_gain, target_gain, teacher_index):
    joined = jnp.zeros((TOKENS, D), jnp.float32)
    for member in range(3):
        joined = joined + jnp.dot(features[member], fc_weight[member], preferred_element_type=jnp.float32)
    draft_scale = lax.rsqrt(lax.optimization_barrier(jnp.sum(joined * joined, axis=1)) / D + norm_eps)
    normed = (joined * draft_scale[:, None] * draft_gain[None, :]).astype(jnp.bfloat16)
    high_state = features[2].astype(jnp.float32)
    target_scale = lax.rsqrt(lax.optimization_barrier(jnp.sum(high_state * high_state, axis=1)) / D + norm_eps)
    teacher_in = (high_state * target_scale[:, None] * target_gain[None, :]).astype(jnp.bfloat16)
    dims = (((1,), (1,)), ((), ()))
    teacher_logits = lax.dot_general(teacher_in, head, dims, preferred_element_type=jnp.float32)
    draft_logits = lax.dot_general(normed, head, dims, preferred_element_type=jnp.float32)
    teacher_pick = jnp.take_along_axis(teacher_logits, teacher_index, axis=1)
    draft_pick = jnp.take_along_axis(draft_logits, teacher_index, axis=1)
    row_max = lax.optimization_barrier(jnp.max(draft_logits, axis=1))
    exp_total = lax.optimization_barrier(jnp.sum(jnp.exp(draft_logits - row_max[:, None]), axis=1))
    log_total = row_max + jnp.log(exp_total)
    teach_log = jax.nn.log_softmax(teacher_pick, axis=1)
    teach_prob = jnp.exp(teach_log)
    token_loss = lax.optimization_barrier(jnp.sum(teach_prob * (teach_log - draft_pick + log_total[:, None]), axis=1))
    draft_prob = jnp.exp(draft_logits - log_total[:, None])
    row_ids = jnp.broadcast_to(jnp.arange(TOKENS, dtype=jnp.int32)[:, None], teacher_index.shape)
    target_mass = jnp.zeros_like(draft_prob).at[row_ids, teacher_index].add(teach_prob)
    logit_grad = (draft_prob - target_mass).astype(jnp.bfloat16)
    hidden_grad = jnp.dot(logit_grad, head, preferred_element_type=jnp.float32)
    weighted = hidden_grad * draft_gain[None, :]
    inner = lax.optimization_barrier(jnp.sum(weighted * joined, axis=1))
    joined_grad = (draft_scale[:, None] * weighted - joined * (draft_scale ** 3 * inner / D)[:, None]).astype(jnp.bfloat16)
    gain_grad = lax.optimization_barrier(jnp.sum(hidden_grad * joined * draft_scale[:, None], axis=0))
    weight_grad = jnp.stack([jnp.dot(features[member].T, joined_grad, preferred_element_type=jnp.float32) for member in range(3)]).astype(jnp.bfloat16)
    return (weight_grad, gain_grad, token_loss)
```

```python
import jax
import jax.numpy as jnp
from jax import lax
from jax.experimental import pallas as pl
from jax.experimental.pallas import tpu as pltpu
from jax.sharding import PartitionSpec as P

D = 8192
EPS = 1e-05
VOC = 501
ROWS = 512
LOW = -1e30
F32 = jnp.float32
BF16 = jnp.bfloat16
MESH = pl.DeviceIdType.MESH

(A1, T1, TG, B0, TSQ, B1, T2, T3, S0, S1, C1, U1, U2, U3, V1, V2, V3, R1, R2, I0, I1, GM, JM, GS, JS) = range(25)
STAGES = 25


def kernel(
    feat, fc_hbm, head_hbm, dgain, tgain, index,
    feat_out, grad_out, gain_out, loss_out,
    head, fc, featg, part, brecv0, bsum, brecv1, traw, tgain_s, tgain_r, tsq_s, tsq_r, xt, xd, joined,
    sq_s, sq_r0, sq_s1, sq_r1, mask, lt, ld, placed, grad,
    us1, ur1, us2, ur2, us3, ur3, vs1, vr1, vs2, vr2, vs3, vr3,
    hf, hb, r0, r1s, r1r, r2s, r2r, in_s, in_r0, in_s1, in_r1, gp_s, gp_r, gs_s, gs_r, jg,
    load_sem, ssem, rsem, c2s, c2r, c3s, c3r, r0s, r0r,
):
    d = lax.axis_index("dp")
    c = lax.axis_index("section")
    m = lax.axis_index("mp")
    z = m // 2
    yh = m % 2
    p = d * 2 + yh
    sib = (d, 1 - c, m)

    load_fc = pltpu.make_async_copy(fc_hbm, fc, load_sem.at[0])
    load_head = pltpu.make_async_copy(head_hbm, head, load_sem.at[1])
    load_fc.start()
    load_head.start()

    barrier = pltpu.get_barrier_semaphore()
    pl.semaphore_signal(barrier, inc=1, device_id=sib, device_id_type=MESH)

    @pl.loop(1, 16)
    def _(i):
        pl.semaphore_signal(barrier, inc=1, device_id=(d, c, (m + i) % 16), device_id_type=MESH)

    @pl.loop(2, 16)
    def _(i):
        pl.semaphore_signal(
            barrier, inc=1, device_id=((d + i // 2) % 8, c, z * 2 + i % 2), device_id_type=MESH
        )

    pl.semaphore_wait(barrier, 30)

    def send(src, dst, stage, dev):
        pltpu.make_async_remote_copy(
            src_ref=src, dst_ref=dst, send_sem=ssem.at[stage], recv_sem=rsem.at[stage],
            device_id=dev, device_id_type=MESH,
        ).start()

    def arrived(ref, stage):
        pltpu.make_async_copy(ref, ref, rsem.at[stage]).wait()

    def sent(ref, stage):
        pltpu.make_async_copy(ref, ref, ssem.at[stage]).wait()

    def to_mp(src, dst, stage):
        @pl.loop(1, 16)
        def _(i):
            send(src, dst, stage, (d, c, (m + i) % 16))

    def to_dp(src, dst, stage):
        @pl.loop(1, 8)
        def _(i):
            send(src, dst, stage, ((d + i) % 8, c, m))

    def to_z(src, dst, stage):
        @pl.loop(1, 8)
        def _(i):
            send(src, dst, stage, (d, c, ((z + i) % 8) * 2 + yh))

    def to_plane(src, dst, stage):
        @pl.loop(1, 16)
        def _(i):
            q = (p + i) % 16
            send(src, dst, stage, (q // 2, c, z * 2 + q % 2))

    to_dp(feat, featg.at[d], A1)
    to_mp(feat.at[2], traw.at[m], T1)
    tgain_s[...] = jnp.broadcast_to(tgain[...], (8, 256))
    to_mp(tgain_s, tgain_r.at[m], TG)
    featg[d] = feat[...]
    traw[m] = feat[2]
    tgain_r[m] = tgain_s[...]

    start = ((d * 2 + c) * 16 + m) * VOC
    local = jnp.transpose(index[...]) - start

    @pl.loop(0, ROWS // 64)
    def _(i):
        rows = lax.broadcasted_iota(jnp.int32, (64, 128), 0) + i * 64
        hit = rows == local[0:1, :]
        for k in range(1, 32):
            hit = hit | (rows == local[k : k + 1, :])
        hit = hit & (rows < VOC)
        mask[pl.ds(pl.multiple_of(i * 64, 64), 64), :] = hit.astype(F32)

    load_fc.wait()
    arrived(featg.at[pl.ds(0, 7)], A1)
    for half in range(4):
        cols = slice(half * 256, half * 256 + 256)
        acc = jnp.dot(featg[:, 0].reshape(128, 256), fc[0, :, cols], preferred_element_type=F32)
        for j in (1, 2):
            acc += jnp.dot(featg[:, j].reshape(128, 256), fc[j, :, cols], preferred_element_type=F32)
        for zz in range(8):
            part[half // 2, zz * 2 + half % 2] = acc[zz * 16 : zz * 16 + 16]
    send(part.at[1 - c], brecv0, B0, sib)

    arrived(traw.at[pl.ds(0, 15)], T1)
    arrived(tgain_r.at[pl.ds(0, 15)], TG)
    tsq = jnp.zeros((16, 256), F32)
    for k in range(16):
        row = traw[k].astype(F32)
        tsq += row * row
    tsq = tsq[:, :128] + tsq[:, 128:]
    tsq_s[...] = tsq
    send(tsq_s, tsq_r, TSQ, sib)

    arrived(brecv0, B0)
    bsum[...] = part[c] + brecv0[...]

    @pl.loop(1, 16)
    def _(i):
        k = (m + i) % 16
        send(bsum.at[k], brecv1.at[m], B1, (d, c, k))

    brecv1[m] = bsum[m]

    arrived(tsq_r, TSQ)
    tsum = jnp.sum(tsq_s[...] + tsq_r[...], axis=1, keepdims=True)
    tscale = lax.rsqrt(tsum / D + EPS)
    for k in range(16):
        xt[c, d, k] = (traw[k].astype(F32) * tscale * tgain_r[k][0:1, :]).astype(BF16)
    to_dp(xt.at[c, d], xt.at[c, d], T2)

    arrived(brecv1.at[pl.ds(0, 15)], B1)
    js = brecv1[0]
    for k in range(1, 16):
        js += brecv1[k]
    joined[...] = js

    sq = js * js
    sq_s[...] = sq[:, :128] + sq[:, 128:]
    send(sq_s, sq_r0, S0, sib)
    arrived(sq_r0, S0)
    sq_s1[...] = sq_s[...] + sq_r0[...]
    to_plane(sq_s1, sq_r1.at[p], S1)
    sq_r1[p] = sq_s1[...]
    arrived(sq_r1.at[pl.ds(0, 15)], S1)
    total = sq_r1[0]
    for k in range(1, 16):
        total += sq_r1[k]
    dscale = lax.rsqrt(jnp.sum(total, axis=1, keepdims=True) / D + EPS)
    own_cols = pl.multiple_of((c * 2 + yh) * 256, 256)
    gain = dgain[:, pl.ds(own_cols, 256)]
    xd[c, p, z] = (js * dscale * gain).astype(BF16)
    to_z(xd.at[c, p, z], xd.at[c, p, z], C1)

    arrived(xt.at[c, pl.ds(0, 7)], T2)
    send(xt.at[c], xt.at[c], T3, sib)

    arrived(xd.at[c, p, pl.ds(0, 7)], C1)

    def c2(i):
        q = (p + i) % 16
        return pltpu.make_async_remote_copy(
            src_ref=xd.at[c, p], dst_ref=xd.at[c, p], send_sem=c2s, recv_sem=c2r.at[p],
            device_id=(q // 2, c, z * 2 + q % 2), device_id_type=MESH,
        )

    def c3(q):
        return pltpu.make_async_remote_copy(
            src_ref=xd.at[c, q], dst_ref=xd.at[c, q], send_sem=c3s, recv_sem=c3r,
            device_id=sib, device_id_type=MESH,
        )

    @pl.loop(1, 16)
    def _(i):
        c2(i).start()

    c3(p).start()

    load_head.wait()
    arrived(xt.at[1 - c], T3)
    lt[...] = jnp.zeros_like(lt)

    @pl.loop(0, 8)
    def _(i):
        cc = i // 4
        mm = (i % 4) * 4
        x = jnp.concatenate([xt[cc, :, mm + k].reshape(128, 256) for k in range(4)], axis=1)
        cols = pl.ds(pl.multiple_of(i * 1024, 1024), 1024)
        lt[...] += lax.dot_general(head[:, cols], x, (((1,), (1,)), ((), ())), preferred_element_type=F32)

    on = mask[0:VOC, :] > 0.5
    logits = jnp.where(on, lt[...], LOW)
    tmax = jnp.max(logits, axis=0, keepdims=True)
    away = logits - tmax
    e = jnp.where(on, jnp.exp(away), 0.0)
    tz = jnp.sum(e, axis=0, keepdims=True)
    tw = jnp.sum(jnp.where(on, e * away, 0.0), axis=0, keepdims=True)

    def rows_of(a, b, w):
        return jnp.concatenate([a, b, w, jnp.zeros((5, 128), F32)], axis=0)

    def merge_t(ref):
        a = ref[...]
        top = jnp.max(a[:, 0:1, :], axis=0)
        low = a[:, 0:1, :] - top[None]
        f = jnp.exp(low)
        zz = jnp.sum(f * a[:, 1:2, :], axis=0)
        ww = jnp.sum(f * (a[:, 2:3, :] + jnp.where(a[:, 1:2, :] > 0.0, low, 0.0) * a[:, 1:2, :]), axis=0)
        return top, zz, ww

    def merge_d(ref):
        a = ref[...]
        top = jnp.max(a[:, 0:1, :], axis=0)
        f = jnp.exp(a[:, 0:1, :] - top[None])
        return top, jnp.sum(f * a[:, 1:2, :], axis=0), jnp.sum(a[:, 2:3, :], axis=0)

    us1[...] = rows_of(tmax, tz, tw)
    to_z(us1, ur1.at[z], U1)
    ur1[z] = us1[...]

    @pl.loop(1, 16)
    def _(i):
        q = (p + 16 - i) % 16
        pltpu.make_async_copy(xd.at[c, q], xd.at[c, q], c2r.at[q]).wait()
        c3(q).start()

    arrived(ur1.at[pl.ds(0, 7)], U1)
    us2[...] = rows_of(*merge_t(ur1))
    to_plane(us2, ur2.at[p], U2)
    ur2[p] = us2[...]
    arrived(ur2.at[pl.ds(0, 15)], U2)
    us3[...] = rows_of(*merge_t(ur2))
    send(us3, ur3.at[c], U3, sib)
    ur3[c] = us3[...]

    pltpu.make_async_copy(xd.at[1 - c], xd.at[1 - c], c3r).wait()
    ld[...] = jnp.zeros_like(ld)

    @pl.loop(0, 8)
    def _(i):
        x = jnp.concatenate([xd[k // 2, i * 2 + k % 2].reshape(128, 256) for k in range(4)], axis=1)
        cols = pl.ds(pl.multiple_of(i * 1024, 1024), 1024)
        ld[...] += lax.dot_general(head[:, cols], x, (((1,), (1,)), ((), ())), preferred_element_type=F32)

    arrived(ur3.at[1 - c], U3)
    tmax, tz, tw = merge_t(ur3)
    tp = jnp.where(mask[0:VOC, :] > 0.5, jnp.exp(jnp.minimum(lt[...] - tmax, 0.0)) / tz, 0.0)
    placed[...] = tp
    teach = tw / tz - jnp.log(tz)

    logits = ld[...]
    dmax = jnp.max(logits, axis=0, keepdims=True)
    dz = jnp.sum(jnp.exp(logits - dmax), axis=0, keepdims=True)
    dw = jnp.sum(tp * logits, axis=0, keepdims=True)
    vs1[...] = rows_of(dmax, dz, dw)
    to_z(vs1, vr1.at[z], V1)
    vr1[z] = vs1[...]
    arrived(vr1.at[pl.ds(0, 7)], V1)
    vs2[...] = rows_of(*merge_d(vr1))
    to_plane(vs2, vr2.at[p], V2)
    vr2[p] = vs2[...]
    arrived(vr2.at[pl.ds(0, 15)], V2)
    vs3[...] = rows_of(*merge_d(vr2))
    send(vs3, vr3.at[c], V3, sib)
    vr3[c] = vs3[...]
    arrived(vr3.at[1 - c], V3)
    dmax, dz, dw = merge_d(vr3)
    log_total = dmax + jnp.log(dz)
    loss = teach - dw + log_total
    loss_out[...] = pltpu.roll(jnp.broadcast_to(loss, (8, 128)), (128 - d * 16) % 128, 1)

    g = jnp.exp(ld[...] - log_total) - placed[...]
    grad[...] = jnp.zeros_like(grad)
    grad[0:VOC, :] = g
    grad_rows = jnp.transpose(grad[...])[:, 0:VOC].astype(BF16)

    def r0_copy(dd):
        return pltpu.make_async_remote_copy(
            src_ref=hb.at[1 - c, pl.ds(dd * 2, 2)], dst_ref=r0.at[pl.ds(dd * 2, 2)],
            send_sem=r0s, recv_sem=r0r.at[dd], device_id=sib, device_id_type=MESH,
        )

    def compute(dd):
        for k in range(4):
            cols = pl.ds(pl.multiple_of(dd * 1024 + k * 256, 256), 256)
            h = jnp.dot(grad_rows, head[:, cols], preferred_element_type=F32)
            hf[k // 2, dd * 2 + k % 2] = h
            hb[k // 2, dd * 2 + k % 2] = h.astype(BF16)
        r0_copy(dd).start()

    def add_up(dd):
        pltpu.make_async_copy(r0.at[pl.ds(dd * 2, 2)], r0.at[pl.ds(dd * 2, 2)], r0r.at[dd]).wait()
        for k in range(2):
            q = dd * 2 + k
            r1s[q] = (hf[c, q] + r0[q].astype(F32)).astype(BF16)

    def to_peer(q):
        send(r1s.at[q], r1r.at[p], R1, (q // 2, c, z * 2 + q % 2))

    compute((d + 1) % 8)

    @pl.loop(2, 9)
    def _(i):
        compute((d + i) % 8)
        dd = (d + i - 1) % 8
        add_up(dd)
        to_peer(dd * 2)
        to_peer(dd * 2 + 1)

    add_up(d)
    to_peer(d * 2 + 1 - yh)
    r1r[p] = r1s[p]
    arrived(r1r.at[pl.ds(0, 15)], R1)
    for zz in range(8):
        acc = r1r[0, zz * 16 : zz * 16 + 16].astype(F32)
        for k in range(1, 16):
            acc += r1r[k, zz * 16 : zz * 16 + 16].astype(F32)
        r2s[zz] = acc.astype(BF16)

    @pl.loop(1, 8)
    def _(i):
        zz = (z + i) % 8
        send(r2s.at[zz], r2r.at[z], R2, (d, c, zz * 2 + yh))

    r2r[z] = r2s[z]
    arrived(r2r.at[pl.ds(0, 7)], R2)
    hidden = r2r[0].astype(F32)
    for k in range(1, 8):
        hidden += r2r[k].astype(F32)

    js = joined[...]
    weighted = hidden * gain
    inner = weighted * js
    in_s[...] = inner[:, :128] + inner[:, 128:]
    send(in_s, in_r0, I0, sib)
    gp = hidden * js * dscale
    gp_s[...] = gp[0:8] + gp[8:16]
    to_mp(gp_s, gp_r.at[m], GM)
    gp_r[m] = gp_s[...]
    arrived(in_r0, I0)
    in_s1[...] = in_s[...] + in_r0[...]
    to_plane(in_s1, in_r1.at[p], I1)
    in_r1[p] = in_s1[...]
    arrived(gp_r.at[pl.ds(0, 15)], GM)
    for k in range(2):
        acc = gp_r[k]
        for zz in range(1, 8):
            acc += gp_r[zz * 2 + k]
        gs_s[k] = acc
    send(gs_s, gs_r.at[c], GS, sib)
    gs_r[c] = gs_s[...]
    arrived(in_r1.at[pl.ds(0, 15)], I1)
    total = in_r1[0]
    for k in range(1, 16):
        total += in_r1[k]
    inner = jnp.sum(total, axis=1, keepdims=True)
    jg[c, m] = (dscale * weighted - js * (dscale * dscale * dscale * inner / D)).astype(BF16)
    to_mp(jg.at[c, m], jg.at[c, m], JM)
    feat_out[...] = jnp.concatenate(
        [jnp.concatenate([featg[k, j : j + 1] for k in range(8)], axis=1) for j in range(3)], axis=0
    )
    arrived(gs_r.at[1 - c], GS)
    for k in range(4):
        gain_out[:, k * 256 : k * 256 + 256] = jnp.sum(gs_r[k // 2, k % 2], axis=0, keepdims=True)
    arrived(jg.at[c, pl.ds(0, 15)], JM)
    send(jg.at[c], jg.at[c], JS, sib)
    arrived(jg.at[1 - c], JS)
    for k in range(4):
        for zz in range(8):
            grad_out[zz * 16 : zz * 16 + 16, k * 256 : k * 256 + 256] = jg[k // 2, zz * 2 + k % 2]

    sent(featg.at[pl.ds(0, 7)], A1)
    sent(traw.at[pl.ds(0, 15)], T1)
    sent(tgain_r.at[pl.ds(0, 15)], TG)
    sent(brecv0, B0)
    sent(tsq_s, TSQ)
    sent(bsum.at[pl.ds(0, 15)], B1)
    sent(xt.at[c, pl.ds(0, 7)], T2)
    sent(xt.at[c], T3)
    sent(sq_s, S0)
    sent(sq_r1.at[pl.ds(0, 15)], S1)
    sent(xd.at[c, p, pl.ds(0, 7)], C1)
    pltpu.make_async_copy(xd.at[c, pl.ds(0, 15)], xd.at[c, pl.ds(0, 15)], c2s).wait()
    pltpu.make_async_copy(xd.at[c], xd.at[c], c3s).wait()
    sent(ur1.at[pl.ds(0, 7)], U1)
    sent(ur2.at[pl.ds(0, 15)], U2)
    sent(us3, U3)
    sent(vr1.at[pl.ds(0, 7)], V1)
    sent(vr2.at[pl.ds(0, 15)], V2)
    sent(vs3, V3)
    pltpu.make_async_copy(r0, r0, r0s).wait()
    sent(r1r.at[pl.ds(0, 15)], R1)
    sent(r2r.at[pl.ds(0, 7)], R2)
    sent(in_s, I0)
    sent(in_r1.at[pl.ds(0, 15)], I1)
    sent(gp_r.at[pl.ds(0, 15)], GM)
    sent(gs_s, GS)
    sent(jg.at[c, pl.ds(0, 15)], JM)
    sent(jg.at[c], JS)


def shards(features, fc_weight, head, draft_gain, target_gain, teacher_index):
    vmem = pl.BlockSpec(memory_space=pltpu.VMEM)
    hbm = pl.BlockSpec(memory_space=pl.ANY)
    V = pltpu.VMEM
    tile = V((16, 128), F32)
    tiles = V((16, 16, 128), F32)
    stat = [V((8, 128), F32), V((8, 8, 128), F32), V((8, 128), F32), V((16, 8, 128), F32), V((8, 128), F32), V((2, 8, 128), F32)]
    feat_all, joined_grad, gain_grad, loss = pl.pallas_call(
        kernel,
        out_shape=(
            jax.ShapeDtypeStruct((3, 128, 256), BF16),
            jax.ShapeDtypeStruct((128, 1024), BF16),
            jax.ShapeDtypeStruct((1, 1024), F32),
            jax.ShapeDtypeStruct((8, 128), F32),
        ),
        in_specs=[vmem, hbm, hbm, vmem, vmem, vmem],
        out_specs=(vmem, vmem, vmem, vmem),
        scratch_shapes=[
            V((VOC, D), BF16),
            V((3, 256, 1024), BF16),
            V((8, 3, 16, 256), BF16),
            V((2, 16, 16, 256), F32),
            V((16, 16, 256), F32),
            V((16, 16, 256), F32),
            V((16, 16, 256), F32),
            V((16, 16, 256), BF16),
            V((8, 256), F32),
            V((16, 8, 256), F32),
            tile,
            tile,
            V((2, 8, 16, 16, 256), BF16),
            V((2, 16, 8, 16, 256), BF16),
            V((16, 256), F32),
            tile, tile, tile, tiles,
            V((ROWS, 128), F32),
            V((VOC, 128), F32),
            V((VOC, 128), F32),
            V((VOC, 128), F32),
            V((ROWS, 128), F32),
            *stat,
            *stat,
            V((2, 16, 128, 256), F32),
            V((2, 16, 128, 256), BF16),
            V((16, 128, 256), BF16),
            V((16, 128, 256), BF16),
            V((16, 128, 256), BF16),
            V((8, 16, 256), BF16),
            V((8, 16, 256), BF16),
            tile, tile, tile, tiles,
            V((8, 256), F32),
            V((16, 8, 256), F32),
            V((2, 8, 256), F32),
            V((2, 2, 8, 256), F32),
            V((2, 16, 16, 256), BF16),
            pltpu.SemaphoreType.DMA((2,)),
            pltpu.SemaphoreType.DMA((STAGES,)),
            pltpu.SemaphoreType.DMA((STAGES,)),
            pltpu.SemaphoreType.DMA,
            pltpu.SemaphoreType.DMA((16,)),
            pltpu.SemaphoreType.DMA,
            pltpu.SemaphoreType.DMA,
            pltpu.SemaphoreType.DMA,
            pltpu.SemaphoreType.DMA((8,)),
        ],
        compiler_params=pltpu.CompilerParams(
            collective_id=0, has_side_effects=True, vmem_limit_bytes=52 * 2**20
        ),
        cost_estimate=pl.CostEstimate(flops=3_600_000_000, bytes_accessed=12_000_000, transcendentals=200_000),
    )(features, fc_weight, head, draft_gain.reshape(1, 1024), target_gain.reshape(1, 256), teacher_index)
    weight_grad = jnp.einsum("jtf,tc->jfc", feat_all, joined_grad, preferred_element_type=F32)
    return (weight_grad.astype(BF16), gain_grad.reshape(1024), loss[0, :16])


def solution(mesh):
    return jax.shard_map(
        shards,
        mesh=mesh,
        in_specs=(
            P(None, "dp", ("section", "mp")),
            P(None, ("section", "mp"), "dp"),
            P(("dp", "section", "mp"), None),
            P("dp"),
            P(("section", "mp")),
            P(),
        ),
        out_specs=(P(None, ("section", "mp"), "dp"), P("dp"), P("dp")),
        check_vma=False,
    )
```

```python
import jax
import jax.numpy as jnp
from jax import lax
from jax.experimental import pallas as pl
from jax.experimental.pallas import tpu as pltpu
from jax.sharding import PartitionSpec as P

D = 8192
EPS = 1e-05
VOC = 501
ROWS = 512
LOW = -1e30
F32 = jnp.float32
BF16 = jnp.bfloat16
MESH = pl.DeviceIdType.MESH

(A1, T1, TG, TY, TX, T3, TGS, B0, B1, S1, C1, U1, U2, V1, V2, R1, R2, I1, GM, GS, JM, JS) = range(22)
STAGES = 22


def kernel(
    feat, fc_hbm, head_hbm, dgain_hbm, tgain_hbm, index_hbm,
    feat_out, grad_out, gain_out, loss_out,
    head, fc, featg, dgain, index, part, brecv0, bsum, brecv1, xr, tg, xd, joined,
    sq_s, sq_r, mask, lt, ld, placed, grad,
    us1, ur1, us2, ur2, vs1, vr1, vs2, vr2,
    hf, hb, r0, r1s, r1r, r2s, r2r, in_s, in_r, gp_s, gp_r, gs_s, gs_r, jg,
    load_sem, ssem, rsem, c2s, c2r, c3s, c3r, r0s, r0r,
):
    d = lax.axis_index("dp")
    c = lax.axis_index("section")
    m = lax.axis_index("mp")
    z = m // 2
    yh = m % 2
    p = d * 2 + yh
    sib = (d, 1 - c, m)

    loads = [
        pltpu.make_async_copy(src, dst, load_sem.at[k])
        for k, (src, dst) in enumerate((
            (feat, featg.at[d]), (feat.at[2], xr.at[c, d, m]), (tgain_hbm, tg.at[c, m]), (index_hbm, index),
            (dgain_hbm, dgain), (fc_hbm, fc), (head_hbm, head),
        ))
    ]
    for load in loads:
        load.start()
    load_feat, load_high, load_tg, load_index, load_dg, load_fc, load_head = loads

    barrier = pltpu.get_barrier_semaphore()

    @pl.loop(1, 16)
    def _(i):
        pl.semaphore_signal(barrier, inc=1, device_id=(d, c, (m + i) % 16), device_id_type=MESH)

    @pl.loop(1, 32)
    def _(i):
        k = (p * 2 + c + i) % 32
        pl.semaphore_signal(
            barrier, inc=1, device_id=(k // 4, k % 2, z * 2 + k // 2 % 2), device_id_type=MESH
        )

    pl.semaphore_wait(barrier, 46)

    def send(src, dst, stage, dev):
        pltpu.make_async_remote_copy(
            src_ref=src, dst_ref=dst, send_sem=ssem.at[stage], recv_sem=rsem.at[stage],
            device_id=dev, device_id_type=MESH,
        ).start()

    volume = {
        A1: featg.at[pl.ds(0, 7)], T1: xr.at[c, d, pl.ds(0, 15)], TG: tg.at[c, pl.ds(0, 15)], TY: xr.at[c, d],
        TX: xr.at[c, pl.ds(0, 6)], T3: xr.at[c], TGS: tg.at[c], B0: brecv0, B1: bsum.at[pl.ds(0, 15)],
        S1: sq_r.at[pl.ds(0, 31)], C1: xd.at[c, p, pl.ds(0, 7)], U1: ur1.at[pl.ds(0, 15)], U2: ur2.at[pl.ds(0, 15)],
        V1: vr1.at[pl.ds(0, 15)], V2: vr2.at[pl.ds(0, 15)], R1: r1r.at[pl.ds(0, 15)], R2: r2r.at[pl.ds(0, 7)],
        I1: in_r.at[pl.ds(0, 31)], GM: gp_r.at[pl.ds(0, 15)], GS: gs_s, JM: jg.at[c, pl.ds(0, 15)], JS: jg.at[c],
    }

    def arrived(stage):
        pltpu.make_async_copy(volume[stage], volume[stage], rsem.at[stage]).wait()

    def sent(stage):
        pltpu.make_async_copy(volume[stage], volume[stage], ssem.at[stage]).wait()

    def to_mp(src, dst, stage):
        @pl.loop(1, 16)
        def _(i):
            send(src, dst, stage, (d, c, (m + i) % 16))

    def to_dp(src, dst, stage):
        @pl.loop(1, 8)
        def _(i):
            send(src, dst, stage, ((d + i) % 8, c, m))

    def to_dp_both(src, dst, stage):
        @pl.loop(1, 16)
        def _(i):
            k = (d * 2 + c + i) % 16
            send(src, dst, stage, (k // 2, k % 2, m))

    def to_z(src, dst, stage):
        @pl.loop(1, 8)
        def _(i):
            send(src, dst, stage, (d, c, ((z + i) % 8) * 2 + yh))

    def to_plane_both(src, dst, stage):
        @pl.loop(1, 32)
        def _(i):
            k = (p * 2 + c + i) % 32
            send(src, dst, stage, (k // 4, k % 2, z * 2 + k // 2 % 2))

    to_dp(feat, featg.at[d], A1)
    to_mp(feat.at[2], xr.at[c, d, m], T1)
    to_mp(tgain_hbm, tg.at[c, m], TG)

    start = ((d * 2 + c) * 16 + m) * VOC
    load_index.wait()

    @pl.loop(0, ROWS // 64)
    def _(i):
        rows = lax.broadcasted_iota(jnp.int32, (64, 128), 0) + (i * 64 + start)
        hit = rows == index[0:1, :]
        for k in range(1, 32):
            hit = hit | (rows == index[k : k + 1, :])
        hit = hit & (rows < start + VOC)
        mask[pl.ds(pl.multiple_of(i * 64, 64), 64), :] = hit.astype(F32)

    load_fc.wait()
    load_feat.wait()
    arrived(A1)
    load_high.wait()
    arrived(T1)
    other = d + 1 - 2 * (d % 2)
    send(xr.at[c, d], xr.at[c, d], TY, (other, c, m))
    for half in range(4):
        cols = slice(half * 256, half * 256 + 256)
        acc = jnp.dot(featg[:, 0].reshape(128, 256), fc[0, :, cols], preferred_element_type=F32)
        for j in (1, 2):
            acc += jnp.dot(featg[:, j].reshape(128, 256), fc[j, :, cols], preferred_element_type=F32)
        for zz in range(8):
            part[half // 2, zz * 2 + half % 2] = acc[zz * 16 : zz * 16 + 16]
    send(part.at[1 - c], brecv0, B0, sib)

    arrived(TY)
    pair = xr.at[c, pl.ds(d - d % 2, 2)]

    @pl.loop(1, 4)
    def _(i):
        send(pair, pair, TX, ((d + 2 * i) % 8, c, m))

    arrived(B0)
    bsum[...] = part[c] + brecv0[...]

    @pl.loop(1, 16)
    def _(i):
        k = (m + i) % 16
        send(bsum.at[k], brecv1.at[m], B1, (d, c, k))

    brecv1[m] = bsum[m]
    arrived(B1)
    js = brecv1[0]
    for k in range(1, 16):
        js += brecv1[k]
    joined[...] = js

    eye = lax.broadcasted_iota(jnp.int32, (16, 128), 0) == lax.broadcasted_iota(jnp.int32, (16, 128), 1)

    def as_row(x):
        return jnp.sum(jnp.where(eye, jnp.sum(x, axis=1, keepdims=True), 0.0), axis=0, keepdims=True)

    def as_column(ref):
        return jnp.sum(jnp.where(eye, jnp.sum(ref[...], axis=0), 0.0), axis=1, keepdims=True)

    sq_s[...] = as_row(js * js)
    to_plane_both(sq_s, sq_r.at[p * 2 + c], S1)
    sq_r[p * 2 + c] = sq_s[...]
    arrived(S1)
    dscale = lax.rsqrt(as_column(sq_r) / D + EPS)
    load_dg.wait()
    own_cols = pl.multiple_of((c * 2 + yh) * 256, 256)
    gain = dgain[:, pl.ds(own_cols, 256)]
    xd[c, p, z] = (js * dscale * gain).astype(BF16)
    to_z(xd.at[c, p, z], xd.at[c, p, z], C1)

    arrived(TX)
    send(xr.at[c], xr.at[c], T3, sib)
    load_tg.wait()
    arrived(TG)
    send(tg.at[c], tg.at[c], TGS, sib)

    arrived(C1)

    def c2(i):
        q = (p + i) % 16
        return pltpu.make_async_remote_copy(
            src_ref=xd.at[c, p], dst_ref=xd.at[c, p], send_sem=c2s, recv_sem=c2r.at[p],
            device_id=(q // 2, c, z * 2 + q % 2), device_id_type=MESH,
        )

    def c3(q):
        return pltpu.make_async_remote_copy(
            src_ref=xd.at[c, q], dst_ref=xd.at[c, q], send_sem=c3s, recv_sem=c3r,
            device_id=sib, device_id_type=MESH,
        )

    @pl.loop(1, 16)
    def _(i):
        c2(i).start()

    c3(p).start()

    arrived(T3)
    arrived(TGS)

    def add_squares(i, acc):
        x = xr[i // 16, :, i % 16].reshape(128, 256).astype(F32)
        x = x * x
        return acc + x[:, :128] + x[:, 128:]

    squares = lax.fori_loop(0, 32, add_squares, jnp.zeros((128, 128), F32))
    tscale = lax.rsqrt(jnp.sum(squares, axis=1, keepdims=True) / D + EPS)

    load_head.wait()
    lt[...] = jnp.zeros_like(lt)

    @pl.loop(0, 8)
    def _(i):
        cc = i // 4
        mm = (i % 4) * 4
        x = jnp.concatenate(
            [
                (xr[cc, :, mm + k].reshape(128, 256).astype(F32) * tscale * tg[cc, mm + k]).astype(BF16)
                for k in range(4)
            ],
            axis=1,
        )
        cols = pl.ds(pl.multiple_of(i * 1024, 1024), 1024)
        lt[...] += lax.dot_general(head[:, cols], x, (((1,), (1,)), ((), ())), preferred_element_type=F32)

    on = mask[0:VOC, :] > 0.5
    logits = jnp.where(on, lt[...], LOW)
    tmax = jnp.max(logits, axis=0, keepdims=True)
    away = logits - tmax
    e = jnp.where(on, jnp.exp(away), 0.0)
    tz = jnp.sum(e, axis=0, keepdims=True)
    tw = jnp.sum(jnp.where(on, e * away, 0.0), axis=0, keepdims=True)

    def rows_of(a, b, w):
        return jnp.concatenate([a, b, w, jnp.zeros((1, 128), F32)], axis=0)

    def merge_t(ref):
        a = ref[...]
        top = jnp.max(a[:, 0:1, :], axis=0)
        low = a[:, 0:1, :] - top[None]
        f = jnp.exp(low)
        zz = jnp.sum(f * a[:, 1:2, :], axis=0)
        ww = jnp.sum(f * (a[:, 2:3, :] + jnp.where(a[:, 1:2, :] > 0.0, low, 0.0) * a[:, 1:2, :]), axis=0)
        return top, zz, ww

    def merge_d(ref):
        a = ref[...]
        top = jnp.max(a[:, 0:1, :], axis=0)
        f = jnp.exp(a[:, 0:1, :] - top[None])
        return top, jnp.sum(f * a[:, 1:2, :], axis=0), jnp.sum(a[:, 2:3, :], axis=0)

    us1[...] = rows_of(tmax, tz, tw)
    to_mp(us1, ur1.at[m], U1)
    ur1[m] = us1[...]

    @pl.loop(1, 12)
    def _(i):
        q = (p + 16 - i) % 16
        pltpu.make_async_copy(xd.at[c, q], xd.at[c, q], c2r.at[q]).wait()
        c3(q).start()

    arrived(U1)
    us2[...] = rows_of(*merge_t(ur1))
    to_dp_both(us2, ur2.at[d * 2 + c], U2)
    ur2[d * 2 + c] = us2[...]

    @pl.loop(12, 16)
    def _(i):
        q = (p + 16 - i) % 16
        pltpu.make_async_copy(xd.at[c, q], xd.at[c, q], c2r.at[q]).wait()
        c3(q).start()

    pltpu.make_async_copy(xd.at[1 - c], xd.at[1 - c], c3r).wait()
    ld[...] = jnp.zeros_like(ld)

    @pl.loop(0, 8)
    def _(i):
        x = jnp.concatenate([xd[k // 2, i * 2 + k % 2].reshape(128, 256) for k in range(4)], axis=1)
        cols = pl.ds(pl.multiple_of(i * 1024, 1024), 1024)
        ld[...] += lax.dot_general(head[:, cols], x, (((1,), (1,)), ((), ())), preferred_element_type=F32)

    arrived(U2)
    tmax, tz, tw = merge_t(ur2)
    tp = jnp.where(mask[0:VOC, :] > 0.5, jnp.exp(jnp.minimum(lt[...] - tmax, 0.0)) / tz, 0.0)
    placed[...] = tp
    teach = tw / tz - jnp.log(tz)

    logits = ld[...]
    dmax = jnp.max(logits, axis=0, keepdims=True)
    dz = jnp.sum(jnp.exp(logits - dmax), axis=0, keepdims=True)
    dw = jnp.sum(tp * logits, axis=0, keepdims=True)
    vs1[...] = rows_of(dmax, dz, dw)
    to_mp(vs1, vr1.at[m], V1)
    vr1[m] = vs1[...]
    arrived(V1)
    vs2[...] = rows_of(*merge_d(vr1))
    to_dp_both(vs2, vr2.at[d * 2 + c], V2)
    vr2[d * 2 + c] = vs2[...]
    arrived(V2)
    dmax, dz, dw = merge_d(vr2)
    log_total = dmax + jnp.log(dz)
    loss = teach - dw + log_total
    loss_out[...] = pltpu.roll(jnp.broadcast_to(loss, (8, 128)), (128 - d * 16) % 128, 1)

    g = jnp.exp(ld[...] - log_total) - placed[...]
    grad[...] = jnp.zeros_like(grad)
    grad[0:VOC, :] = g
    grad_rows = jnp.transpose(grad[...])[:, 0:VOC].astype(BF16)

    def r0_copy(dd):
        return pltpu.make_async_remote_copy(
            src_ref=hb.at[1 - c, pl.ds(dd * 2, 2)], dst_ref=r0.at[pl.ds(dd * 2, 2)],
            send_sem=r0s, recv_sem=r0r.at[dd], device_id=sib, device_id_type=MESH,
        )

    def compute(dd):
        for k in range(4):
            cols = pl.ds(pl.multiple_of(dd * 1024 + k * 256, 256), 256)
            h = jnp.dot(grad_rows, head[:, cols], preferred_element_type=F32)
            hf[k // 2, dd * 2 + k % 2] = h
            hb[k // 2, dd * 2 + k % 2] = h.astype(BF16)
        r0_copy(dd).start()

    def add_up(dd):
        pltpu.make_async_copy(r0.at[pl.ds(dd * 2, 2)], r0.at[pl.ds(dd * 2, 2)], r0r.at[dd]).wait()
        for k in range(2):
            q = dd * 2 + k
            r1s[q] = (hf[c, q] + r0[q].astype(F32)).astype(BF16)

    def to_peer(q):
        send(r1s.at[q], r1r.at[p], R1, (q // 2, c, z * 2 + q % 2))

    compute((d + 1) % 8)

    @pl.loop(2, 9)
    def _(i):
        compute((d + i) % 8)
        dd = (d + i - 1) % 8
        add_up(dd)
        to_peer(dd * 2)
        to_peer(dd * 2 + 1)

    add_up(d)
    to_peer(d * 2 + 1 - yh)
    r1r[p] = r1s[p]
    arrived(R1)
    for zz in range(8):
        acc = r1r[0, zz * 16 : zz * 16 + 16].astype(F32)
        for k in range(1, 16):
            acc += r1r[k, zz * 16 : zz * 16 + 16].astype(F32)
        r2s[zz] = acc.astype(BF16)

    @pl.loop(1, 8)
    def _(i):
        zz = (z + i) % 8
        send(r2s.at[zz], r2r.at[z], R2, (d, c, zz * 2 + yh))

    r2r[z] = r2s[z]
    arrived(R2)
    hidden = r2r[0].astype(F32)
    for k in range(1, 8):
        hidden += r2r[k].astype(F32)

    js = joined[...]
    weighted = hidden * gain
    in_s[...] = as_row(weighted * js)
    to_plane_both(in_s, in_r.at[p * 2 + c], I1)
    in_r[p * 2 + c] = in_s[...]
    gp_s[...] = jnp.sum(hidden * js * dscale, axis=0, keepdims=True)
    to_mp(gp_s, gp_r.at[m], GM)
    gp_r[m] = gp_s[...]
    arrived(I1)
    inner = as_column(in_r)
    jg[c, m] = (dscale * weighted - js * (dscale * dscale * dscale * inner / D)).astype(BF16)
    to_mp(jg.at[c, m], jg.at[c, m], JM)
    arrived(GM)
    for k in range(2):
        acc = gp_r[k]
        for zz in range(1, 8):
            acc += gp_r[zz * 2 + k]
        gs_s[k] = acc
    send(gs_s, gs_r.at[c], GS, sib)
    gs_r[c] = gs_s[...]
    feat_out[...] = jnp.concatenate(
        [jnp.concatenate([featg[k, j : j + 1] for k in range(8)], axis=1) for j in range(3)], axis=0
    )
    arrived(GS)
    for k in range(4):
        gain_out[:, k * 256 : k * 256 + 256] = gs_r[k // 2, k % 2]
    arrived(JM)
    send(jg.at[c], jg.at[c], JS, sib)
    arrived(JS)
    for k in range(4):
        for zz in range(8):
            grad_out[zz * 16 : zz * 16 + 16, k * 256 : k * 256 + 256] = jg[k // 2, zz * 2 + k % 2]

    for stage in volume:
        sent(stage)
    pltpu.make_async_copy(xd.at[c, pl.ds(0, 15)], xd.at[c, pl.ds(0, 15)], c2s).wait()
    pltpu.make_async_copy(xd.at[c], xd.at[c], c3s).wait()
    pltpu.make_async_copy(r0, r0, r0s).wait()


def shards(features, fc_weight, head, draft_gain, target_gain, teacher_index):
    vmem = pl.BlockSpec(memory_space=pltpu.VMEM)
    hbm = pl.BlockSpec(memory_space=pl.ANY)
    V = pltpu.VMEM
    stat = [V((4, 128), F32), V((16, 4, 128), F32)] * 2
    feat_all, joined_grad, gain_grad, loss = pl.pallas_call(
        kernel,
        out_shape=(
            jax.ShapeDtypeStruct((3, 128, 256), BF16),
            jax.ShapeDtypeStruct((128, 1024), BF16),
            jax.ShapeDtypeStruct((1, 1024), F32),
            jax.ShapeDtypeStruct((8, 128), F32),
        ),
        in_specs=[hbm] * 6,
        out_specs=(vmem, vmem, vmem, vmem),
        scratch_shapes=[
            V((VOC, D), BF16),
            V((3, 256, 1024), BF16),
            V((8, 3, 16, 256), BF16),
            V((1, 1024), F32),
            V((32, 128), jnp.int32),
            V((2, 16, 16, 256), F32),
            V((16, 16, 256), F32),
            V((16, 16, 256), F32),
            V((16, 16, 256), F32),
            V((2, 8, 16, 16, 256), BF16),
            V((2, 16, 1, 256), F32),
            V((2, 16, 8, 16, 256), BF16),
            V((16, 256), F32),
            V((1, 128), F32),
            V((32, 1, 128), F32),
            V((ROWS, 128), F32),
            V((VOC, 128), F32),
            V((VOC, 128), F32),
            V((VOC, 128), F32),
            V((ROWS, 128), F32),
            *stat,
            *stat,
            V((2, 16, 128, 256), F32),
            V((2, 16, 128, 256), BF16),
            V((16, 128, 256), BF16),
            V((16, 128, 256), BF16),
            V((16, 128, 256), BF16),
            V((8, 16, 256), BF16),
            V((8, 16, 256), BF16),
            V((1, 128), F32),
            V((32, 1, 128), F32),
            V((1, 256), F32),
            V((16, 1, 256), F32),
            V((2, 1, 256), F32),
            V((2, 2, 1, 256), F32),
            V((2, 16, 16, 256), BF16),
            pltpu.SemaphoreType.DMA((7,)),
            pltpu.SemaphoreType.DMA((STAGES,)),
            pltpu.SemaphoreType.DMA((STAGES,)),
            pltpu.SemaphoreType.DMA,
            pltpu.SemaphoreType.DMA((16,)),
            pltpu.SemaphoreType.DMA,
            pltpu.SemaphoreType.DMA,
            pltpu.SemaphoreType.DMA,
            pltpu.SemaphoreType.DMA((8,)),
        ],
        compiler_params=pltpu.CompilerParams(
            collective_id=0, has_side_effects=True, vmem_limit_bytes=60 * 2**20
        ),
        cost_estimate=pl.CostEstimate(flops=3_600_000_000, bytes_accessed=12_000_000, transcendentals=200_000),
    )(features, fc_weight, head, draft_gain.reshape(1, 1024), target_gain.reshape(1, 256), teacher_index.T)
    weight_grad = jnp.einsum("jtf,tc->jfc", feat_all, joined_grad, preferred_element_type=F32)
    return (weight_grad.astype(BF16), gain_grad.reshape(1024), loss[0, :16])


def solution(mesh):
    return jax.shard_map(
        shards,
        mesh=mesh,
        in_specs=(
            P(None, "dp", ("section", "mp")),
            P(None, ("section", "mp"), "dp"),
            P(("dp", "section", "mp"), None),
            P("dp"),
            P(("section", "mp")),
            P(),
        ),
        out_specs=(P(None, ("section", "mp"), "dp"), P("dp"), P("dp")),
        check_vma=False,
    )
```

```python
import jax
import jax.numpy as jnp
from jax import lax
from jax.experimental import pallas as pl
from jax.experimental.pallas import tpu as pltpu
from jax.sharding import PartitionSpec as P

D = 8192
EPS = 1e-05
VOC = 501
ROWS = 512
LOW = -1e30
F32 = jnp.float32
BF16 = jnp.bfloat16
MESH = pl.DeviceIdType.MESH

(A1, T1, TG, TY, TX, TX2, T3, TGS, B0, B1, S1, C1, U1, U2, V1, V2, R1, R2, GM, GS, JM, JS) = range(22)
STAGES = 22


def kernel(
    feat, fc_hbm, head_hbm, dgain_hbm, tgain_hbm, index_hbm,
    feat_out, grad_out, gain_out, loss_out,
    head, fc, featg, dgain, index, part, brecv0, bsum, brecv1, xr, tg, xd, joined,
    sq_s, sq_r, mask, lt, ld, placed, grad,
    us1, ur1, us2, ur2, vs1, vr1, vs2, vr2,
    hf, hb, r0, r1s, r1r, r2s, r2r, gp_s, gp_r, gs_s, gs_r, jg,
    load_sem, ssem, rsem, c2s, c2r, c3s, c3r, r0s, r0r,
):
    d = lax.axis_index("dp")
    c = lax.axis_index("section")
    m = lax.axis_index("mp")
    z = m // 2
    yh = m % 2
    p = d * 2 + yh
    sib = (d, 1 - c, m)

    loads = [
        pltpu.make_async_copy(src, dst, load_sem.at[k])
        for k, (src, dst) in enumerate((
            (feat, featg.at[d]), (feat.at[2], xr.at[c, d, m]), (tgain_hbm, tg.at[c, m]), (index_hbm, index),
            (dgain_hbm, dgain), (fc_hbm, fc), (head_hbm, head),
        ))
    ]
    for load in loads:
        load.start()
    load_feat, load_high, load_tg, load_index, load_dg, load_fc, load_head = loads

    barrier = pltpu.get_barrier_semaphore()

    @pl.loop(1, 16)
    def _(i):
        pl.semaphore_signal(barrier, inc=1, device_id=(d, c, (m + i) % 16), device_id_type=MESH)

    @pl.loop(1, 32)
    def _(i):
        k = (p * 2 + c + i) % 32
        pl.semaphore_signal(
            barrier, inc=1, device_id=(k // 4, k % 2, z * 2 + k // 2 % 2), device_id_type=MESH
        )

    pl.semaphore_wait(barrier, 46)

    def send(src, dst, stage, dev):
        pltpu.make_async_remote_copy(
            src_ref=src, dst_ref=dst, send_sem=ssem.at[stage], recv_sem=rsem.at[stage],
            device_id=dev, device_id_type=MESH,
        ).start()

    volume = {
        A1: featg.at[pl.ds(0, 7)], T1: xr.at[c, d, pl.ds(0, 15)], TG: tg.at[c, pl.ds(0, 15)], TY: xr.at[c, d],
        TX: xr.at[c, pl.ds(0, 6), pl.ds(0, 8)], TX2: xr.at[c, pl.ds(0, 6), pl.ds(0, 8)], T3: xr.at[c], TGS: tg.at[c], B0: brecv0, B1: bsum.at[pl.ds(0, 15)],
        S1: sq_r.at[pl.ds(0, 31)], C1: xd.at[c, p, pl.ds(0, 7)], U1: ur1.at[pl.ds(0, 15)], U2: ur2.at[pl.ds(0, 15)],
        V1: vr1.at[pl.ds(0, 15)], V2: vr2.at[pl.ds(0, 15)], R1: r1r.at[pl.ds(0, 15)], R2: r2r.at[pl.ds(0, 7)],
        GM: gp_r.at[pl.ds(0, 15)], GS: gs_s, JM: jg.at[c, pl.ds(0, 15)], JS: jg.at[c],
    }

    def arrived(stage):
        pltpu.make_async_copy(volume[stage], volume[stage], rsem.at[stage]).wait()

    def sent(stage):
        pltpu.make_async_copy(volume[stage], volume[stage], ssem.at[stage]).wait()

    def to_mp(src, dst, stage):
        @pl.loop(1, 16)
        def _(i):
            send(src, dst, stage, (d, c, (m + i) % 16))

    def to_dp(src, dst, stage):
        @pl.loop(1, 8)
        def _(i):
            send(src, dst, stage, ((d + i) % 8, c, m))

    def to_dp_both(src, dst, stage):
        @pl.loop(1, 16)
        def _(i):
            k = (d * 2 + c + i) % 16
            send(src, dst, stage, (k // 2, k % 2, m))

    def to_z(src, dst, stage):
        @pl.loop(1, 8)
        def _(i):
            send(src, dst, stage, (d, c, ((z + i) % 8) * 2 + yh))

    def to_plane_both(src, dst, stage):
        @pl.loop(1, 32)
        def _(i):
            k = (p * 2 + c + i) % 32
            send(src, dst, stage, (k // 4, k % 2, z * 2 + k // 2 % 2))

    to_dp(feat, featg.at[d], A1)
    to_mp(feat.at[2], xr.at[c, d, m], T1)
    to_mp(tgain_hbm, tg.at[c, m], TG)

    start = ((d * 2 + c) * 16 + m) * VOC
    load_index.wait()

    @pl.loop(0, ROWS // 64)
    def _(i):
        rows = lax.broadcasted_iota(jnp.int32, (64, 128), 0) + (i * 64 + start)
        hit = rows == index[0:1, :]
        for k in range(1, 32):
            hit = hit | (rows == index[k : k + 1, :])
        hit = hit & (rows < start + VOC)
        mask[pl.ds(pl.multiple_of(i * 64, 64), 64), :] = hit.astype(F32)

    load_fc.wait()
    load_feat.wait()
    arrived(A1)
    for half in range(4):
        cols = slice(half * 256, half * 256 + 256)
        acc = jnp.dot(featg[:, 0].reshape(128, 256), fc[0, :, cols], preferred_element_type=F32)
        for j in (1, 2):
            acc += jnp.dot(featg[:, j].reshape(128, 256), fc[j, :, cols], preferred_element_type=F32)
        for zz in range(8):
            part[half // 2, zz * 2 + half % 2] = acc[zz * 16 : zz * 16 + 16]
    send(part.at[1 - c], brecv0, B0, sib)

    arrived(B0)
    bsum[...] = part[c] + brecv0[...]

    @pl.loop(1, 16)
    def _(i):
        k = (m + i) % 16
        send(bsum.at[k], brecv1.at[m], B1, (d, c, k))

    brecv1[m] = bsum[m]

    load_high.wait()
    arrived(T1)
    other = d + 1 - 2 * (d % 2)
    send(xr.at[c, d], xr.at[c, d], TY, (other, c, m))
    arrived(TY)

    def along_x(first, stage):
        pair = xr.at[c, pl.ds(d - d % 2, 2), pl.ds(first, 8)]

        @pl.loop(1, 4)
        def _(i):
            send(pair, pair, stage, ((d + 2 * i) % 8, c, m))

    along_x(0, TX)
    arrived(B1)
    js = brecv1[0]
    for k in range(1, 16):
        js += brecv1[k]
    joined[...] = js

    eye = lax.broadcasted_iota(jnp.int32, (16, 128), 0) == lax.broadcasted_iota(jnp.int32, (16, 128), 1)

    def as_row(x):
        return jnp.sum(jnp.where(eye, jnp.sum(x, axis=1, keepdims=True), 0.0), axis=0, keepdims=True)

    def as_column(ref):
        return jnp.sum(jnp.where(eye, jnp.sum(ref[...], axis=0), 0.0), axis=1, keepdims=True)

    sq_s[...] = as_row(js * js)
    to_plane_both(sq_s, sq_r.at[p * 2 + c], S1)
    sq_r[p * 2 + c] = sq_s[...]
    arrived(S1)
    dscale = lax.rsqrt(as_column(sq_r) / D + EPS)
    load_dg.wait()
    own_cols = pl.multiple_of((c * 2 + yh) * 256, 256)
    gain = dgain[:, pl.ds(own_cols, 256)]
    xd[c, p, z] = (js * dscale * gain).astype(BF16)
    to_z(xd.at[c, p, z], xd.at[c, p, z], C1)

    along_x(8, TX2)
    load_tg.wait()
    arrived(TG)
    send(tg.at[c], tg.at[c], TGS, sib)

    arrived(C1)

    def c2(i):
        q = (p + i) % 16
        return pltpu.make_async_remote_copy(
            src_ref=xd.at[c, p], dst_ref=xd.at[c, p], send_sem=c2s, recv_sem=c2r.at[p],
            device_id=(q // 2, c, z * 2 + q % 2), device_id_type=MESH,
        )

    def c3(q):
        return pltpu.make_async_remote_copy(
            src_ref=xd.at[c, q], dst_ref=xd.at[c, q], send_sem=c3s, recv_sem=c3r,
            device_id=sib, device_id_type=MESH,
        )

    @pl.loop(1, 16)
    def _(i):
        c2(i).start()

    c3(p).start()
    arrived(TX)
    arrived(TX2)
    send(xr.at[c], xr.at[c], T3, sib)

    arrived(T3)
    arrived(TGS)

    def add_squares(i, acc):
        x = xr[i // 16, :, i % 16].reshape(128, 256).astype(F32)
        x = x * x
        return acc + x[:, :128] + x[:, 128:]

    squares = lax.fori_loop(0, 32, add_squares, jnp.zeros((128, 128), F32))
    tscale = lax.rsqrt(jnp.sum(squares, axis=1, keepdims=True) / D + EPS)

    load_head.wait()
    lt[...] = jnp.zeros_like(lt)

    @pl.loop(0, 8)
    def _(i):
        cc = i // 4
        mm = (i % 4) * 4
        x = jnp.concatenate(
            [
                (xr[cc, :, mm + k].reshape(128, 256).astype(F32) * tscale * tg[cc, mm + k]).astype(BF16)
                for k in range(4)
            ],
            axis=1,
        )
        cols = pl.ds(pl.multiple_of(i * 1024, 1024), 1024)
        lt[...] += lax.dot_general(head[:, cols], x, (((1,), (1,)), ((), ())), preferred_element_type=F32)

    on = mask[0:VOC, :] > 0.5
    logits = jnp.where(on, lt[...], LOW)
    tmax = jnp.max(logits, axis=0, keepdims=True)
    away = logits - tmax
    e = jnp.where(on, jnp.exp(away), 0.0)
    tz = jnp.sum(e, axis=0, keepdims=True)
    tw = jnp.sum(jnp.where(on, e * away, 0.0), axis=0, keepdims=True)

    def rows_of(*rows):
        return jnp.concatenate(rows, axis=0)

    def merge(ref):
        a = ref[...]
        top = jnp.max(a[:, 0:1, :], axis=0)
        low = a[:, 0:1, :] - top[None]
        f = jnp.exp(low)
        zz = jnp.sum(f * a[:, 1:2, :], axis=0)
        ww = jnp.sum(f * (a[:, 2:3, :] + jnp.where(a[:, 1:2, :] > 0.0, low, 0.0) * a[:, 1:2, :]), axis=0)
        return top, zz, ww, jnp.sum(a[:, 3:4, :], axis=0)

    us1[...] = rows_of(tmax, tz, tw, jnp.zeros_like(tw))
    to_mp(us1, ur1.at[m], U1)
    ur1[m] = us1[...]

    @pl.loop(1, 12)
    def _(i):
        q = (p + 16 - i) % 16
        pltpu.make_async_copy(xd.at[c, q], xd.at[c, q], c2r.at[q]).wait()
        c3(q).start()

    arrived(U1)
    us2[...] = rows_of(*merge(ur1))
    to_dp_both(us2, ur2.at[d * 2 + c], U2)
    ur2[d * 2 + c] = us2[...]

    @pl.loop(12, 16)
    def _(i):
        q = (p + 16 - i) % 16
        pltpu.make_async_copy(xd.at[c, q], xd.at[c, q], c2r.at[q]).wait()
        c3(q).start()

    pltpu.make_async_copy(xd.at[1 - c], xd.at[1 - c], c3r).wait()
    ld[...] = jnp.zeros_like(ld)

    @pl.loop(0, 8)
    def _(i):
        x = jnp.concatenate([xd[k // 2, i * 2 + k % 2].reshape(128, 256) for k in range(4)], axis=1)
        cols = pl.ds(pl.multiple_of(i * 1024, 1024), 1024)
        ld[...] += lax.dot_general(head[:, cols], x, (((1,), (1,)), ((), ())), preferred_element_type=F32)

    arrived(U2)
    tmax, tz, tw, _ = merge(ur2)
    tp = jnp.where(mask[0:VOC, :] > 0.5, jnp.exp(jnp.minimum(lt[...] - tmax, 0.0)) / tz, 0.0)
    placed[...] = tp
    teach = tw / tz - jnp.log(tz)

    logits = ld[...]
    dmax = jnp.max(logits, axis=0, keepdims=True)
    away = logits - dmax
    e = jnp.exp(away)
    dz = jnp.sum(e, axis=0, keepdims=True)
    ds = jnp.sum(e * away, axis=0, keepdims=True)
    dw = jnp.sum(tp * logits, axis=0, keepdims=True)
    vs1[...] = rows_of(dmax, dz, ds, dw)
    to_mp(vs1, vr1.at[m], V1)
    vr1[m] = vs1[...]
    arrived(V1)
    vs2[...] = rows_of(*merge(vr1))
    to_dp_both(vs2, vr2.at[d * 2 + c], V2)
    vr2[d * 2 + c] = vs2[...]
    arrived(V2)
    dmax, dz, ds, dw = merge(vr2)
    log_total = dmax + jnp.log(dz)
    loss = teach - dw + log_total
    moment = ds / dz + (dmax - dw)
    loss_out[...] = pltpu.roll(jnp.broadcast_to(loss, (8, 128)), (128 - d * 16) % 128, 1)

    g = jnp.exp(ld[...] - log_total) - placed[...]
    grad[...] = jnp.zeros_like(grad)
    grad[0:VOC, :] = g
    grad_rows = jnp.transpose(grad[...])[:, 0:VOC].astype(BF16)

    def r0_copy(dd):
        return pltpu.make_async_remote_copy(
            src_ref=hb.at[1 - c, pl.ds(dd * 2, 2)], dst_ref=r0.at[pl.ds(dd * 2, 2)],
            send_sem=r0s, recv_sem=r0r.at[dd], device_id=sib, device_id_type=MESH,
        )

    def compute(dd):
        for k in range(4):
            cols = pl.ds(pl.multiple_of(dd * 1024 + k * 256, 256), 256)
            h = jnp.dot(grad_rows, head[:, cols], preferred_element_type=F32)
            hf[k // 2, dd * 2 + k % 2] = h
            hb[k // 2, dd * 2 + k % 2] = h.astype(BF16)
        r0_copy(dd).start()

    def add_up(dd):
        pltpu.make_async_copy(r0.at[pl.ds(dd * 2, 2)], r0.at[pl.ds(dd * 2, 2)], r0r.at[dd]).wait()
        for k in range(2):
            q = dd * 2 + k
            r1s[q] = (hf[c, q] + r0[q].astype(F32)).astype(BF16)

    def to_peer(q):
        send(r1s.at[q], r1r.at[p], R1, (q // 2, c, z * 2 + q % 2))

    compute((d + 1) % 8)

    @pl.loop(2, 9)
    def _(i):
        compute((d + i) % 8)
        dd = (d + i - 1) % 8
        add_up(dd)
        to_peer(dd * 2)
        to_peer(dd * 2 + 1)

    add_up(d)
    to_peer(d * 2 + 1 - yh)
    r1r[p] = r1s[p]
    arrived(R1)
    for zz in range(8):
        acc = r1r[0, zz * 16 : zz * 16 + 16].astype(F32)
        for k in range(1, 16):
            acc += r1r[k, zz * 16 : zz * 16 + 16].astype(F32)
        r2s[zz] = acc.astype(BF16)

    @pl.loop(1, 8)
    def _(i):
        zz = (z + i) % 8
        send(r2s.at[zz], r2r.at[z], R2, (d, c, zz * 2 + yh))

    r2r[z] = r2s[z]
    arrived(R2)
    hidden = r2r[0].astype(F32)
    for k in range(1, 8):
        hidden += r2r[k].astype(F32)

    js = joined[...]
    weighted = hidden * gain
    own_tokens = lax.broadcasted_iota(jnp.int32, (16, 128), 0) + z * 16 == lax.broadcasted_iota(jnp.int32, (16, 128), 1)
    back = jnp.sum(jnp.where(own_tokens, moment, 0.0), axis=1, keepdims=True)
    jg[c, m] = (dscale * weighted - js * (dscale * dscale * back / D)).astype(BF16)
    to_mp(jg.at[c, m], jg.at[c, m], JM)
    gp_s[...] = jnp.sum(hidden * js * dscale, axis=0, keepdims=True)
    to_mp(gp_s, gp_r.at[m], GM)
    gp_r[m] = gp_s[...]
    arrived(GM)
    for k in range(2):
        acc = gp_r[k]
        for zz in range(1, 8):
            acc += gp_r[zz * 2 + k]
        gs_s[k] = acc
    send(gs_s, gs_r.at[c], GS, sib)
    gs_r[c] = gs_s[...]
    feat_out[...] = jnp.concatenate(
        [jnp.concatenate([featg[k, j : j + 1] for k in range(8)], axis=1) for j in range(3)], axis=0
    )
    arrived(GS)
    for k in range(4):
        gain_out[:, k * 256 : k * 256 + 256] = gs_r[k // 2, k % 2]
    arrived(JM)
    send(jg.at[c], jg.at[c], JS, sib)
    arrived(JS)
    for k in range(4):
        for zz in range(8):
            grad_out[zz * 16 : zz * 16 + 16, k * 256 : k * 256 + 256] = jg[k // 2, zz * 2 + k % 2]

    for stage in volume:
        sent(stage)
    pltpu.make_async_copy(xd.at[c, pl.ds(0, 15)], xd.at[c, pl.ds(0, 15)], c2s).wait()
    pltpu.make_async_copy(xd.at[c], xd.at[c], c3s).wait()
    pltpu.make_async_copy(r0, r0, r0s).wait()


def shards(features, fc_weight, head, draft_gain, target_gain, teacher_index):
    vmem = pl.BlockSpec(memory_space=pltpu.VMEM)
    hbm = pl.BlockSpec(memory_space=pl.ANY)
    V = pltpu.VMEM
    stat = [V((4, 128), F32), V((16, 4, 128), F32)] * 2
    feat_all, joined_grad, gain_grad, loss = pl.pallas_call(
        kernel,
        out_shape=(
            jax.ShapeDtypeStruct((3, 128, 256), BF16),
            jax.ShapeDtypeStruct((128, 1024), BF16),
            jax.ShapeDtypeStruct((1, 1024), F32),
            jax.ShapeDtypeStruct((8, 128), F32),
        ),
        in_specs=[hbm] * 6,
        out_specs=(vmem, vmem, vmem, vmem),
        scratch_shapes=[
            V((VOC, D), BF16),
            V((3, 256, 1024), BF16),
            V((8, 3, 16, 256), BF16),
            V((1, 1024), F32),
            V((32, 128), jnp.int32),
            V((2, 16, 16, 256), F32),
            V((16, 16, 256), F32),
            V((16, 16, 256), F32),
            V((16, 16, 256), F32),
            V((2, 8, 16, 16, 256), BF16),
            V((2, 16, 1, 256), F32),
            V((2, 16, 8, 16, 256), BF16),
            V((16, 256), F32),
            V((1, 128), F32),
            V((32, 1, 128), F32),
            V((ROWS, 128), F32),
            V((VOC, 128), F32),
            V((VOC, 128), F32),
            V((VOC, 128), F32),
            V((ROWS, 128), F32),
            *stat,
            *stat,
            V((2, 16, 128, 256), F32),
            V((2, 16, 128, 256), BF16),
            V((16, 128, 256), BF16),
            V((16, 128, 256), BF16),
            V((16, 128, 256), BF16),
            V((8, 16, 256), BF16),
            V((8, 16, 256), BF16),
            V((1, 256), F32),
            V((16, 1, 256), F32),
            V((2, 1, 256), F32),
            V((2, 2, 1, 256), F32),
            V((2, 16, 16, 256), BF16),
            pltpu.SemaphoreType.DMA((7,)),
            pltpu.SemaphoreType.DMA((STAGES,)),
            pltpu.SemaphoreType.DMA((STAGES,)),
            pltpu.SemaphoreType.DMA,
            pltpu.SemaphoreType.DMA((16,)),
            pltpu.SemaphoreType.DMA,
            pltpu.SemaphoreType.DMA,
            pltpu.SemaphoreType.DMA,
            pltpu.SemaphoreType.DMA((8,)),
        ],
        compiler_params=pltpu.CompilerParams(
            collective_id=0, has_side_effects=True, vmem_limit_bytes=60 * 2**20
        ),
        cost_estimate=pl.CostEstimate(flops=3_600_000_000, bytes_accessed=12_000_000, transcendentals=200_000),
    )(features, fc_weight, head, draft_gain.reshape(1, 1024), target_gain.reshape(1, 256), teacher_index.T)
    weight_grad = jnp.einsum("jtf,tc->jfc", feat_all, joined_grad, preferred_element_type=F32)
    return (weight_grad.astype(BF16), gain_grad.reshape(1024), loss[0, :16])


def solution(mesh):
    return jax.shard_map(
        shards,
        mesh=mesh,
        in_specs=(
            P(None, "dp", ("section", "mp")),
            P(None, ("section", "mp"), "dp"),
            P(("dp", "section", "mp"), None),
            P("dp"),
            P(("section", "mp")),
            P(),
        ),
        out_specs=(P(None, ("section", "mp"), "dp"), P("dp"), P("dp")),
        check_vma=False,
    )
```

```python
import jax
import jax.numpy as jnp
from jax import lax
from jax.experimental import pallas as pl
from jax.experimental.pallas import tpu as pltpu
from jax.sharding import PartitionSpec as P

D = 8192
EPS = 1e-05
VOC = 501
ROWS = 512
LOW = -1e30
F32 = jnp.float32
BF16 = jnp.bfloat16
MESH = pl.DeviceIdType.MESH

(A1, T1, TG, TY, TX, TX2, T3, TGS, B0, B1, S1, C1, U1, U2, V1, V2, R1, R2, GM, GS, JM, JS) = range(22)
STAGES = 22


def kernel(
    feat, fc_hbm, head_hbm, dgain_hbm, tgain_hbm, index_hbm,
    grad_out, gain_out, loss_out,
    head, fc, featg, dgain, index, part, brecv0, bsum, brecv1, xr, tg, xd, joined,
    sq_s, sq_r, mask, lt, ld, placed, grad,
    us1, ur1, us2, ur2, vs1, vr1, vs2, vr2,
    hf, hb, r0, r1s, r1r, r2s, r2r, gp_s, gp_r, gs_s, gs_r, jg, feat_t, wg,
    load_sem, ssem, rsem, c2s, c2r, c3s, c3r, r0s, r0r, out_sem,
):
    d = lax.axis_index("dp")
    c = lax.axis_index("section")
    m = lax.axis_index("mp")
    z = m // 2
    yh = m % 2
    p = d * 2 + yh
    sib = (d, 1 - c, m)

    loads = [
        pltpu.make_async_copy(src, dst, load_sem.at[k])
        for k, (src, dst) in enumerate((
            (feat, featg.at[d]), (feat.at[2], xr.at[c, d, m]), (tgain_hbm, tg.at[c, m]), (index_hbm, index),
            (dgain_hbm, dgain), (fc_hbm, fc), (head_hbm, head),
        ))
    ]
    for load in loads:
        load.start()
    load_feat, load_high, load_tg, load_index, load_dg, load_fc, load_head = loads

    barrier = pltpu.get_barrier_semaphore()

    @pl.loop(1, 16)
    def _(i):
        pl.semaphore_signal(barrier, inc=1, device_id=(d, c, (m + i) % 16), device_id_type=MESH)

    @pl.loop(1, 32)
    def _(i):
        k = (p * 2 + c + i) % 32
        pl.semaphore_signal(
            barrier, inc=1, device_id=(k // 4, k % 2, z * 2 + k // 2 % 2), device_id_type=MESH
        )

    pl.semaphore_wait(barrier, 46)

    def send(src, dst, stage, dev):
        pltpu.make_async_remote_copy(
            src_ref=src, dst_ref=dst, send_sem=ssem.at[stage], recv_sem=rsem.at[stage],
            device_id=dev, device_id_type=MESH,
        ).start()

    volume = {
        A1: featg.at[pl.ds(0, 7)], T1: xr.at[c, d, pl.ds(0, 15)], TG: tg.at[c, pl.ds(0, 15)], TY: xr.at[c, d],
        TX: xr.at[c, pl.ds(0, 6), pl.ds(0, 8)], TX2: xr.at[c, pl.ds(0, 6), pl.ds(0, 8)], T3: xr.at[c], TGS: tg.at[c], B0: brecv0, B1: bsum.at[pl.ds(0, 15)],
        S1: sq_r.at[pl.ds(0, 31)], C1: xd.at[c, p, pl.ds(0, 7)], U1: ur1.at[pl.ds(0, 15)], U2: ur2.at[pl.ds(0, 15)],
        V1: vr1.at[pl.ds(0, 15)], V2: vr2.at[pl.ds(0, 15)], R1: r1r.at[pl.ds(0, 15)], R2: r2r.at[pl.ds(0, 7)],
        GM: gp_r.at[pl.ds(0, 15)], GS: gs_s, JM: jg.at[c, pl.ds(0, 15)], JS: jg.at[c],
    }

    def arrived(stage):
        pltpu.make_async_copy(volume[stage], volume[stage], rsem.at[stage]).wait()

    def sent(stage):
        pltpu.make_async_copy(volume[stage], volume[stage], ssem.at[stage]).wait()

    def step(i, n):
        return i % 2 * ((i + 1) // 2) + (1 - i % 2) * (n - i // 2)

    def to_mp(src, dst, stage):
        @pl.loop(1, 16)
        def _(i):
            send(src, dst, stage, (d, c, (m + step(i, 16)) % 16))

    def to_dp(src, dst, stage):
        @pl.loop(1, 8)
        def _(i):
            send(src, dst, stage, ((d + step(i, 8)) % 8, c, m))

    def to_dp_both(src, dst, stage):
        @pl.loop(1, 16)
        def _(i):
            k = (d * 2 + c + step(i, 16)) % 16
            send(src, dst, stage, (k // 2, k % 2, m))

    def to_z(src, dst, stage):
        @pl.loop(1, 8)
        def _(i):
            send(src, dst, stage, (d, c, ((z + step(i, 8)) % 8) * 2 + yh))

    def to_plane_both(src, dst, stage):
        @pl.loop(1, 32)
        def _(i):
            k = (p * 2 + c + step(i, 32)) % 32
            send(src, dst, stage, (k // 4, k % 2, z * 2 + k // 2 % 2))

    to_dp(feat, featg.at[d], A1)
    to_mp(feat.at[2], xr.at[c, d, m], T1)
    to_mp(tgain_hbm, tg.at[c, m], TG)

    start = ((d * 2 + c) * 16 + m) * VOC
    load_index.wait()

    @pl.loop(0, ROWS // 64)
    def _(i):
        rows = lax.broadcasted_iota(jnp.int32, (64, 128), 0) + (i * 64 + start)
        hit = rows == index[0:1, :]
        for k in range(1, 32):
            hit = hit | (rows == index[k : k + 1, :])
        hit = hit & (rows < start + VOC)
        mask[pl.ds(pl.multiple_of(i * 64, 64), 64), :] = hit.astype(F32)

    load_fc.wait()
    load_feat.wait()
    arrived(A1)
    for half in range(4):
        cols = slice(half * 256, half * 256 + 256)
        acc = jnp.dot(featg[:, 0].reshape(128, 256), fc[0, :, cols], preferred_element_type=F32)
        for j in (1, 2):
            acc += jnp.dot(featg[:, j].reshape(128, 256), fc[j, :, cols], preferred_element_type=F32)
        for zz in range(8):
            part[half // 2, zz * 2 + half % 2] = acc[zz * 16 : zz * 16 + 16]
    send(part.at[1 - c], brecv0, B0, sib)

    load_high.wait()
    arrived(T1)
    other = d + 1 - 2 * (d % 2)
    send(xr.at[c, d], xr.at[c, d], TY, (other, c, m))

    arrived(B0)
    bsum[...] = part[c] + brecv0[...]

    @pl.loop(1, 16)
    def _(i):
        k = (m + step(i, 16)) % 16
        send(bsum.at[k], brecv1.at[m], B1, (d, c, k))

    brecv1[m] = bsum[m]

    arrived(TY)

    def along_x(first, stage):
        pair = xr.at[c, pl.ds(d - d % 2, 2), pl.ds(first, 8)]

        @pl.loop(1, 4)
        def _(i):
            send(pair, pair, stage, ((d + 2 * i) % 8, c, m))

    along_x(0, TX)
    arrived(B1)
    js = brecv1[0]
    for k in range(1, 16):
        js += brecv1[k]
    joined[...] = js

    eye = lax.broadcasted_iota(jnp.int32, (16, 128), 0) == lax.broadcasted_iota(jnp.int32, (16, 128), 1)

    def as_row(x):
        return jnp.sum(jnp.where(eye, jnp.sum(x, axis=1, keepdims=True), 0.0), axis=0, keepdims=True)

    def as_column(ref):
        return jnp.sum(jnp.where(eye, jnp.sum(ref[...], axis=0), 0.0), axis=1, keepdims=True)

    sq_s[...] = as_row(js * js)
    to_plane_both(sq_s, sq_r.at[p * 2 + c], S1)
    sq_r[p * 2 + c] = sq_s[...]
    arrived(S1)
    dscale = lax.rsqrt(as_column(sq_r) / D + EPS)
    load_dg.wait()
    own_cols = pl.multiple_of((c * 2 + yh) * 256, 256)
    gain = dgain[:, pl.ds(own_cols, 256)]
    xd[c, p, z] = (js * dscale * gain).astype(BF16)
    to_z(xd.at[c, p, z], xd.at[c, p, z], C1)

    along_x(8, TX2)
    load_tg.wait()
    arrived(TG)
    send(tg.at[c], tg.at[c], TGS, sib)

    arrived(C1)

    def c2(i):
        q = (p + step(i, 16)) % 16
        return pltpu.make_async_remote_copy(
            src_ref=xd.at[c, p], dst_ref=xd.at[c, p], send_sem=c2s, recv_sem=c2r.at[p],
            device_id=(q // 2, c, z * 2 + q % 2), device_id_type=MESH,
        )

    def c3(q):
        return pltpu.make_async_remote_copy(
            src_ref=xd.at[c, q], dst_ref=xd.at[c, q], send_sem=c3s, recv_sem=c3r,
            device_id=sib, device_id_type=MESH,
        )

    @pl.loop(1, 16)
    def _(i):
        c2(i).start()

    c3(p).start()
    arrived(TX)
    arrived(TX2)
    send(xr.at[c], xr.at[c], T3, sib)

    arrived(T3)
    arrived(TGS)

    def add_squares(i, acc):
        x = xr[i // 16, :, i % 16].reshape(128, 256).astype(F32)
        x = x * x
        return acc + x[:, :128] + x[:, 128:]

    squares = lax.fori_loop(0, 32, add_squares, jnp.zeros((128, 128), F32))
    tscale = lax.rsqrt(jnp.sum(squares, axis=1, keepdims=True) / D + EPS)

    load_head.wait()
    lt[...] = jnp.zeros_like(lt)

    @pl.loop(0, 8)
    def _(i):
        cc = i // 4
        mm = (i % 4) * 4
        x = jnp.concatenate(
            [
                (xr[cc, :, mm + k].reshape(128, 256).astype(F32) * tscale * tg[cc, mm + k]).astype(BF16)
                for k in range(4)
            ],
            axis=1,
        )
        cols = pl.ds(pl.multiple_of(i * 1024, 1024), 1024)
        lt[...] += lax.dot_general(head[:, cols], x, (((1,), (1,)), ((), ())), preferred_element_type=F32)

    on = mask[0:VOC, :] > 0.5
    logits = jnp.where(on, lt[...], LOW)
    tmax = jnp.max(logits, axis=0, keepdims=True)
    away = logits - tmax
    e = jnp.where(on, jnp.exp(away), 0.0)
    tz = jnp.sum(e, axis=0, keepdims=True)
    tw = jnp.sum(jnp.where(on, e * away, 0.0), axis=0, keepdims=True)

    def rows_of(*rows):
        return jnp.concatenate(rows, axis=0)

    def merge(ref):
        a = ref[...]
        top = jnp.max(a[:, 0:1, :], axis=0)
        low = a[:, 0:1, :] - top[None]
        f = jnp.exp(low)
        zz = jnp.sum(f * a[:, 1:2, :], axis=0)
        ww = jnp.sum(f * (a[:, 2:3, :] + jnp.where(a[:, 1:2, :] > 0.0, low, 0.0) * a[:, 1:2, :]), axis=0)
        return top, zz, ww, jnp.sum(a[:, 3:4, :], axis=0)

    us1[...] = rows_of(tmax, tz, tw, jnp.zeros_like(tw))
    to_mp(us1, ur1.at[m], U1)
    ur1[m] = us1[...]

    @pl.loop(1, 12)
    def _(i):
        q = (p + step(i, 16)) % 16
        pltpu.make_async_copy(xd.at[c, q], xd.at[c, q], c2r.at[q]).wait()
        c3(q).start()

    arrived(U1)
    us2[...] = rows_of(*merge(ur1))
    to_dp_both(us2, ur2.at[d * 2 + c], U2)
    ur2[d * 2 + c] = us2[...]

    @pl.loop(12, 16)
    def _(i):
        q = (p + step(i, 16)) % 16
        pltpu.make_async_copy(xd.at[c, q], xd.at[c, q], c2r.at[q]).wait()
        c3(q).start()

    pltpu.make_async_copy(xd.at[1 - c], xd.at[1 - c], c3r).wait()
    ld[...] = jnp.zeros_like(ld)

    @pl.loop(0, 8)
    def _(i):
        x = jnp.concatenate([xd[k // 2, i * 2 + k % 2].reshape(128, 256) for k in range(4)], axis=1)
        cols = pl.ds(pl.multiple_of(i * 1024, 1024), 1024)
        ld[...] += lax.dot_general(head[:, cols], x, (((1,), (1,)), ((), ())), preferred_element_type=F32)

    arrived(U2)
    tmax, tz, tw, _ = merge(ur2)
    tp = jnp.where(mask[0:VOC, :] > 0.5, jnp.exp(jnp.minimum(lt[...] - tmax, 0.0)) / tz, 0.0)
    placed[...] = tp
    teach = tw / tz - jnp.log(tz)

    logits = ld[...]
    dmax = jnp.max(logits, axis=0, keepdims=True)
    away = logits - dmax
    e = jnp.exp(away)
    dz = jnp.sum(e, axis=0, keepdims=True)
    ds = jnp.sum(e * away, axis=0, keepdims=True)
    dw = jnp.sum(tp * logits, axis=0, keepdims=True)
    vs1[...] = rows_of(dmax, dz, ds, dw)
    to_mp(vs1, vr1.at[m], V1)
    vr1[m] = vs1[...]
    arrived(V1)
    vs2[...] = rows_of(*merge(vr1))
    to_dp_both(vs2, vr2.at[d * 2 + c], V2)
    vr2[d * 2 + c] = vs2[...]
    arrived(V2)
    dmax, dz, ds, dw = merge(vr2)
    log_total = dmax + jnp.log(dz)
    loss = teach - dw + log_total
    moment = ds / dz + (dmax - dw)
    loss_out[...] = pltpu.roll(jnp.broadcast_to(loss, (8, 128)), (128 - d * 16) % 128, 1)[0:1, 0:16]

    g = jnp.exp(ld[...] - log_total) - placed[...]
    grad[...] = jnp.zeros_like(grad)
    grad[0:VOC, :] = g
    grad_rows = jnp.transpose(grad[...])[:, 0:VOC].astype(BF16)

    def r0_copy(dd):
        return pltpu.make_async_remote_copy(
            src_ref=hb.at[1 - c, pl.ds(dd * 2, 2)], dst_ref=r0.at[pl.ds(dd * 2, 2)],
            send_sem=r0s, recv_sem=r0r.at[dd], device_id=sib, device_id_type=MESH,
        )

    def compute(dd):
        for k in range(4):
            cols = pl.ds(pl.multiple_of(dd * 1024 + k * 256, 256), 256)
            h = jnp.dot(grad_rows, head[:, cols], preferred_element_type=F32)
            hf[k // 2, dd * 2 + k % 2] = h
            hb[k // 2, dd * 2 + k % 2] = h.astype(BF16)
        r0_copy(dd).start()

    def add_up(dd):
        pltpu.make_async_copy(r0.at[pl.ds(dd * 2, 2)], r0.at[pl.ds(dd * 2, 2)], r0r.at[dd]).wait()
        for k in range(2):
            q = dd * 2 + k
            r1s[q] = (hf[c, q] + r0[q].astype(F32)).astype(BF16)

    def to_peer(q):
        send(r1s.at[q], r1r.at[p], R1, (q // 2, c, z * 2 + q % 2))

    compute((d + 1) % 8)

    @pl.loop(2, 9)
    def _(i):
        compute((d + step(i, 8) * (1 - i // 8)) % 8)
        dd = (d + step(i - 1, 8)) % 8
        add_up(dd)
        to_peer(dd * 2)
        to_peer(dd * 2 + 1)

    add_up(d)
    to_peer(d * 2 + 1 - yh)
    r1r[p] = r1s[p]
    arrived(R1)
    for zz in range(8):
        acc = r1r[0, zz * 16 : zz * 16 + 16].astype(F32)
        for k in range(1, 16):
            acc += r1r[k, zz * 16 : zz * 16 + 16].astype(F32)
        r2s[zz] = acc.astype(BF16)

    @pl.loop(1, 8)
    def _(i):
        zz = (z + step(i, 8)) % 8
        send(r2s.at[zz], r2r.at[z], R2, (d, c, zz * 2 + yh))

    r2r[z] = r2s[z]
    arrived(R2)
    hidden = r2r[0].astype(F32)
    for k in range(1, 8):
        hidden += r2r[k].astype(F32)

    js = joined[...]
    weighted = hidden * gain
    own_tokens = lax.broadcasted_iota(jnp.int32, (16, 128), 0) + z * 16 == lax.broadcasted_iota(jnp.int32, (16, 128), 1)
    back = jnp.sum(jnp.where(own_tokens, moment, 0.0), axis=1, keepdims=True)
    jg[c, m] = (dscale * weighted - js * (dscale * dscale * back / D)).astype(BF16)
    to_mp(jg.at[c, m], jg.at[c, m], JM)
    gp_s[...] = jnp.sum(hidden * js * dscale, axis=0, keepdims=True)
    to_mp(gp_s, gp_r.at[m], GM)
    gp_r[m] = gp_s[...]
    for j in range(3):
        feat_t[j] = jnp.transpose(featg[:, j].reshape(128, 256).astype(F32)).astype(BF16)
    arrived(JM)
    send(jg.at[c], jg.at[c], JS, sib)

    def weight_grad(cc):
        cols = pl.ds(pl.multiple_of(cc * 512, 512), 512)
        for k in range(2):
            rows = jnp.concatenate([jg[cc, zz * 2 + k] for zz in range(8)], axis=0)
            part_cols = pl.ds(pl.multiple_of(cc * 512 + k * 256, 256), 256)
            for j in range(3):
                wg[j, :, part_cols] = jnp.dot(feat_t[j], rows, preferred_element_type=F32).astype(BF16)
        return pltpu.make_async_copy(wg.at[:, :, cols], grad_out.at[:, :, cols], out_sem.at[cc])

    weight_grad(c).start()
    arrived(GM)
    for k in range(2):
        acc = gp_r[k]
        for zz in range(1, 8):
            acc += gp_r[zz * 2 + k]
        gs_s[k] = acc
    send(gs_s, gs_r.at[c], GS, sib)
    gs_r[c] = gs_s[...]
    arrived(JS)
    weight_grad(1 - c).start()
    arrived(GS)
    for k in range(4):
        gain_out[:, k * 256 : k * 256 + 256] = gs_r[k // 2, k % 2]
    for k in range(2):
        half = slice(k * 512, k * 512 + 512)
        pltpu.make_async_copy(wg.at[:, :, half], grad_out.at[:, :, half], out_sem.at[k]).wait()

    for stage in volume:
        sent(stage)
    pltpu.make_async_copy(xd.at[c, pl.ds(0, 15)], xd.at[c, pl.ds(0, 15)], c2s).wait()
    pltpu.make_async_copy(xd.at[c], xd.at[c], c3s).wait()
    pltpu.make_async_copy(r0, r0, r0s).wait()


def shards(features, fc_weight, head, draft_gain, target_gain, teacher_index):
    vmem = pl.BlockSpec(memory_space=pltpu.VMEM)
    hbm = pl.BlockSpec(memory_space=pl.ANY)
    V = pltpu.VMEM
    stat = [V((4, 128), F32), V((16, 4, 128), F32)] * 2
    weight_grad, gain_grad, loss = pl.pallas_call(
        kernel,
        out_shape=(
            jax.ShapeDtypeStruct((3, 256, 1024), BF16),
            jax.ShapeDtypeStruct((1, 1024), F32),
            jax.ShapeDtypeStruct((1, 16), F32),
        ),
        in_specs=[hbm] * 6,
        out_specs=(hbm, vmem, vmem),
        scratch_shapes=[
            V((VOC, D), BF16),
            V((3, 256, 1024), BF16),
            V((8, 3, 16, 256), BF16),
            V((1, 1024), F32),
            V((32, 128), jnp.int32),
            V((2, 16, 16, 256), F32),
            V((16, 16, 256), F32),
            V((16, 16, 256), F32),
            V((16, 16, 256), F32),
            V((2, 8, 16, 16, 256), BF16),
            V((2, 16, 1, 256), F32),
            V((2, 16, 8, 16, 256), BF16),
            V((16, 256), F32),
            V((1, 128), F32),
            V((32, 1, 128), F32),
            V((ROWS, 128), F32),
            V((VOC, 128), F32),
            V((VOC, 128), F32),
            V((VOC, 128), F32),
            V((ROWS, 128), F32),
            *stat,
            *stat,
            V((2, 16, 128, 256), F32),
            V((2, 16, 128, 256), BF16),
            V((16, 128, 256), BF16),
            V((16, 128, 256), BF16),
            V((16, 128, 256), BF16),
            V((8, 16, 256), BF16),
            V((8, 16, 256), BF16),
            V((1, 256), F32),
            V((16, 1, 256), F32),
            V((2, 1, 256), F32),
            V((2, 2, 1, 256), F32),
            V((2, 16, 16, 256), BF16),
            V((3, 256, 128), BF16),
            V((3, 256, 1024), BF16),
            pltpu.SemaphoreType.DMA((7,)),
            pltpu.SemaphoreType.DMA((STAGES,)),
            pltpu.SemaphoreType.DMA((STAGES,)),
            pltpu.SemaphoreType.DMA,
            pltpu.SemaphoreType.DMA((16,)),
            pltpu.SemaphoreType.DMA,
            pltpu.SemaphoreType.DMA,
            pltpu.SemaphoreType.DMA,
            pltpu.SemaphoreType.DMA((8,)),
            pltpu.SemaphoreType.DMA((2,)),
        ],
        compiler_params=pltpu.CompilerParams(
            collective_id=0, has_side_effects=True, vmem_limit_bytes=60 * 2**20
        ),
        cost_estimate=pl.CostEstimate(flops=3_600_000_000, bytes_accessed=12_000_000, transcendentals=200_000),
    )(features, fc_weight, head, draft_gain.reshape(1, 1024), target_gain.reshape(1, 256), teacher_index.T)
    return (weight_grad, gain_grad.reshape(1024), loss.reshape(16))


def solution(mesh):
    return jax.shard_map(
        shards,
        mesh=mesh,
        in_specs=(
            P(None, "dp", ("section", "mp")),
            P(None, ("section", "mp"), "dp"),
            P(("dp", "section", "mp"), None),
            P("dp"),
            P(("section", "mp")),
            P(),
        ),
        out_specs=(P(None, ("section", "mp"), "dp"), P("dp"), P("dp")),
        check_vma=False,
    )
```

```python
import jax
import jax.numpy as jnp
from jax import lax
from jax.experimental import pallas as pl
from jax.experimental.pallas import tpu as pltpu
from jax.sharding import PartitionSpec as P

D = 8192
EPS = 1e-05
VOC = 501
ROWS = 512
LOW = -1e30
F32 = jnp.float32
BF16 = jnp.bfloat16
MESH = pl.DeviceIdType.MESH

(A1, T1, TG, TY, TX, TX2, T3, TGS, B0, B1, S1, C1, U1, U2, V1, V2, W1, W2, R1, R2, GM, GS, JM, JS) = range(24)
STAGES = 24


def kernel(
    feat, fc_hbm, head_hbm, dgain_hbm, tgain_hbm, index_hbm,
    grad_out, gain_out, loss_out,
    head, fc, featg, dgain, index, part, brecv0, bsum, brecv1, xr, tg, xd, joined,
    sq_s, sq_r, mask, lt, ld, placed, grad,
    us1, ur1, us2, ur2, vs1, vr1, vs2, vr2, ws1, wr1, ws2, wr2,
    hf, hb, r0, r1s, r1r, r2s, r2r, gp_s, gp_r, gs_s, gs_r, jg, feat_t, wg,
    load_sem, ssem, rsem, c2s, c2r, c3s, c3r, r0s, r0r, out_sem,
):
    d = lax.axis_index("dp")
    c = lax.axis_index("section")
    m = lax.axis_index("mp")
    z = m // 2
    yh = m % 2
    p = d * 2 + yh
    sib = (d, 1 - c, m)

    loads = [
        pltpu.make_async_copy(src, dst, load_sem.at[k])
        for k, (src, dst) in enumerate((
            (feat, featg.at[d]), (feat.at[2], xr.at[c, d, m]), (tgain_hbm, tg.at[c, m]), (index_hbm, index),
            (dgain_hbm, dgain), (fc_hbm, fc), (head_hbm, head),
        ))
    ]
    for load in loads:
        load.start()
    load_feat, load_high, load_tg, load_index, load_dg, load_fc, load_head = loads

    barrier = pltpu.get_barrier_semaphore()

    @pl.loop(1, 16)
    def _(i):
        pl.semaphore_signal(barrier, inc=1, device_id=(d, c, (m + i) % 16), device_id_type=MESH)

    @pl.loop(1, 32)
    def _(i):
        k = (p * 2 + c + i) % 32
        pl.semaphore_signal(
            barrier, inc=1, device_id=(k // 4, k % 2, z * 2 + k // 2 % 2), device_id_type=MESH
        )

    pl.semaphore_wait(barrier, 46)

    def send(src, dst, stage, dev):
        pltpu.make_async_remote_copy(
            src_ref=src, dst_ref=dst, send_sem=ssem.at[stage], recv_sem=rsem.at[stage],
            device_id=dev, device_id_type=MESH,
        ).start()

    volume = {
        A1: featg.at[pl.ds(0, 7)], T1: xr.at[c, d, pl.ds(0, 15)], TG: tg.at[c, pl.ds(0, 15)], TY: xr.at[c, d],
        TX: xr.at[c, pl.ds(0, 6), pl.ds(0, 8)], TX2: xr.at[c, pl.ds(0, 6), pl.ds(0, 8)], T3: xr.at[c], TGS: tg.at[c], B0: brecv0, B1: bsum.at[pl.ds(0, 15)],
        S1: sq_r.at[pl.ds(0, 31)], C1: xd.at[c, p, pl.ds(0, 7)], U1: ur1.at[pl.ds(0, 15)], U2: ur2.at[pl.ds(0, 15)],
        W1: wr1.at[pl.ds(0, 15)], W2: wr2.at[pl.ds(0, 15)], V1: vr1.at[pl.ds(0, 15)], V2: vr2.at[pl.ds(0, 15)], R1: r1r.at[pl.ds(0, 15)], R2: r2r.at[pl.ds(0, 7)],
        GM: gp_r.at[pl.ds(0, 15)], GS: gs_s, JM: jg.at[c, pl.ds(0, 15)], JS: jg.at[c],
    }

    def arrived(stage):
        pltpu.make_async_copy(volume[stage], volume[stage], rsem.at[stage]).wait()

    def sent(stage):
        pltpu.make_async_copy(volume[stage], volume[stage], ssem.at[stage]).wait()

    def step(i, n):
        return i % 2 * ((i + 1) // 2) + (1 - i % 2) * (n - i // 2)

    def to_mp(src, dst, stage):
        @pl.loop(1, 16)
        def _(i):
            send(src, dst, stage, (d, c, (m + step(i, 16)) % 16))

    def to_dp(src, dst, stage):
        @pl.loop(1, 8)
        def _(i):
            send(src, dst, stage, ((d + step(i, 8)) % 8, c, m))

    def to_dp_both(src, dst, stage):
        @pl.loop(1, 16)
        def _(i):
            k = (d * 2 + c + step(i, 16)) % 16
            send(src, dst, stage, (k // 2, k % 2, m))

    def to_z(src, dst, stage):
        @pl.loop(1, 8)
        def _(i):
            send(src, dst, stage, (d, c, ((z + step(i, 8)) % 8) * 2 + yh))

    def to_plane_both(src, dst, stage):
        @pl.loop(1, 32)
        def _(i):
            k = (p * 2 + c + step(i, 32)) % 32
            send(src, dst, stage, (k // 4, k % 2, z * 2 + k // 2 % 2))

    to_dp(feat, featg.at[d], A1)
    to_mp(feat.at[2], xr.at[c, d, m], T1)
    to_mp(tgain_hbm, tg.at[c, m], TG)

    start = ((d * 2 + c) * 16 + m) * VOC
    load_index.wait()

    @pl.loop(0, ROWS // 64)
    def _(i):
        rows = lax.broadcasted_iota(jnp.int32, (64, 128), 0) + (i * 64 + start)
        hit = rows == index[0:1, :]
        for k in range(1, 32):
            hit = hit | (rows == index[k : k + 1, :])
        hit = hit & (rows < start + VOC)
        mask[pl.ds(pl.multiple_of(i * 64, 64), 64), :] = hit.astype(F32)

    load_fc.wait()
    load_feat.wait()
    arrived(A1)
    for half in range(4):
        cols = slice(half * 256, half * 256 + 256)
        acc = jnp.dot(featg[:, 0].reshape(128, 256), fc[0, :, cols], preferred_element_type=F32)
        for j in (1, 2):
            acc += jnp.dot(featg[:, j].reshape(128, 256), fc[j, :, cols], preferred_element_type=F32)
        for zz in range(8):
            part[half // 2, zz * 2 + half % 2] = acc[zz * 16 : zz * 16 + 16]
    send(part.at[1 - c], brecv0, B0, sib)

    load_high.wait()
    arrived(T1)
    other = d + 1 - 2 * (d % 2)
    send(xr.at[c, d], xr.at[c, d], TY, (other, c, m))

    arrived(B0)
    bsum[...] = part[c] + brecv0[...]

    @pl.loop(1, 16)
    def _(i):
        k = (m + step(i, 16)) % 16
        send(bsum.at[k], brecv1.at[m], B1, (d, c, k))

    brecv1[m] = bsum[m]

    arrived(TY)

    def along_x(first, stage):
        pair = xr.at[c, pl.ds(d - d % 2, 2), pl.ds(first, 8)]

        @pl.loop(1, 4)
        def _(i):
            send(pair, pair, stage, ((d + 2 * i) % 8, c, m))

    along_x(0, TX)
    arrived(B1)
    js = brecv1[0]
    for k in range(1, 16):
        js += brecv1[k]
    joined[...] = js

    eye = lax.broadcasted_iota(jnp.int32, (16, 128), 0) == lax.broadcasted_iota(jnp.int32, (16, 128), 1)

    def as_row(x):
        return jnp.sum(jnp.where(eye, jnp.sum(x, axis=1, keepdims=True), 0.0), axis=0, keepdims=True)

    def as_column(ref):
        return jnp.sum(jnp.where(eye, jnp.sum(ref[...], axis=0), 0.0), axis=1, keepdims=True)

    sq_s[...] = as_row(js * js)
    to_plane_both(sq_s, sq_r.at[p * 2 + c], S1)
    sq_r[p * 2 + c] = sq_s[...]
    arrived(S1)
    dscale = lax.rsqrt(as_column(sq_r) / D + EPS)
    load_dg.wait()
    own_cols = pl.multiple_of((c * 2 + yh) * 256, 256)
    gain = dgain[:, pl.ds(own_cols, 256)]
    xd[c, p, z] = (js * dscale * gain).astype(BF16)
    to_z(xd.at[c, p, z], xd.at[c, p, z], C1)

    along_x(8, TX2)
    load_tg.wait()
    arrived(TG)
    send(tg.at[c], tg.at[c], TGS, sib)

    arrived(C1)

    def c2(i):
        q = (p + step(i, 16)) % 16
        return pltpu.make_async_remote_copy(
            src_ref=xd.at[c, p], dst_ref=xd.at[c, p], send_sem=c2s, recv_sem=c2r.at[p],
            device_id=(q // 2, c, z * 2 + q % 2), device_id_type=MESH,
        )

    def c3(q):
        return pltpu.make_async_remote_copy(
            src_ref=xd.at[c, q], dst_ref=xd.at[c, q], send_sem=c3s, recv_sem=c3r,
            device_id=sib, device_id_type=MESH,
        )

    @pl.loop(1, 16)
    def _(i):
        c2(i).start()

    c3(p).start()
    arrived(TX)
    arrived(TX2)
    send(xr.at[c], xr.at[c], T3, sib)

    arrived(T3)
    arrived(TGS)

    def add_squares(i, acc):
        x = xr[i // 16, :, i % 16].reshape(128, 256).astype(F32)
        x = x * x
        return acc + x[:, :128] + x[:, 128:]

    squares = lax.fori_loop(0, 32, add_squares, jnp.zeros((128, 128), F32))
    tscale = lax.rsqrt(jnp.sum(squares, axis=1, keepdims=True) / D + EPS)

    load_head.wait()
    lt[...] = jnp.zeros_like(lt)

    @pl.loop(0, 8)
    def _(i):
        cc = i // 4
        mm = (i % 4) * 4
        x = jnp.concatenate(
            [
                (xr[cc, :, mm + k].reshape(128, 256).astype(F32) * tscale * tg[cc, mm + k]).astype(BF16)
                for k in range(4)
            ],
            axis=1,
        )
        cols = pl.ds(pl.multiple_of(i * 1024, 1024), 1024)
        lt[...] += lax.dot_general(head[:, cols], x, (((1,), (1,)), ((), ())), preferred_element_type=F32)

    on = mask[0:VOC, :] > 0.5
    logits = jnp.where(on, lt[...], LOW)
    tmax = jnp.max(logits, axis=0, keepdims=True)
    away = logits - tmax
    e = jnp.where(on, jnp.exp(away), 0.0)
    tz = jnp.sum(e, axis=0, keepdims=True)
    tw = jnp.sum(jnp.where(on, e * away, 0.0), axis=0, keepdims=True)

    def rows_of(a, b, w):
        return jnp.concatenate([a, b, w, jnp.zeros((1, 128), F32)], axis=0)

    def merge(ref):
        a = ref[...]
        top = jnp.max(a[:, 0:1, :], axis=0)
        low = a[:, 0:1, :] - top[None]
        f = jnp.exp(low)
        zz = jnp.sum(f * a[:, 1:2, :], axis=0)
        ww = jnp.sum(f * (a[:, 2:3, :] + jnp.where(a[:, 1:2, :] > 0.0, low, 0.0) * a[:, 1:2, :]), axis=0)
        return top, zz, ww

    us1[...] = rows_of(tmax, tz, tw)
    to_mp(us1, ur1.at[m], U1)
    ur1[m] = us1[...]

    @pl.loop(1, 16)
    def _(i):
        q = (p + step(i, 16)) % 16
        pltpu.make_async_copy(xd.at[c, q], xd.at[c, q], c2r.at[q]).wait()
        c3(q).start()

    pltpu.make_async_copy(xd.at[1 - c], xd.at[1 - c], c3r).wait()
    ld[...] = jnp.zeros_like(ld)

    @pl.loop(0, 8)
    def _(i):
        x = jnp.concatenate([xd[k // 2, i * 2 + k % 2].reshape(128, 256) for k in range(4)], axis=1)
        cols = pl.ds(pl.multiple_of(i * 1024, 1024), 1024)
        ld[...] += lax.dot_general(head[:, cols], x, (((1,), (1,)), ((), ())), preferred_element_type=F32)

    logits = ld[...]
    dmax = jnp.max(logits, axis=0, keepdims=True)
    away = logits - dmax
    e = jnp.exp(away)
    dz = jnp.sum(e, axis=0, keepdims=True)
    ds = jnp.sum(e * away, axis=0, keepdims=True)
    vs1[...] = rows_of(dmax, dz, ds)
    to_mp(vs1, vr1.at[m], V1)
    vr1[m] = vs1[...]

    arrived(U1)
    us2[...] = rows_of(*merge(ur1))
    to_dp_both(us2, ur2.at[d * 2 + c], U2)
    ur2[d * 2 + c] = us2[...]

    arrived(V1)
    vs2[...] = rows_of(*merge(vr1))
    to_dp_both(vs2, vr2.at[d * 2 + c], V2)
    vr2[d * 2 + c] = vs2[...]

    arrived(U2)
    tmax, tz, tw = merge(ur2)
    tp = jnp.where(mask[0:VOC, :] > 0.5, jnp.exp(jnp.minimum(lt[...] - tmax, 0.0)) / tz, 0.0)
    placed[...] = tp
    teach = tw / tz - jnp.log(tz)
    ws1[...] = jnp.sum(tp * ld[...], axis=0, keepdims=True)
    to_mp(ws1, wr1.at[m], W1)
    wr1[m] = ws1[...]

    arrived(V2)
    dmax, dz, ds = merge(vr2)
    log_total = dmax + jnp.log(dz)
    g = jnp.exp(ld[...] - log_total) - placed[...]
    grad[...] = jnp.zeros_like(grad)
    grad[0:VOC, :] = g
    grad_rows = jnp.transpose(grad[...])[:, 0:VOC].astype(BF16)

    def r0_copy(dd):
        return pltpu.make_async_remote_copy(
            src_ref=hb.at[1 - c, pl.ds(dd * 2, 2)], dst_ref=r0.at[pl.ds(dd * 2, 2)],
            send_sem=r0s, recv_sem=r0r.at[dd], device_id=sib, device_id_type=MESH,
        )

    def compute(dd):
        for k in range(4):
            cols = pl.ds(pl.multiple_of(dd * 1024 + k * 256, 256), 256)
            h = jnp.dot(grad_rows, head[:, cols], preferred_element_type=F32)
            hf[k // 2, dd * 2 + k % 2] = h
            hb[k // 2, dd * 2 + k % 2] = h.astype(BF16)
        r0_copy(dd).start()

    def add_up(dd):
        pltpu.make_async_copy(r0.at[pl.ds(dd * 2, 2)], r0.at[pl.ds(dd * 2, 2)], r0r.at[dd]).wait()
        for k in range(2):
            q = dd * 2 + k
            r1s[q] = (hf[c, q] + r0[q].astype(F32)).astype(BF16)

    def to_peer(q):
        send(r1s.at[q], r1r.at[p], R1, (q // 2, c, z * 2 + q % 2))

    compute((d + 1) % 8)

    @pl.loop(2, 9)
    def _(i):
        compute((d + step(i, 8) * (1 - i // 8)) % 8)
        dd = (d + step(i - 1, 8)) % 8
        add_up(dd)
        to_peer(dd * 2)
        to_peer(dd * 2 + 1)

    add_up(d)
    to_peer(d * 2 + 1 - yh)
    r1r[p] = r1s[p]
    arrived(W1)
    ws2[...] = jnp.sum(wr1[...], axis=0)
    to_dp_both(ws2, wr2.at[d * 2 + c], W2)
    wr2[d * 2 + c] = ws2[...]
    arrived(R1)
    for zz in range(8):
        acc = r1r[0, zz * 16 : zz * 16 + 16].astype(F32)
        for k in range(1, 16):
            acc += r1r[k, zz * 16 : zz * 16 + 16].astype(F32)
        r2s[zz] = acc.astype(BF16)

    @pl.loop(1, 8)
    def _(i):
        zz = (z + step(i, 8)) % 8
        send(r2s.at[zz], r2r.at[z], R2, (d, c, zz * 2 + yh))

    r2r[z] = r2s[z]
    arrived(W2)
    dw = jnp.sum(wr2[...], axis=0)
    loss = teach - dw + log_total
    moment = ds / dz + (dmax - dw)
    loss_out[...] = pltpu.roll(jnp.broadcast_to(loss, (8, 128)), (128 - d * 16) % 128, 1)[0:1, 0:16]

    arrived(R2)
    hidden = r2r[0].astype(F32)
    for k in range(1, 8):
        hidden += r2r[k].astype(F32)

    js = joined[...]
    weighted = hidden * gain
    own_tokens = lax.broadcasted_iota(jnp.int32, (16, 128), 0) + z * 16 == lax.broadcasted_iota(jnp.int32, (16, 128), 1)
    back = jnp.sum(jnp.where(own_tokens, moment, 0.0), axis=1, keepdims=True)
    jg[c, m] = (dscale * weighted - js * (dscale * dscale * back / D)).astype(BF16)
    to_mp(jg.at[c, m], jg.at[c, m], JM)
    gp_s[...] = jnp.sum(hidden * js * dscale, axis=0, keepdims=True)
    to_mp(gp_s, gp_r.at[m], GM)
    gp_r[m] = gp_s[...]
    for j in range(3):
        feat_t[j] = jnp.transpose(featg[:, j].reshape(128, 256).astype(F32)).astype(BF16)
    arrived(JM)
    send(jg.at[c], jg.at[c], JS, sib)

    def weight_grad(cc):
        cols = pl.ds(pl.multiple_of(cc * 512, 512), 512)
        for k in range(2):
            rows = jnp.concatenate([jg[cc, zz * 2 + k] for zz in range(8)], axis=0)
            part_cols = pl.ds(pl.multiple_of(cc * 512 + k * 256, 256), 256)
            for j in range(3):
                wg[j, :, part_cols] = jnp.dot(feat_t[j], rows, preferred_element_type=F32).astype(BF16)
        return pltpu.make_async_copy(wg.at[:, :, cols], grad_out.at[:, :, cols], out_sem.at[cc])

    weight_grad(c).start()
    arrived(GM)
    for k in range(2):
        acc = gp_r[k]
        for zz in range(1, 8):
            acc += gp_r[zz * 2 + k]
        gs_s[k] = acc
    send(gs_s, gs_r.at[c], GS, sib)
    gs_r[c] = gs_s[...]
    arrived(JS)
    weight_grad(1 - c).start()
    arrived(GS)
    for k in range(4):
        gain_out[:, k * 256 : k * 256 + 256] = gs_r[k // 2, k % 2]
    for k in range(2):
        half = slice(k * 512, k * 512 + 512)
        pltpu.make_async_copy(wg.at[:, :, half], grad_out.at[:, :, half], out_sem.at[k]).wait()

    for stage in volume:
        sent(stage)
    pltpu.make_async_copy(xd.at[c, pl.ds(0, 15)], xd.at[c, pl.ds(0, 15)], c2s).wait()
    pltpu.make_async_copy(xd.at[c], xd.at[c], c3s).wait()
    pltpu.make_async_copy(r0, r0, r0s).wait()


def shards(features, fc_weight, head, draft_gain, target_gain, teacher_index):
    vmem = pl.BlockSpec(memory_space=pltpu.VMEM)
    hbm = pl.BlockSpec(memory_space=pl.ANY)
    V = pltpu.VMEM
    stat = [V((4, 128), F32), V((16, 4, 128), F32)] * 2
    weight_grad, gain_grad, loss = pl.pallas_call(
        kernel,
        out_shape=(
            jax.ShapeDtypeStruct((3, 256, 1024), BF16),
            jax.ShapeDtypeStruct((1, 1024), F32),
            jax.ShapeDtypeStruct((1, 16), F32),
        ),
        in_specs=[hbm] * 6,
        out_specs=(hbm, vmem, vmem),
        scratch_shapes=[
            V((VOC, D), BF16),
            V((3, 256, 1024), BF16),
            V((8, 3, 16, 256), BF16),
            V((1, 1024), F32),
            V((32, 128), jnp.int32),
            V((2, 16, 16, 256), F32),
            V((16, 16, 256), F32),
            V((16, 16, 256), F32),
            V((16, 16, 256), F32),
            V((2, 8, 16, 16, 256), BF16),
            V((2, 16, 1, 256), F32),
            V((2, 16, 8, 16, 256), BF16),
            V((16, 256), F32),
            V((1, 128), F32),
            V((32, 1, 128), F32),
            V((ROWS, 128), F32),
            V((VOC, 128), F32),
            V((VOC, 128), F32),
            V((VOC, 128), F32),
            V((ROWS, 128), F32),
            *stat,
            *stat,
            V((1, 128), F32), V((16, 1, 128), F32), V((1, 128), F32), V((16, 1, 128), F32),
            V((2, 16, 128, 256), F32),
            V((2, 16, 128, 256), BF16),
            V((16, 128, 256), BF16),
            V((16, 128, 256), BF16),
            V((16, 128, 256), BF16),
            V((8, 16, 256), BF16),
            V((8, 16, 256), BF16),
            V((1, 256), F32),
            V((16, 1, 256), F32),
            V((2, 1, 256), F32),
            V((2, 2, 1, 256), F32),
            V((2, 16, 16, 256), BF16),
            V((3, 256, 128), BF16),
            V((3, 256, 1024), BF16),
            pltpu.SemaphoreType.DMA((7,)),
            pltpu.SemaphoreType.DMA((STAGES,)),
            pltpu.SemaphoreType.DMA((STAGES,)),
            pltpu.SemaphoreType.DMA,
            pltpu.SemaphoreType.DMA((16,)),
            pltpu.SemaphoreType.DMA,
            pltpu.SemaphoreType.DMA,
            pltpu.SemaphoreType.DMA,
            pltpu.SemaphoreType.DMA((8,)),
            pltpu.SemaphoreType.DMA((2,)),
        ],
        compiler_params=pltpu.CompilerParams(
            collective_id=0, has_side_effects=True, vmem_limit_bytes=60 * 2**20
        ),
        cost_estimate=pl.CostEstimate(flops=3_600_000_000, bytes_accessed=12_000_000, transcendentals=200_000),
    )(features, fc_weight, head, draft_gain.reshape(1, 1024), target_gain.reshape(1, 256), teacher_index.T)
    return (weight_grad, gain_grad.reshape(1024), loss.reshape(16))


def solution(mesh):
    return jax.shard_map(
        shards,
        mesh=mesh,
        in_specs=(
            P(None, "dp", ("section", "mp")),
            P(None, ("section", "mp"), "dp"),
            P(("dp", "section", "mp"), None),
            P("dp"),
            P(("section", "mp")),
            P(),
        ),
        out_specs=(P(None, ("section", "mp"), "dp"), P("dp"), P("dp")),
        check_vma=False,
    )
```

```python
import jax
import jax.numpy as jnp
from jax import lax
from jax.experimental import pallas as pl
from jax.experimental.pallas import tpu as pltpu
from jax.sharding import PartitionSpec as P

D = 8192
EPS = 1e-05
VOC = 501
ROWS = 512
LOW = -1e30
F32 = jnp.float32
BF16 = jnp.bfloat16
MESH = pl.DeviceIdType.MESH

(A1, T1, TG, TY, TX, TX2, T3, TGS, B0, B1, S1, C1, U1, U2, V1, V2, W1, W2, R1, R2, GM, GS, JM, JS) = range(24)
STAGES = 24


def kernel(
    feat, fc_hbm, head_hbm, dgain_hbm, tgain_hbm, index_hbm,
    grad_out, gain_out, loss_out,
    head, fc, featg, dgain, index, part, brecv0, bsum, brecv1, xr, tg, xd, joined,
    sq_s, sq_r, mask, lt, ld, placed, grad,
    us1, ur1, us2, ur2, vs1, vr1, vs2, vr2, ws1, wr1, ws2, wr2,
    hf, hb, r0, r1s, r1r, r2s, r2r, gp_s, gp_r, gs_s, gs_r, jg, feat_t, wg,
    load_sem, ssem, rsem, c2s, c2r, c3s, c3r, r0s, r0r, out_sem,
):
    d = lax.axis_index("dp")
    c = lax.axis_index("section")
    m = lax.axis_index("mp")
    z = m // 2
    yh = m % 2
    p = d * 2 + yh
    sib = (d, 1 - c, m)

    loads = [
        pltpu.make_async_copy(src, dst, load_sem.at[k])
        for k, (src, dst) in enumerate((
            (feat, featg.at[d]), (feat.at[2], xr.at[c, d, m]), (tgain_hbm, tg.at[c, m]), (index_hbm, index),
            (dgain_hbm, dgain), (fc_hbm, fc), (head_hbm, head),
        ))
    ]
    for load in loads:
        load.start()
    load_feat, load_high, load_tg, load_index, load_dg, load_fc, load_head = loads

    barrier = pltpu.get_barrier_semaphore()

    @pl.loop(1, 16)
    def _(i):
        pl.semaphore_signal(barrier, inc=1, device_id=(d, c, (m + i) % 16), device_id_type=MESH)

    @pl.loop(1, 32)
    def _(i):
        k = (p * 2 + c + i) % 32
        pl.semaphore_signal(
            barrier, inc=1, device_id=(k // 4, k % 2, z * 2 + k // 2 % 2), device_id_type=MESH
        )

    other = d + 1 - 2 * (d % 2)

    @pl.loop(0, 16)
    def _(i):
        pl.semaphore_signal(barrier, inc=1, device_id=(other, c, (m + i) % 16), device_id_type=MESH)

    pl.semaphore_wait(barrier, 62)

    def send(src, dst, stage, dev):
        pltpu.make_async_remote_copy(
            src_ref=src, dst_ref=dst, send_sem=ssem.at[stage], recv_sem=rsem.at[stage],
            device_id=dev, device_id_type=MESH,
        ).start()

    volume = {
        A1: featg.at[pl.ds(0, 7)], T1: xr.at[c, d, pl.ds(0, 15)], TG: tg.at[c, pl.ds(0, 15)], TY: xr.at[c, d],
        TX: xr.at[c, pl.ds(0, 6), pl.ds(0, 10)],
        TX2: xr.at[c, pl.ds(0, 6), pl.ds(0, 6)], T3: xr.at[c], TGS: tg.at[c], B0: brecv0, B1: bsum.at[pl.ds(0, 15)],
        S1: sq_r.at[pl.ds(0, 31)], C1: xd.at[c, p, pl.ds(0, 7)], U1: ur1.at[pl.ds(0, 15)], U2: ur2.at[pl.ds(0, 15)],
        W1: wr1.at[pl.ds(0, 15)], W2: wr2.at[pl.ds(0, 15)], V1: vr1.at[pl.ds(0, 15)], V2: vr2.at[pl.ds(0, 15)], R1: r1r.at[pl.ds(0, 15)], R2: r2r.at[pl.ds(0, 7)],
        GM: gp_r.at[pl.ds(0, 15)], GS: gs_s, JM: jg.at[c, pl.ds(0, 15)], JS: jg.at[c],
    }

    def arrived(stage):
        pltpu.make_async_copy(volume[stage], volume[stage], rsem.at[stage]).wait()

    def sent(stage):
        pltpu.make_async_copy(volume[stage], volume[stage], ssem.at[stage]).wait()

    def step(i, n):
        return i % 2 * ((i + 1) // 2) + (1 - i % 2) * (n - i // 2)

    def to_mp(src, dst, stage):
        @pl.loop(1, 16)
        def _(i):
            send(src, dst, stage, (d, c, (m + step(i, 16)) % 16))

    def to_dp(src, dst, stage):
        @pl.loop(1, 8)
        def _(i):
            send(src, dst, stage, ((d + step(i, 8)) % 8, c, m))

    def to_dp_both(src, dst, stage):
        @pl.loop(1, 16)
        def _(i):
            k = (d * 2 + c + step(i, 16)) % 16
            send(src, dst, stage, (k // 2, k % 2, m))

    def to_z(src, dst, stage):
        @pl.loop(1, 8)
        def _(i):
            send(src, dst, stage, (d, c, ((z + step(i, 8)) % 8) * 2 + yh))

    def to_plane_both(src, dst, stage):
        @pl.loop(1, 32)
        def _(i):
            k = (p * 2 + c + step(i, 32)) % 32
            send(src, dst, stage, (k // 4, k % 2, z * 2 + k // 2 % 2))

    to_dp(feat, featg.at[d], A1)
    to_mp(feat.at[2], xr.at[c, d, m], T1)

    @pl.loop(0, 16)
    def _(i):
        send(feat.at[2], xr.at[c, d, m], TY, (other, c, (m + step(i, 16)) % 16))

    to_mp(tgain_hbm, tg.at[c, m], TG)

    start = ((d * 2 + c) * 16 + m) * VOC
    load_index.wait()

    @pl.loop(0, ROWS // 64)
    def _(i):
        rows = lax.broadcasted_iota(jnp.int32, (64, 128), 0) + (i * 64 + start)
        hit = rows == index[0:1, :]
        for k in range(1, 32):
            hit = hit | (rows == index[k : k + 1, :])
        hit = hit & (rows < start + VOC)
        mask[pl.ds(pl.multiple_of(i * 64, 64), 64), :] = hit.astype(F32)

    load_fc.wait()
    load_feat.wait()
    arrived(A1)
    for half in range(4):
        cols = slice(half * 256, half * 256 + 256)
        acc = jnp.dot(featg[:, 0].reshape(128, 256), fc[0, :, cols], preferred_element_type=F32)
        for j in (1, 2):
            acc += jnp.dot(featg[:, j].reshape(128, 256), fc[j, :, cols], preferred_element_type=F32)
        for zz in range(8):
            part[half // 2, zz * 2 + half % 2] = acc[zz * 16 : zz * 16 + 16]
    send(part.at[1 - c], brecv0, B0, sib)

    arrived(B0)
    bsum[...] = part[c] + brecv0[...]

    @pl.loop(1, 16)
    def _(i):
        k = (m + step(i, 16)) % 16
        send(bsum.at[k], brecv1.at[m], B1, (d, c, k))

    brecv1[m] = bsum[m]

    load_high.wait()
    arrived(T1)
    arrived(TY)

    def along_x(first, count, stage):
        pair = xr.at[c, pl.ds(d - d % 2, 2), pl.ds(first, count)]

        @pl.loop(1, 4)
        def _(i):
            send(pair, pair, stage, ((d + 2 * i) % 8, c, m))

    along_x(0, 10, TX)
    arrived(B1)
    js = brecv1[0]
    for k in range(1, 16):
        js += brecv1[k]
    joined[...] = js

    eye = lax.broadcasted_iota(jnp.int32, (16, 128), 0) == lax.broadcasted_iota(jnp.int32, (16, 128), 1)

    def as_row(x):
        return jnp.sum(jnp.where(eye, jnp.sum(x, axis=1, keepdims=True), 0.0), axis=0, keepdims=True)

    def as_column(ref):
        return jnp.sum(jnp.where(eye, jnp.sum(ref[...], axis=0), 0.0), axis=1, keepdims=True)

    sq_s[...] = as_row(js * js)
    to_plane_both(sq_s, sq_r.at[p * 2 + c], S1)
    sq_r[p * 2 + c] = sq_s[...]
    along_x(10, 6, TX2)
    arrived(S1)
    dscale = lax.rsqrt(as_column(sq_r) / D + EPS)
    load_dg.wait()
    own_cols = pl.multiple_of((c * 2 + yh) * 256, 256)
    gain = dgain[:, pl.ds(own_cols, 256)]
    xd[c, p, z] = (js * dscale * gain).astype(BF16)
    to_z(xd.at[c, p, z], xd.at[c, p, z], C1)

    load_tg.wait()
    arrived(TG)
    send(tg.at[c], tg.at[c], TGS, sib)

    arrived(C1)

    def c2(i):
        q = (p + step(i, 16)) % 16
        return pltpu.make_async_remote_copy(
            src_ref=xd.at[c, p], dst_ref=xd.at[c, p], send_sem=c2s, recv_sem=c2r.at[p],
            device_id=(q // 2, c, z * 2 + q % 2), device_id_type=MESH,
        )

    def c3(q):
        return pltpu.make_async_remote_copy(
            src_ref=xd.at[c, q], dst_ref=xd.at[c, q], send_sem=c3s, recv_sem=c3r,
            device_id=sib, device_id_type=MESH,
        )

    @pl.loop(1, 16)
    def _(i):
        c2(i).start()

    c3(p).start()
    arrived(TX)
    arrived(TX2)
    send(xr.at[c], xr.at[c], T3, sib)

    arrived(T3)
    arrived(TGS)

    def add_squares(i, acc):
        x = xr[i // 16, :, i % 16].reshape(128, 256).astype(F32)
        x = x * x
        return acc + x[:, :128] + x[:, 128:]

    squares = lax.fori_loop(0, 32, add_squares, jnp.zeros((128, 128), F32))
    tscale = lax.rsqrt(jnp.sum(squares, axis=1, keepdims=True) / D + EPS)

    load_head.wait()
    lt[...] = jnp.zeros_like(lt)

    @pl.loop(0, 8)
    def _(i):
        cc = i // 4
        mm = (i % 4) * 4
        x = jnp.concatenate(
            [
                (xr[cc, :, mm + k].reshape(128, 256).astype(F32) * tscale * tg[cc, mm + k]).astype(BF16)
                for k in range(4)
            ],
            axis=1,
        )
        cols = pl.ds(pl.multiple_of(i * 1024, 1024), 1024)
        lt[...] += lax.dot_general(head[:, cols], x, (((1,), (1,)), ((), ())), preferred_element_type=F32)

    on = mask[0:VOC, :] > 0.5
    logits = jnp.where(on, lt[...], LOW)
    tmax = jnp.max(logits, axis=0, keepdims=True)
    away = logits - tmax
    e = jnp.where(on, jnp.exp(away), 0.0)
    tz = jnp.sum(e, axis=0, keepdims=True)
    tw = jnp.sum(jnp.where(on, e * away, 0.0), axis=0, keepdims=True)

    def rows_of(a, b, w):
        return jnp.concatenate([a, b, w, jnp.zeros((1, 128), F32)], axis=0)

    def merge(ref):
        a = ref[...]
        top = jnp.max(a[:, 0:1, :], axis=0)
        low = a[:, 0:1, :] - top[None]
        f = jnp.exp(low)
        zz = jnp.sum(f * a[:, 1:2, :], axis=0)
        ww = jnp.sum(f * (a[:, 2:3, :] + jnp.where(a[:, 1:2, :] > 0.0, low, 0.0) * a[:, 1:2, :]), axis=0)
        return top, zz, ww

    us1[...] = rows_of(tmax, tz, tw)
    to_mp(us1, ur1.at[m], U1)
    ur1[m] = us1[...]

    @pl.loop(1, 16)
    def _(i):
        q = (p + step(i, 16)) % 16
        pltpu.make_async_copy(xd.at[c, q], xd.at[c, q], c2r.at[q]).wait()
        c3(q).start()

    pltpu.make_async_copy(xd.at[1 - c], xd.at[1 - c], c3r).wait()
    ld[...] = jnp.zeros_like(ld)

    @pl.loop(0, 8)
    def _(i):
        x = jnp.concatenate([xd[k // 2, i * 2 + k % 2].reshape(128, 256) for k in range(4)], axis=1)
        cols = pl.ds(pl.multiple_of(i * 1024, 1024), 1024)
        ld[...] += lax.dot_general(head[:, cols], x, (((1,), (1,)), ((), ())), preferred_element_type=F32)

    logits = ld[...]
    dmax = jnp.max(logits, axis=0, keepdims=True)
    away = logits - dmax
    e = jnp.exp(away)
    dz = jnp.sum(e, axis=0, keepdims=True)
    ds = jnp.sum(e * away, axis=0, keepdims=True)
    vs1[...] = rows_of(dmax, dz, ds)
    to_mp(vs1, vr1.at[m], V1)
    vr1[m] = vs1[...]

    arrived(U1)
    us2[...] = rows_of(*merge(ur1))
    to_dp_both(us2, ur2.at[d * 2 + c], U2)
    ur2[d * 2 + c] = us2[...]

    arrived(V1)
    vs2[...] = rows_of(*merge(vr1))
    to_dp_both(vs2, vr2.at[d * 2 + c], V2)
    vr2[d * 2 + c] = vs2[...]

    arrived(U2)
    tmax, tz, tw = merge(ur2)
    tp = jnp.where(mask[0:VOC, :] > 0.5, jnp.exp(jnp.minimum(lt[...] - tmax, 0.0)) / tz, 0.0)
    placed[...] = tp
    teach = tw / tz - jnp.log(tz)
    ws1[...] = jnp.sum(tp * ld[...], axis=0, keepdims=True)
    to_mp(ws1, wr1.at[m], W1)
    wr1[m] = ws1[...]

    arrived(V2)
    dmax, dz, ds = merge(vr2)
    log_total = dmax + jnp.log(dz)
    g = jnp.exp(ld[...] - log_total) - placed[...]
    grad[...] = jnp.zeros_like(grad)
    grad[0:VOC, :] = g
    grad_rows = jnp.transpose(grad[...])[:, 0:VOC].astype(BF16)

    def r0_copy(dd):
        return pltpu.make_async_remote_copy(
            src_ref=hb.at[1 - c, pl.ds(dd * 2, 2)], dst_ref=r0.at[pl.ds(dd * 2, 2)],
            send_sem=r0s, recv_sem=r0r.at[dd], device_id=sib, device_id_type=MESH,
        )

    def compute(dd):
        for k in range(4):
            cols = pl.ds(pl.multiple_of(dd * 1024 + k * 256, 256), 256)
            h = jnp.dot(grad_rows, head[:, cols], preferred_element_type=F32)
            hf[k // 2, dd * 2 + k % 2] = h
            hb[k // 2, dd * 2 + k % 2] = h.astype(BF16)
        r0_copy(dd).start()

    def add_up(dd):
        pltpu.make_async_copy(r0.at[pl.ds(dd * 2, 2)], r0.at[pl.ds(dd * 2, 2)], r0r.at[dd]).wait()
        for k in range(2):
            q = dd * 2 + k
            r1s[q] = (hf[c, q] + r0[q].astype(F32)).astype(BF16)

    def to_peer(q):
        send(r1s.at[q], r1r.at[p], R1, (q // 2, c, z * 2 + q % 2))

    compute((d + 1) % 8)

    @pl.loop(2, 9)
    def _(i):
        compute((d + step(i, 8) * (1 - i // 8)) % 8)
        dd = (d + step(i - 1, 8)) % 8
        add_up(dd)
        to_peer(dd * 2)
        to_peer(dd * 2 + 1)

    add_up(d)
    to_peer(d * 2 + 1 - yh)
    r1r[p] = r1s[p]
    arrived(W1)
    ws2[...] = jnp.sum(wr1[...], axis=0)
    to_dp_both(ws2, wr2.at[d * 2 + c], W2)
    wr2[d * 2 + c] = ws2[...]
    arrived(R1)
    for zz in range(8):
        acc = r1r[0, zz * 16 : zz * 16 + 16].astype(F32)
        for k in range(1, 16):
            acc += r1r[k, zz * 16 : zz * 16 + 16].astype(F32)
        r2s[zz] = acc.astype(BF16)

    @pl.loop(1, 8)
    def _(i):
        zz = (z + step(i, 8)) % 8
        send(r2s.at[zz], r2r.at[z], R2, (d, c, zz * 2 + yh))

    r2r[z] = r2s[z]
    arrived(W2)
    dw = jnp.sum(wr2[...], axis=0)
    loss = teach - dw + log_total
    moment = ds / dz + (dmax - dw)
    loss_out[...] = pltpu.roll(jnp.broadcast_to(loss, (8, 128)), (128 - d * 16) % 128, 1)[0:1, 0:16]

    arrived(R2)
    hidden = r2r[0].astype(F32)
    for k in range(1, 8):
        hidden += r2r[k].astype(F32)

    js = joined[...]
    weighted = hidden * gain
    own_tokens = lax.broadcasted_iota(jnp.int32, (16, 128), 0) + z * 16 == lax.broadcasted_iota(jnp.int32, (16, 128), 1)
    back = jnp.sum(jnp.where(own_tokens, moment, 0.0), axis=1, keepdims=True)
    jg[c, m] = (dscale * weighted - js * (dscale * dscale * back / D)).astype(BF16)
    to_mp(jg.at[c, m], jg.at[c, m], JM)
    gp_s[...] = jnp.sum(hidden * js * dscale, axis=0, keepdims=True)
    to_mp(gp_s, gp_r.at[m], GM)
    gp_r[m] = gp_s[...]
    for j in range(3):
        feat_t[j] = jnp.transpose(featg[:, j].reshape(128, 256).astype(F32)).astype(BF16)
    arrived(JM)
    send(jg.at[c], jg.at[c], JS, sib)

    def weight_grad(cc):
        cols = pl.ds(pl.multiple_of(cc * 512, 512), 512)
        for k in range(2):
            rows = jnp.concatenate([jg[cc, zz * 2 + k] for zz in range(8)], axis=0)
            part_cols = pl.ds(pl.multiple_of(cc * 512 + k * 256, 256), 256)
            for j in range(3):
                wg[j, :, part_cols] = jnp.dot(feat_t[j], rows, preferred_element_type=F32).astype(BF16)
        return pltpu.make_async_copy(wg.at[:, :, cols], grad_out.at[:, :, cols], out_sem.at[cc])

    weight_grad(c).start()
    arrived(GM)
    for k in range(2):
        acc = gp_r[k]
        for zz in range(1, 8):
            acc += gp_r[zz * 2 + k]
        gs_s[k] = acc
    send(gs_s, gs_r.at[c], GS, sib)
    gs_r[c] = gs_s[...]
    arrived(JS)
    weight_grad(1 - c).start()
    arrived(GS)
    for k in range(4):
        gain_out[:, k * 256 : k * 256 + 256] = gs_r[k // 2, k % 2]
    for k in range(2):
        half = slice(k * 512, k * 512 + 512)
        pltpu.make_async_copy(wg.at[:, :, half], grad_out.at[:, :, half], out_sem.at[k]).wait()

    for stage in volume:
        sent(stage)
    pltpu.make_async_copy(xd.at[c, pl.ds(0, 15)], xd.at[c, pl.ds(0, 15)], c2s).wait()
    pltpu.make_async_copy(xd.at[c], xd.at[c], c3s).wait()
    pltpu.make_async_copy(r0, r0, r0s).wait()


def shards(features, fc_weight, head, draft_gain, target_gain, teacher_index):
    vmem = pl.BlockSpec(memory_space=pltpu.VMEM)
    hbm = pl.BlockSpec(memory_space=pl.ANY)
    V = pltpu.VMEM
    stat = [V((4, 128), F32), V((16, 4, 128), F32)] * 2
    weight_grad, gain_grad, loss = pl.pallas_call(
        kernel,
        out_shape=(
            jax.ShapeDtypeStruct((3, 256, 1024), BF16),
            jax.ShapeDtypeStruct((1, 1024), F32),
            jax.ShapeDtypeStruct((1, 16), F32),
        ),
        in_specs=[hbm] * 6,
        out_specs=(hbm, vmem, vmem),
        scratch_shapes=[
            V((VOC, D), BF16),
            V((3, 256, 1024), BF16),
            V((8, 3, 16, 256), BF16),
            V((1, 1024), F32),
            V((32, 128), jnp.int32),
            V((2, 16, 16, 256), F32),
            V((16, 16, 256), F32),
            V((16, 16, 256), F32),
            V((16, 16, 256), F32),
            V((2, 8, 16, 16, 256), BF16),
            V((2, 16, 1, 256), F32),
            V((2, 16, 8, 16, 256), BF16),
            V((16, 256), F32),
            V((1, 128), F32),
            V((32, 1, 128), F32),
            V((ROWS, 128), F32),
            V((VOC, 128), F32),
            V((VOC, 128), F32),
            V((VOC, 128), F32),
            V((ROWS, 128), F32),
            *stat,
            *stat,
            V((1, 128), F32), V((16, 1, 128), F32), V((1, 128), F32), V((16, 1, 128), F32),
            V((2, 16, 128, 256), F32),
            V((2, 16, 128, 256), BF16),
            V((16, 128, 256), BF16),
            V((16, 128, 256), BF16),
            V((16, 128, 256), BF16),
            V((8, 16, 256), BF16),
            V((8, 16, 256), BF16),
            V((1, 256), F32),
            V((16, 1, 256), F32),
            V((2, 1, 256), F32),
            V((2, 2, 1, 256), F32),
            V((2, 16, 16, 256), BF16),
            V((3, 256, 128), BF16),
            V((3, 256, 1024), BF16),
            pltpu.SemaphoreType.DMA((7,)),
            pltpu.SemaphoreType.DMA((STAGES,)),
            pltpu.SemaphoreType.DMA((STAGES,)),
            pltpu.SemaphoreType.DMA,
            pltpu.SemaphoreType.DMA((16,)),
            pltpu.SemaphoreType.DMA,
            pltpu.SemaphoreType.DMA,
            pltpu.SemaphoreType.DMA,
            pltpu.SemaphoreType.DMA((8,)),
            pltpu.SemaphoreType.DMA((2,)),
        ],
        compiler_params=pltpu.CompilerParams(
            collective_id=0, has_side_effects=True, vmem_limit_bytes=60 * 2**20
        ),
        cost_estimate=pl.CostEstimate(flops=3_600_000_000, bytes_accessed=12_000_000, transcendentals=200_000),
    )(features, fc_weight, head, draft_gain.reshape(1, 1024), target_gain.reshape(1, 256), teacher_index.T)
    return (weight_grad, gain_grad.reshape(1024), loss.reshape(16))


def solution(mesh):
    return jax.shard_map(
        shards,
        mesh=mesh,
        in_specs=(
            P(None, "dp", ("section", "mp")),
            P(None, ("section", "mp"), "dp"),
            P(("dp", "section", "mp"), None),
            P("dp"),
            P(("section", "mp")),
            P(),
        ),
        out_specs=(P(None, ("section", "mp"), "dp"), P("dp"), P("dp")),
        check_vma=False,
    )
```

```python
import jax
import jax.numpy as jnp
from jax import lax
from jax.experimental import pallas as pl
from jax.experimental.pallas import tpu as pltpu
from jax.sharding import PartitionSpec as P

D = 8192
EPS = 1e-05
VOC = 501
ROWS = 512
LOW = -1e30
F32 = jnp.float32
BF16 = jnp.bfloat16
MESH = pl.DeviceIdType.MESH

(A1, T1, TG, TY, TX, TX2, T3, TGS, B0, B1, S1, C1, U1, U2, V1, V2, W1, W2, R1, R2, GM, GS, JM, JS, LX, LY, LXY, LYX) = range(28)
STAGES = 28


def kernel(
    feat, fc_hbm, head_hbm, dgain_hbm, tgain_hbm, index_hbm,
    grad_out, gain_out, loss_out,
    head, fc, featg, dgain, index, part, brecv0, bsum, brecv1, xr, tg, xd, joined,
    sq_s, sq_r, mask, lt, ld, placed, grad,
    us1, ur1, us2, ur2, vs1, vr1, vs2, vr2, ws1, wr1, ws2, wr2,
    hf, hb, r0, r1s, r1r, r2s, r2r, gp_s, gp_r, gs_s, gs_r, jg, feat_t, wg,
    load_sem, ssem, rsem, c2r, c3s, c3r, r0s, r0r, out_sem,
):
    d = lax.axis_index("dp")
    c = lax.axis_index("section")
    m = lax.axis_index("mp")
    z = m // 2
    yh = m % 2
    p = d * 2 + yh
    px = d // 2
    py = d % 2 * 2 + yh
    sib = (d, 1 - c, m)

    loads = [
        pltpu.make_async_copy(src, dst, load_sem.at[k])
        for k, (src, dst) in enumerate((
            (feat, featg.at[d]), (feat.at[2], xr.at[c, d, m]), (tgain_hbm, tg.at[c, m]), (index_hbm, index),
            (dgain_hbm, dgain), (fc_hbm, fc), (head_hbm, head),
        ))
    ]
    for load in loads:
        load.start()
    load_feat, load_high, load_tg, load_index, load_dg, load_fc, load_head = loads

    barrier = pltpu.get_barrier_semaphore()

    @pl.loop(1, 16)
    def _(i):
        pl.semaphore_signal(barrier, inc=1, device_id=(d, c, (m + i) % 16), device_id_type=MESH)

    @pl.loop(1, 32)
    def _(i):
        k = (p * 2 + c + i) % 32
        pl.semaphore_signal(
            barrier, inc=1, device_id=(k // 4, k % 2, z * 2 + k // 2 % 2), device_id_type=MESH
        )

    other = d + 1 - 2 * (d % 2)

    @pl.loop(0, 16)
    def _(i):
        pl.semaphore_signal(barrier, inc=1, device_id=(other, c, (m + i) % 16), device_id_type=MESH)

    pl.semaphore_wait(barrier, 62)

    def send(src, dst, stage, dev):
        pltpu.make_async_remote_copy(
            src_ref=src, dst_ref=dst, send_sem=ssem.at[stage], recv_sem=rsem.at[stage],
            device_id=dev, device_id_type=MESH,
        ).start()

    volume = {
        A1: featg.at[pl.ds(0, 7)], T1: xr.at[c, d, pl.ds(0, 15)], TG: tg.at[c, pl.ds(0, 15)], TY: xr.at[c, d],
        TX: xr.at[c, pl.ds(0, 6), pl.ds(0, 10)],
        TX2: xr.at[c, pl.ds(0, 6), pl.ds(0, 6)], T3: xr.at[c], TGS: tg.at[c], B0: brecv0, B1: bsum.at[pl.ds(0, 15)],
        S1: sq_r.at[pl.ds(0, 31)], C1: xd.at[:, c, px, py, pl.ds(0, 7)],
        LX: xd.at[0, c, pl.ds(0, 3), py], LY: xd.at[1, c, px, pl.ds(0, 3)], LXY: xd.at[0, c, pl.ds(0, 3)], LYX: xd.at[1, c, pl.ds(0, 3)],
        U1: ur1.at[pl.ds(0, 7)], U2: ur2.at[pl.ds(0, 31)],
        W1: wr1.at[pl.ds(0, 15)], W2: wr2.at[pl.ds(0, 15)], V1: vr1.at[pl.ds(0, 7)], V2: vr2.at[pl.ds(0, 31)], R1: r1r.at[pl.ds(0, 15)], R2: r2r.at[pl.ds(0, 7)],
        GM: gp_r.at[pl.ds(0, 15)], GS: gs_s, JM: jg.at[c, pl.ds(0, 15)], JS: jg.at[c],
    }

    def arrived(stage):
        pltpu.make_async_copy(volume[stage], volume[stage], rsem.at[stage]).wait()

    def sent(stage):
        pltpu.make_async_copy(volume[stage], volume[stage], ssem.at[stage]).wait()

    def step(i, n):
        return i % 2 * ((i + 1) // 2) + (1 - i % 2) * (n - i // 2)

    def to_mp(src, dst, stage):
        @pl.loop(1, 16)
        def _(i):
            send(src, dst, stage, (d, c, (m + step(i, 16)) % 16))

    def to_dp(src, dst, stage):
        @pl.loop(1, 8)
        def _(i):
            send(src, dst, stage, ((d + step(i, 8)) % 8, c, m))

    def to_dp_both(src, dst, stage):
        @pl.loop(1, 16)
        def _(i):
            k = (d * 2 + c + step(i, 16)) % 16
            send(src, dst, stage, (k // 2, k % 2, m))

    def to_z(src, dst, stage):
        @pl.loop(1, 8)
        def _(i):
            send(src, dst, stage, (d, c, ((z + step(i, 8)) % 8) * 2 + yh))

    def to_plane_both(src, dst, stage):
        @pl.loop(1, 32)
        def _(i):
            k = (p * 2 + c + step(i, 32)) % 32
            send(src, dst, stage, (k // 4, k % 2, z * 2 + k // 2 % 2))

    to_dp(feat, featg.at[d], A1)
    to_mp(feat.at[2], xr.at[c, d, m], T1)

    @pl.loop(0, 16)
    def _(i):
        send(feat.at[2], xr.at[c, d, m], TY, (other, c, (m + step(i, 16)) % 16))

    to_mp(tgain_hbm, tg.at[c, m], TG)

    start = ((d * 2 + c) * 16 + m) * VOC
    load_index.wait()

    @pl.loop(0, ROWS // 64)
    def _(i):
        rows = lax.broadcasted_iota(jnp.int32, (64, 128), 0) + (i * 64 + start)
        hit = rows == index[0:1, :]
        for k in range(1, 32):
            hit = hit | (rows == index[k : k + 1, :])
        hit = hit & (rows < start + VOC)
        mask[pl.ds(pl.multiple_of(i * 64, 64), 64), :] = hit.astype(F32)

    load_fc.wait()
    load_feat.wait()
    arrived(A1)
    for half in range(4):
        cols = slice(half * 256, half * 256 + 256)
        acc = jnp.dot(featg[:, 0].reshape(128, 256), fc[0, :, cols], preferred_element_type=F32)
        for j in (1, 2):
            acc += jnp.dot(featg[:, j].reshape(128, 256), fc[j, :, cols], preferred_element_type=F32)
        for zz in range(8):
            part[half // 2, zz * 2 + half % 2] = acc[zz * 16 : zz * 16 + 16]
    send(part.at[1 - c], brecv0, B0, sib)

    arrived(B0)
    bsum[...] = part[c] + brecv0[...]

    @pl.loop(1, 16)
    def _(i):
        k = (m + step(i, 16)) % 16
        send(bsum.at[k], brecv1.at[m], B1, (d, c, k))

    brecv1[m] = bsum[m]

    load_high.wait()
    arrived(T1)
    arrived(TY)

    def along_x(first, count, stage):
        pair = xr.at[c, pl.ds(d - d % 2, 2), pl.ds(first, count)]

        @pl.loop(1, 4)
        def _(i):
            send(pair, pair, stage, ((d + 2 * i) % 8, c, m))

    along_x(0, 10, TX)
    arrived(B1)
    js = brecv1[0]
    for k in range(1, 16):
        js += brecv1[k]
    joined[...] = js

    eye = lax.broadcasted_iota(jnp.int32, (16, 128), 0) == lax.broadcasted_iota(jnp.int32, (16, 128), 1)

    def as_row(x):
        return jnp.sum(jnp.where(eye, jnp.sum(x, axis=1, keepdims=True), 0.0), axis=0, keepdims=True)

    def as_column(ref):
        return jnp.sum(jnp.where(eye, jnp.sum(ref[...], axis=0), 0.0), axis=1, keepdims=True)

    sq_s[...] = as_row(js * js)
    to_plane_both(sq_s, sq_r.at[p * 2 + c], S1)
    sq_r[p * 2 + c] = sq_s[...]
    along_x(10, 6, TX2)
    arrived(S1)
    dscale = lax.rsqrt(as_column(sq_r) / D + EPS)
    load_dg.wait()
    own_cols = pl.multiple_of((c * 2 + yh) * 256, 256)
    gain = dgain[:, pl.ds(own_cols, 256)]
    normed = (js * dscale * gain).astype(BF16)
    xd[0, c, px, py, z] = normed[:, :128]
    xd[1, c, px, py, z] = normed[:, 128:]
    to_z(xd.at[:, c, px, py, z], xd.at[:, c, px, py, z], C1)

    load_tg.wait()
    arrived(TG)
    send(tg.at[c], tg.at[c], TGS, sib)

    arrived(C1)

    def at_x(i):
        return ((px + i) % 4 * 2 + d % 2, c, m)

    def at_y(i):
        k = (py + i) % 4
        return (px * 2 + k // 2, c, z * 2 + k % 2)

    for i in (1, 3, 2):
        send(xd.at[0, c, px, py], xd.at[0, c, px, py], LX, at_x(i))
        send(xd.at[1, c, px, py], xd.at[1, c, px, py], LY, at_y(i))

    def line(half, k):
        return xd.at[0, c, :, k] if half == 0 else xd.at[1, c, k]

    def second(half, i):
        own = line(half, (py, px)[half])
        return pltpu.make_async_remote_copy(
            src_ref=own, dst_ref=own, send_sem=ssem.at[(LXY, LYX)[half]], recv_sem=c2r.at[half * 4 + (py, px)[half]],
            device_id=(at_y, at_x)[half](i), device_id_type=MESH,
        )

    def c3(half, k):
        return pltpu.make_async_remote_copy(
            src_ref=line(half, k), dst_ref=line(half, k), send_sem=c3s, recv_sem=c3r,
            device_id=sib, device_id_type=MESH,
        )

    arrived(TX)
    arrived(TX2)
    send(xr.at[c], xr.at[c], T3, sib)
    for half in range(2):
        arrived((LX, LY)[half])
        for i in (1, 3, 2):
            second(half, i).start()
    for half in range(2):
        c3(half, (py, px)[half]).start()

    arrived(T3)
    arrived(TGS)

    def add_squares(i, acc):
        x = xr[i // 16, :, i % 16].reshape(128, 256).astype(F32)
        x = x * x
        return acc + x[:, :128] + x[:, 128:]

    squares = lax.fori_loop(0, 32, add_squares, jnp.zeros((128, 128), F32))
    tscale = lax.rsqrt(jnp.sum(squares, axis=1, keepdims=True) / D + EPS)

    load_head.wait()
    lt[...] = jnp.zeros_like(lt)

    @pl.loop(0, 8)
    def _(i):
        cc = i // 4
        mm = (i % 4) * 4
        x = jnp.concatenate(
            [
                (xr[cc, :, mm + k].reshape(128, 256).astype(F32) * tscale * tg[cc, mm + k]).astype(BF16)
                for k in range(4)
            ],
            axis=1,
        )
        cols = pl.ds(pl.multiple_of(i * 1024, 1024), 1024)
        lt[...] += lax.dot_general(head[:, cols], x, (((1,), (1,)), ((), ())), preferred_element_type=F32)

    on = mask[0:VOC, :] > 0.5
    logits = jnp.where(on, lt[...], LOW)
    tmax = jnp.max(logits, axis=0, keepdims=True)
    away = logits - tmax
    e = jnp.where(on, jnp.exp(away), 0.0)
    tz = jnp.sum(e, axis=0, keepdims=True)
    tw = jnp.sum(jnp.where(on, e * away, 0.0), axis=0, keepdims=True)

    def rows_of(a, b, w):
        return jnp.concatenate([a, b, w, jnp.zeros((1, 128), F32)], axis=0)

    def merge(ref):
        a = ref[...]
        top = jnp.max(a[:, 0:1, :], axis=0)
        low = a[:, 0:1, :] - top[None]
        f = jnp.exp(low)
        zz = jnp.sum(f * a[:, 1:2, :], axis=0)
        ww = jnp.sum(f * (a[:, 2:3, :] + jnp.where(a[:, 1:2, :] > 0.0, low, 0.0) * a[:, 1:2, :]), axis=0)
        return top, zz, ww

    us1[...] = rows_of(tmax, tz, tw)
    to_z(us1, ur1.at[z], U1)
    ur1[z] = us1[...]

    for i in (1, 3, 2):
        for half in range(2):
            k = ((py, px)[half] + i) % 4
            pltpu.make_async_copy(line(half, k), line(half, k), c2r.at[half * 4 + k]).wait()
            c3(half, k).start()

    pltpu.make_async_copy(xd.at[:, 1 - c], xd.at[:, 1 - c], c3r).wait()
    ld[...] = jnp.zeros_like(ld)

    @pl.loop(0, 8)
    def _(i):
        x = jnp.concatenate(
            [xd[h, k // 2, i // 2, i % 2 * 2 + k % 2].reshape(128, 128) for k in range(4) for h in range(2)], axis=1
        )
        cols = pl.ds(pl.multiple_of(i * 1024, 1024), 1024)
        ld[...] += lax.dot_general(head[:, cols], x, (((1,), (1,)), ((), ())), preferred_element_type=F32)

    logits = ld[...]
    dmax = jnp.max(logits, axis=0, keepdims=True)
    away = logits - dmax
    e = jnp.exp(away)
    dz = jnp.sum(e, axis=0, keepdims=True)
    ds = jnp.sum(e * away, axis=0, keepdims=True)
    vs1[...] = rows_of(dmax, dz, ds)
    to_z(vs1, vr1.at[z], V1)
    vr1[z] = vs1[...]

    arrived(U1)
    us2[...] = rows_of(*merge(ur1))
    to_plane_both(us2, ur2.at[p * 2 + c], U2)
    ur2[p * 2 + c] = us2[...]

    arrived(V1)
    vs2[...] = rows_of(*merge(vr1))
    to_plane_both(vs2, vr2.at[p * 2 + c], V2)
    vr2[p * 2 + c] = vs2[...]

    arrived(U2)
    tmax, tz, tw = merge(ur2)
    tp = jnp.where(mask[0:VOC, :] > 0.5, jnp.exp(jnp.minimum(lt[...] - tmax, 0.0)) / tz, 0.0)
    placed[...] = tp
    teach = tw / tz - jnp.log(tz)
    ws1[...] = jnp.sum(tp * ld[...], axis=0, keepdims=True)
    to_mp(ws1, wr1.at[m], W1)
    wr1[m] = ws1[...]

    arrived(V2)
    dmax, dz, ds = merge(vr2)
    log_total = dmax + jnp.log(dz)
    g = jnp.exp(ld[...] - log_total) - placed[...]
    grad[...] = jnp.zeros_like(grad)
    grad[0:VOC, :] = g
    grad_rows = jnp.transpose(grad[...])[:, 0:VOC].astype(BF16)

    def r0_copy(dd):
        return pltpu.make_async_remote_copy(
            src_ref=hb.at[1 - c, pl.ds(dd * 2, 2)], dst_ref=r0.at[pl.ds(dd * 2, 2)],
            send_sem=r0s, recv_sem=r0r.at[dd], device_id=sib, device_id_type=MESH,
        )

    def compute(dd):
        for k in range(4):
            cols = pl.ds(pl.multiple_of(dd * 1024 + k * 256, 256), 256)
            h = jnp.dot(grad_rows, head[:, cols], preferred_element_type=F32)
            hf[k // 2, dd * 2 + k % 2] = h
            hb[k // 2, dd * 2 + k % 2] = h.astype(BF16)
        r0_copy(dd).start()

    def add_up(dd):
        pltpu.make_async_copy(r0.at[pl.ds(dd * 2, 2)], r0.at[pl.ds(dd * 2, 2)], r0r.at[dd]).wait()
        for k in range(2):
            q = dd * 2 + k
            r1s[q] = (hf[c, q] + r0[q].astype(F32)).astype(BF16)

    def to_peer(q):
        send(r1s.at[q], r1r.at[p], R1, (q // 2, c, z * 2 + q % 2))

    compute((d + 1) % 8)

    @pl.loop(2, 9)
    def _(i):
        compute((d + step(i, 8) * (1 - i // 8)) % 8)
        dd = (d + step(i - 1, 8)) % 8
        add_up(dd)
        to_peer(dd * 2)
        to_peer(dd * 2 + 1)

    add_up(d)
    to_peer(d * 2 + 1 - yh)
    r1r[p] = r1s[p]
    arrived(W1)
    ws2[...] = jnp.sum(wr1[...], axis=0)
    to_dp_both(ws2, wr2.at[d * 2 + c], W2)
    wr2[d * 2 + c] = ws2[...]
    arrived(R1)
    for zz in range(8):
        acc = r1r[0, zz * 16 : zz * 16 + 16].astype(F32)
        for k in range(1, 16):
            acc += r1r[k, zz * 16 : zz * 16 + 16].astype(F32)
        r2s[zz] = acc.astype(BF16)

    @pl.loop(1, 8)
    def _(i):
        zz = (z + step(i, 8)) % 8
        send(r2s.at[zz], r2r.at[z], R2, (d, c, zz * 2 + yh))

    r2r[z] = r2s[z]
    arrived(W2)
    dw = jnp.sum(wr2[...], axis=0)
    loss = teach - dw + log_total
    moment = ds / dz + (dmax - dw)
    loss_out[...] = pltpu.roll(jnp.broadcast_to(loss, (8, 128)), (128 - d * 16) % 128, 1)[0:1, 0:16]

    arrived(R2)
    hidden = r2r[0].astype(F32)
    for k in range(1, 8):
        hidden += r2r[k].astype(F32)

    js = joined[...]
    weighted = hidden * gain
    own_tokens = lax.broadcasted_iota(jnp.int32, (16, 128), 0) + z * 16 == lax.broadcasted_iota(jnp.int32, (16, 128), 1)
    back = jnp.sum(jnp.where(own_tokens, moment, 0.0), axis=1, keepdims=True)
    jg[c, m] = (dscale * weighted - js * (dscale * dscale * back / D)).astype(BF16)
    to_mp(jg.at[c, m], jg.at[c, m], JM)
    gp_s[...] = jnp.sum(hidden * js * dscale, axis=0, keepdims=True)
    to_mp(gp_s, gp_r.at[m], GM)
    gp_r[m] = gp_s[...]
    for j in range(3):
        feat_t[j] = jnp.transpose(featg[:, j].reshape(128, 256).astype(F32)).astype(BF16)
    arrived(JM)
    send(jg.at[c], jg.at[c], JS, sib)

    def weight_grad(cc):
        cols = pl.ds(pl.multiple_of(cc * 512, 512), 512)
        for k in range(2):
            rows = jnp.concatenate([jg[cc, zz * 2 + k] for zz in range(8)], axis=0)
            part_cols = pl.ds(pl.multiple_of(cc * 512 + k * 256, 256), 256)
            for j in range(3):
                wg[j, :, part_cols] = jnp.dot(feat_t[j], rows, preferred_element_type=F32).astype(BF16)
        return pltpu.make_async_copy(wg.at[:, :, cols], grad_out.at[:, :, cols], out_sem.at[cc])

    weight_grad(c).start()
    arrived(GM)
    for k in range(2):
        acc = gp_r[k]
        for zz in range(1, 8):
            acc += gp_r[zz * 2 + k]
        gs_s[k] = acc
    send(gs_s, gs_r.at[c], GS, sib)
    gs_r[c] = gs_s[...]
    arrived(JS)
    weight_grad(1 - c).start()
    arrived(GS)
    for k in range(4):
        gain_out[:, k * 256 : k * 256 + 256] = gs_r[k // 2, k % 2]
    for k in range(2):
        half = slice(k * 512, k * 512 + 512)
        pltpu.make_async_copy(wg.at[:, :, half], grad_out.at[:, :, half], out_sem.at[k]).wait()

    for stage in volume:
        sent(stage)
    pltpu.make_async_copy(xd.at[:, c], xd.at[:, c], c3s).wait()
    pltpu.make_async_copy(r0, r0, r0s).wait()


def shards(features, fc_weight, head, draft_gain, target_gain, teacher_index):
    vmem = pl.BlockSpec(memory_space=pltpu.VMEM)
    hbm = pl.BlockSpec(memory_space=pl.ANY)
    V = pltpu.VMEM
    stat = [V((4, 128), F32), V((8, 4, 128), F32), V((4, 128), F32), V((32, 4, 128), F32)]
    weight_grad, gain_grad, loss = pl.pallas_call(
        kernel,
        out_shape=(
            jax.ShapeDtypeStruct((3, 256, 1024), BF16),
            jax.ShapeDtypeStruct((1, 1024), F32),
            jax.ShapeDtypeStruct((1, 16), F32),
        ),
        in_specs=[hbm] * 6,
        out_specs=(hbm, vmem, vmem),
        scratch_shapes=[
            V((VOC, D), BF16),
            V((3, 256, 1024), BF16),
            V((8, 3, 16, 256), BF16),
            V((1, 1024), F32),
            V((32, 128), jnp.int32),
            V((2, 16, 16, 256), F32),
            V((16, 16, 256), F32),
            V((16, 16, 256), F32),
            V((16, 16, 256), F32),
            V((2, 8, 16, 16, 256), BF16),
            V((2, 16, 1, 256), F32),
            V((2, 2, 4, 4, 8, 16, 128), BF16),
            V((16, 256), F32),
            V((1, 128), F32),
            V((32, 1, 128), F32),
            V((ROWS, 128), F32),
            V((VOC, 128), F32),
            V((VOC, 128), F32),
            V((VOC, 128), F32),
            V((ROWS, 128), F32),
            *stat,
            *stat,
            V((1, 128), F32), V((16, 1, 128), F32), V((1, 128), F32), V((16, 1, 128), F32),
            V((2, 16, 128, 256), F32),
            V((2, 16, 128, 256), BF16),
            V((16, 128, 256), BF16),
            V((16, 128, 256), BF16),
            V((16, 128, 256), BF16),
            V((8, 16, 256), BF16),
            V((8, 16, 256), BF16),
            V((1, 256), F32),
            V((16, 1, 256), F32),
            V((2, 1, 256), F32),
            V((2, 2, 1, 256), F32),
            V((2, 16, 16, 256), BF16),
            V((3, 256, 128), BF16),
            V((3, 256, 1024), BF16),
            pltpu.SemaphoreType.DMA((7,)),
            pltpu.SemaphoreType.DMA((STAGES,)),
            pltpu.SemaphoreType.DMA((STAGES,)),
            pltpu.SemaphoreType.DMA((8,)),
            pltpu.SemaphoreType.DMA,
            pltpu.SemaphoreType.DMA,
            pltpu.SemaphoreType.DMA,
            pltpu.SemaphoreType.DMA((8,)),
            pltpu.SemaphoreType.DMA((2,)),
        ],
        compiler_params=pltpu.CompilerParams(
            collective_id=0, has_side_effects=True, vmem_limit_bytes=60 * 2**20
        ),
        cost_estimate=pl.CostEstimate(flops=3_600_000_000, bytes_accessed=12_000_000, transcendentals=200_000),
    )(features, fc_weight, head, draft_gain.reshape(1, 1024), target_gain.reshape(1, 256), teacher_index.T)
    return (weight_grad, gain_grad.reshape(1024), loss.reshape(16))


def solution(mesh):
    return jax.shard_map(
        shards,
        mesh=mesh,
        in_specs=(
            P(None, "dp", ("section", "mp")),
            P(None, ("section", "mp"), "dp"),
            P(("dp", "section", "mp"), None),
            P("dp"),
            P(("section", "mp")),
            P(),
        ),
        out_specs=(P(None, ("section", "mp"), "dp"), P("dp"), P("dp")),
        check_vma=False,
    )
```

```python
import jax
import jax.numpy as jnp
from jax import lax
from jax.experimental import pallas as pl
from jax.experimental.pallas import tpu as pltpu
from jax.sharding import PartitionSpec as P

D = 8192
EPS = 1e-05
VOC = 501
ROWS = 512
LOW = -1e30
F32 = jnp.float32
BF16 = jnp.bfloat16
MESH = pl.DeviceIdType.MESH

(A1, T1, TG, TY, TX, TX2, T3, TGS, B0, B1, S1, C1, U1, U2, V1, V2, W1, W2, RY, RX, RYX, RXY, R2, GM, GS, JM, JS, LX, LY, LXY, LYX) = range(31)
STAGES = 31


def kernel(
    feat, fc_hbm, head_hbm, dgain_hbm, tgain_hbm, index_hbm,
    grad_out, gain_out, loss_out,
    head, fc, featg, dgain, index, part, brecv0, bsum, brecv1, xr, tg, xd, joined,
    sq_s, sq_r, mask, lt, ld, placed, grad,
    us1, ur1, us2, ur2, vs1, vr1, vs2, vr2, ws1, wr1, ws2, wr2,
    hf, hb, r0, r1s, ra, rb_s, rb_r, r2s, r2r, gp_s, gp_r, gs_s, gs_r, jg, feat_t, wg,
    load_sem, ssem, rsem, c2r, c3s, c3r, r0s, r0r, out_sem,
):
    d = lax.axis_index("dp")
    c = lax.axis_index("section")
    m = lax.axis_index("mp")
    z = m // 2
    yh = m % 2
    p = d * 2 + yh
    px = d // 2
    py = d % 2 * 2 + yh
    sib = (d, 1 - c, m)

    loads = [
        pltpu.make_async_copy(src, dst, load_sem.at[k])
        for k, (src, dst) in enumerate((
            (feat, featg.at[d]), (feat.at[2], xr.at[c, d, m]), (tgain_hbm, tg.at[c, m]), (index_hbm, index),
            (dgain_hbm, dgain), (fc_hbm, fc), (head_hbm, head),
        ))
    ]
    for load in loads:
        load.start()
    load_feat, load_high, load_tg, load_index, load_dg, load_fc, load_head = loads

    barrier = pltpu.get_barrier_semaphore()

    @pl.loop(1, 16)
    def _(i):
        pl.semaphore_signal(barrier, inc=1, device_id=(d, c, (m + i) % 16), device_id_type=MESH)

    @pl.loop(1, 32)
    def _(i):
        k = (p * 2 + c + i) % 32
        pl.semaphore_signal(
            barrier, inc=1, device_id=(k // 4, k % 2, z * 2 + k // 2 % 2), device_id_type=MESH
        )

    other = d + 1 - 2 * (d % 2)

    @pl.loop(0, 16)
    def _(i):
        pl.semaphore_signal(barrier, inc=1, device_id=(other, c, (m + i) % 16), device_id_type=MESH)

    pl.semaphore_wait(barrier, 62)

    def send(src, dst, stage, dev):
        pltpu.make_async_remote_copy(
            src_ref=src, dst_ref=dst, send_sem=ssem.at[stage], recv_sem=rsem.at[stage],
            device_id=dev, device_id_type=MESH,
        ).start()

    volume = {
        A1: featg.at[pl.ds(0, 7)], T1: xr.at[c, d, pl.ds(0, 15)], TG: tg.at[c, pl.ds(0, 15)], TY: xr.at[c, d],
        TX: xr.at[c, pl.ds(0, 6), pl.ds(0, 10)],
        TX2: xr.at[c, pl.ds(0, 6), pl.ds(0, 6)], T3: xr.at[c], TGS: tg.at[c], B0: brecv0, B1: bsum.at[pl.ds(0, 15)],
        S1: sq_r.at[pl.ds(0, 31)], C1: xd.at[:, c, px, py, pl.ds(0, 7)],
        LX: xd.at[0, c, pl.ds(0, 3), py], LY: xd.at[1, c, px, pl.ds(0, 3)], LXY: xd.at[0, c, pl.ds(0, 3)], LYX: xd.at[1, c, pl.ds(0, 3)],
        U1: ur1.at[pl.ds(0, 7)], U2: ur2.at[pl.ds(0, 31)],
        W1: wr1.at[pl.ds(0, 15)], W2: wr2.at[pl.ds(0, 15)], V1: vr1.at[pl.ds(0, 7)], V2: vr2.at[pl.ds(0, 31)], RY: ra.at[0, pl.ds(0, 3)], RX: ra.at[1, pl.ds(0, 3)],
        RYX: rb_r.at[0, pl.ds(0, 3)], RXY: rb_r.at[1, pl.ds(0, 3)], R2: r2r.at[pl.ds(0, 7)],
        GM: gp_r.at[pl.ds(0, 15)], GS: gs_s, JM: jg.at[c, pl.ds(0, 15)], JS: jg.at[c],
    }

    def arrived(stage):
        pltpu.make_async_copy(volume[stage], volume[stage], rsem.at[stage]).wait()

    def sent(stage):
        pltpu.make_async_copy(volume[stage], volume[stage], ssem.at[stage]).wait()

    def step(i, n):
        return i % 2 * ((i + 1) // 2) + (1 - i % 2) * (n - i // 2)

    def to_mp(src, dst, stage):
        @pl.loop(1, 16)
        def _(i):
            send(src, dst, stage, (d, c, (m + step(i, 16)) % 16))

    def to_dp(src, dst, stage):
        @pl.loop(1, 8)
        def _(i):
            send(src, dst, stage, ((d + step(i, 8)) % 8, c, m))

    def to_dp_both(src, dst, stage):
        @pl.loop(1, 16)
        def _(i):
            k = (d * 2 + c + step(i, 16)) % 16
            send(src, dst, stage, (k // 2, k % 2, m))

    def to_z(src, dst, stage):
        @pl.loop(1, 8)
        def _(i):
            send(src, dst, stage, (d, c, ((z + step(i, 8)) % 8) * 2 + yh))

    def to_plane_both(src, dst, stage):
        @pl.loop(1, 32)
        def _(i):
            k = (p * 2 + c + step(i, 32)) % 32
            send(src, dst, stage, (k // 4, k % 2, z * 2 + k // 2 % 2))

    to_dp(feat, featg.at[d], A1)
    to_mp(feat.at[2], xr.at[c, d, m], T1)

    @pl.loop(0, 16)
    def _(i):
        send(feat.at[2], xr.at[c, d, m], TY, (other, c, (m + step(i, 16)) % 16))

    to_mp(tgain_hbm, tg.at[c, m], TG)

    start = ((d * 2 + c) * 16 + m) * VOC
    load_index.wait()

    @pl.loop(0, ROWS // 64)
    def _(i):
        rows = lax.broadcasted_iota(jnp.int32, (64, 128), 0) + (i * 64 + start)
        hit = rows == index[0:1, :]
        for k in range(1, 32):
            hit = hit | (rows == index[k : k + 1, :])
        hit = hit & (rows < start + VOC)
        mask[pl.ds(pl.multiple_of(i * 64, 64), 64), :] = hit.astype(F32)

    load_fc.wait()
    load_feat.wait()
    arrived(A1)
    for half in range(4):
        cols = slice(half * 256, half * 256 + 256)
        acc = jnp.dot(featg[:, 0].reshape(128, 256), fc[0, :, cols], preferred_element_type=F32)
        for j in (1, 2):
            acc += jnp.dot(featg[:, j].reshape(128, 256), fc[j, :, cols], preferred_element_type=F32)
        for zz in range(8):
            part[half // 2, zz * 2 + half % 2] = acc[zz * 16 : zz * 16 + 16]
    send(part.at[1 - c], brecv0, B0, sib)

    arrived(B0)
    bsum[...] = part[c] + brecv0[...]

    @pl.loop(1, 16)
    def _(i):
        k = (m + step(i, 16)) % 16
        send(bsum.at[k], brecv1.at[m], B1, (d, c, k))

    brecv1[m] = bsum[m]

    load_high.wait()
    arrived(T1)
    arrived(TY)

    def along_x(first, count, stage):
        pair = xr.at[c, pl.ds(d - d % 2, 2), pl.ds(first, count)]

        @pl.loop(1, 4)
        def _(i):
            send(pair, pair, stage, ((d + 2 * i) % 8, c, m))

    along_x(0, 10, TX)
    arrived(B1)
    js = brecv1[0]
    for k in range(1, 16):
        js += brecv1[k]
    joined[...] = js

    eye = lax.broadcasted_iota(jnp.int32, (16, 128), 0) == lax.broadcasted_iota(jnp.int32, (16, 128), 1)

    def as_row(x):
        return jnp.sum(jnp.where(eye, jnp.sum(x, axis=1, keepdims=True), 0.0), axis=0, keepdims=True)

    def as_column(ref):
        return jnp.sum(jnp.where(eye, jnp.sum(ref[...], axis=0), 0.0), axis=1, keepdims=True)

    sq_s[...] = as_row(js * js)
    to_plane_both(sq_s, sq_r.at[p * 2 + c], S1)
    sq_r[p * 2 + c] = sq_s[...]
    along_x(10, 6, TX2)
    arrived(S1)
    dscale = lax.rsqrt(as_column(sq_r) / D + EPS)
    load_dg.wait()
    own_cols = pl.multiple_of((c * 2 + yh) * 256, 256)
    gain = dgain[:, pl.ds(own_cols, 256)]
    normed = (js * dscale * gain).astype(BF16)
    xd[0, c, px, py, z] = normed[:, :128]
    xd[1, c, px, py, z] = normed[:, 128:]
    to_z(xd.at[:, c, px, py, z], xd.at[:, c, px, py, z], C1)

    load_tg.wait()
    arrived(TG)
    send(tg.at[c], tg.at[c], TGS, sib)

    arrived(C1)

    def at_x(i):
        return ((px + i) % 4 * 2 + d % 2, c, m)

    def at_y(i):
        k = (py + i) % 4
        return (px * 2 + k // 2, c, z * 2 + k % 2)

    for i in (1, 3, 2):
        send(xd.at[0, c, px, py], xd.at[0, c, px, py], LX, at_x(i))
        send(xd.at[1, c, px, py], xd.at[1, c, px, py], LY, at_y(i))

    def line(half, k):
        return xd.at[0, c, :, k] if half == 0 else xd.at[1, c, k]

    def second(half, i):
        own = line(half, (py, px)[half])
        return pltpu.make_async_remote_copy(
            src_ref=own, dst_ref=own, send_sem=ssem.at[(LXY, LYX)[half]], recv_sem=c2r.at[half * 4 + (py, px)[half]],
            device_id=(at_y, at_x)[half](i), device_id_type=MESH,
        )

    def c3(half, k):
        return pltpu.make_async_remote_copy(
            src_ref=line(half, k), dst_ref=line(half, k), send_sem=c3s, recv_sem=c3r,
            device_id=sib, device_id_type=MESH,
        )

    arrived(TX)
    arrived(TX2)
    send(xr.at[c], xr.at[c], T3, sib)
    for half in range(2):
        arrived((LX, LY)[half])
        for i in (1, 3, 2):
            second(half, i).start()
    for half in range(2):
        c3(half, (py, px)[half]).start()

    arrived(T3)
    arrived(TGS)

    def add_squares(i, acc):
        x = xr[i // 16, :, i % 16].reshape(128, 256).astype(F32)
        x = x * x
        return acc + x[:, :128] + x[:, 128:]

    squares = lax.fori_loop(0, 32, add_squares, jnp.zeros((128, 128), F32))
    tscale = lax.rsqrt(jnp.sum(squares, axis=1, keepdims=True) / D + EPS)

    load_head.wait()
    lt[...] = jnp.zeros_like(lt)

    @pl.loop(0, 8)
    def _(i):
        cc = i // 4
        mm = (i % 4) * 4
        x = jnp.concatenate(
            [
                (xr[cc, :, mm + k].reshape(128, 256).astype(F32) * tscale * tg[cc, mm + k]).astype(BF16)
                for k in range(4)
            ],
            axis=1,
        )
        cols = pl.ds(pl.multiple_of(i * 1024, 1024), 1024)
        lt[...] += lax.dot_general(head[:, cols], x, (((1,), (1,)), ((), ())), preferred_element_type=F32)

    on = mask[0:VOC, :] > 0.5
    logits = jnp.where(on, lt[...], LOW)
    tmax = jnp.max(logits, axis=0, keepdims=True)
    away = logits - tmax
    e = jnp.where(on, jnp.exp(away), 0.0)
    tz = jnp.sum(e, axis=0, keepdims=True)
    tw = jnp.sum(jnp.where(on, e * away, 0.0), axis=0, keepdims=True)

    def rows_of(a, b, w):
        return jnp.concatenate([a, b, w, jnp.zeros((1, 128), F32)], axis=0)

    def merge(ref):
        a = ref[...]
        top = jnp.max(a[:, 0:1, :], axis=0)
        low = a[:, 0:1, :] - top[None]
        f = jnp.exp(low)
        zz = jnp.sum(f * a[:, 1:2, :], axis=0)
        ww = jnp.sum(f * (a[:, 2:3, :] + jnp.where(a[:, 1:2, :] > 0.0, low, 0.0) * a[:, 1:2, :]), axis=0)
        return top, zz, ww

    us1[...] = rows_of(tmax, tz, tw)
    to_z(us1, ur1.at[z], U1)
    ur1[z] = us1[...]

    for i in (1, 3, 2):
        for half in range(2):
            k = ((py, px)[half] + i) % 4
            pltpu.make_async_copy(line(half, k), line(half, k), c2r.at[half * 4 + k]).wait()
            c3(half, k).start()

    pltpu.make_async_copy(xd.at[:, 1 - c], xd.at[:, 1 - c], c3r).wait()
    ld[...] = jnp.zeros_like(ld)

    @pl.loop(0, 8)
    def _(i):
        x = jnp.concatenate(
            [xd[h, k // 2, i // 2, i % 2 * 2 + k % 2].reshape(128, 128) for k in range(4) for h in range(2)], axis=1
        )
        cols = pl.ds(pl.multiple_of(i * 1024, 1024), 1024)
        ld[...] += lax.dot_general(head[:, cols], x, (((1,), (1,)), ((), ())), preferred_element_type=F32)

    logits = ld[...]
    dmax = jnp.max(logits, axis=0, keepdims=True)
    away = logits - dmax
    e = jnp.exp(away)
    dz = jnp.sum(e, axis=0, keepdims=True)
    ds = jnp.sum(e * away, axis=0, keepdims=True)
    vs1[...] = rows_of(dmax, dz, ds)
    to_z(vs1, vr1.at[z], V1)
    vr1[z] = vs1[...]

    arrived(U1)
    us2[...] = rows_of(*merge(ur1))
    to_plane_both(us2, ur2.at[p * 2 + c], U2)
    ur2[p * 2 + c] = us2[...]

    arrived(V1)
    vs2[...] = rows_of(*merge(vr1))
    to_plane_both(vs2, vr2.at[p * 2 + c], V2)
    vr2[p * 2 + c] = vs2[...]

    arrived(U2)
    tmax, tz, tw = merge(ur2)
    tp = jnp.where(mask[0:VOC, :] > 0.5, jnp.exp(jnp.minimum(lt[...] - tmax, 0.0)) / tz, 0.0)
    placed[...] = tp
    teach = tw / tz - jnp.log(tz)
    ws1[...] = jnp.sum(tp * ld[...], axis=0, keepdims=True)
    to_mp(ws1, wr1.at[m], W1)
    wr1[m] = ws1[...]

    arrived(V2)
    dmax, dz, ds = merge(vr2)
    log_total = dmax + jnp.log(dz)
    g = jnp.exp(ld[...] - log_total) - placed[...]
    grad[...] = jnp.zeros_like(grad)
    grad[0:VOC, :] = g
    grad_rows = jnp.transpose(grad[...])[:, 0:VOC].astype(BF16)

    def r0_copy(dd):
        return pltpu.make_async_remote_copy(
            src_ref=hb.at[1 - c, pl.ds(dd * 2, 2)], dst_ref=r0.at[pl.ds(dd * 2, 2)],
            send_sem=r0s, recv_sem=r0r.at[dd], device_id=sib, device_id_type=MESH,
        )

    def compute(dd):
        for k in range(4):
            cols = pl.ds(pl.multiple_of(dd * 1024 + k * 256, 256), 256)
            h = jnp.dot(grad_rows, head[:, cols], preferred_element_type=F32)
            hf[k // 2, dd * 2 + k % 2] = h
            hb[k // 2, dd * 2 + k % 2] = h.astype(BF16)
        r0_copy(dd).start()

    def add_up(dd):
        pltpu.make_async_copy(r0.at[pl.ds(dd * 2, 2)], r0.at[pl.ds(dd * 2, 2)], r0r.at[dd]).wait()
        for k in range(2):
            q = dd * 2 + k
            total = (hf[c, q] + r0[q].astype(F32)).astype(BF16)
            r1s[0, dd // 2, dd % 2 * 2 + k] = total[:, :128]
            r1s[1, dd // 2, dd % 2 * 2 + k] = total[:, 128:]

    def to_lines(dd):
        x = dd // 2
        for k in range(2):
            y = dd % 2 * 2 + k

            @pl.when(y != py)
            def _():
                send(r1s.at[0, x, y], ra.at[0, py, x], RY, (px * 2 + y // 2, c, z * 2 + k))

            @pl.when(x != px)
            def _():
                send(r1s.at[1, x, y], ra.at[1, px, y], RX, (x * 2 + d % 2, c, m))

    compute((d + 1) % 8)

    @pl.loop(2, 9)
    def _(i):
        compute((d + step(i, 8) * (1 - i // 8)) % 8)
        dd = (d + step(i - 1, 8)) % 8
        add_up(dd)
        to_lines(dd)

    add_up(d)
    to_lines(d)
    ra[0, py] = r1s[0, :, py]
    ra[1, px] = r1s[1, px]
    arrived(W1)
    ws2[...] = jnp.sum(wr1[...], axis=0)
    to_dp_both(ws2, wr2.at[d * 2 + c], W2)
    wr2[d * 2 + c] = ws2[...]
    for half in range(2):
        arrived((RY, RX)[half])
        for k in range(4):
            acc = ra[half, 0, k].astype(F32)
            for i in range(1, 4):
                acc += ra[half, i, k].astype(F32)
            rb_s[half, k] = acc.astype(BF16)
        own = (px, py)[half]
        for i in (1, 3, 2):
            send(rb_s.at[half, (own + i) % 4], rb_r.at[half, own], (RYX, RXY)[half], (at_x, at_y)[half](i))
        rb_r[half, own] = rb_s[half, own]
    for half in range(2):
        arrived((RYX, RXY)[half])
        for zz in range(8):
            rows = slice(zz * 16, zz * 16 + 16)
            acc = rb_r[half, 0, rows].astype(F32)
            for i in range(1, 4):
                acc += rb_r[half, i, rows].astype(F32)
            r2s[zz, :, half * 128 : half * 128 + 128] = acc.astype(BF16)

    @pl.loop(1, 8)
    def _(i):
        zz = (z + step(i, 8)) % 8
        send(r2s.at[zz], r2r.at[z], R2, (d, c, zz * 2 + yh))

    r2r[z] = r2s[z]
    arrived(W2)
    dw = jnp.sum(wr2[...], axis=0)
    loss = teach - dw + log_total
    moment = ds / dz + (dmax - dw)
    loss_out[...] = pltpu.roll(jnp.broadcast_to(loss, (8, 128)), (128 - d * 16) % 128, 1)[0:1, 0:16]

    arrived(R2)
    hidden = r2r[0].astype(F32)
    for k in range(1, 8):
        hidden += r2r[k].astype(F32)

    js = joined[...]
    weighted = hidden * gain
    own_tokens = lax.broadcasted_iota(jnp.int32, (16, 128), 0) + z * 16 == lax.broadcasted_iota(jnp.int32, (16, 128), 1)
    back = jnp.sum(jnp.where(own_tokens, moment, 0.0), axis=1, keepdims=True)
    jg[c, m] = (dscale * weighted - js * (dscale * dscale * back / D)).astype(BF16)
    to_mp(jg.at[c, m], jg.at[c, m], JM)
    gp_s[...] = jnp.sum(hidden * js * dscale, axis=0, keepdims=True)
    to_mp(gp_s, gp_r.at[m], GM)
    gp_r[m] = gp_s[...]
    for j in range(3):
        feat_t[j] = jnp.transpose(featg[:, j].reshape(128, 256).astype(F32)).astype(BF16)
    arrived(JM)
    send(jg.at[c], jg.at[c], JS, sib)

    def weight_grad(cc):
        cols = pl.ds(pl.multiple_of(cc * 512, 512), 512)
        for k in range(2):
            rows = jnp.concatenate([jg[cc, zz * 2 + k] for zz in range(8)], axis=0)
            part_cols = pl.ds(pl.multiple_of(cc * 512 + k * 256, 256), 256)
            for j in range(3):
                wg[j, :, part_cols] = jnp.dot(feat_t[j], rows, preferred_element_type=F32).astype(BF16)
        return pltpu.make_async_copy(wg.at[:, :, cols], grad_out.at[:, :, cols], out_sem.at[cc])

    weight_grad(c).start()
    arrived(GM)
    for k in range(2):
        acc = gp_r[k]
        for zz in range(1, 8):
            acc += gp_r[zz * 2 + k]
        gs_s[k] = acc
    send(gs_s, gs_r.at[c], GS, sib)
    gs_r[c] = gs_s[...]
    arrived(JS)
    weight_grad(1 - c).start()
    arrived(GS)
    for k in range(4):
        gain_out[:, k * 256 : k * 256 + 256] = gs_r[k // 2, k % 2]
    for k in range(2):
        half = slice(k * 512, k * 512 + 512)
        pltpu.make_async_copy(wg.at[:, :, half], grad_out.at[:, :, half], out_sem.at[k]).wait()

    for stage in volume:
        sent(stage)
    pltpu.make_async_copy(xd.at[:, c], xd.at[:, c], c3s).wait()
    pltpu.make_async_copy(r0, r0, r0s).wait()


def shards(features, fc_weight, head, draft_gain, target_gain, teacher_index):
    vmem = pl.BlockSpec(memory_space=pltpu.VMEM)
    hbm = pl.BlockSpec(memory_space=pl.ANY)
    V = pltpu.VMEM
    stat = [V((4, 128), F32), V((8, 4, 128), F32), V((4, 128), F32), V((32, 4, 128), F32)]
    weight_grad, gain_grad, loss = pl.pallas_call(
        kernel,
        out_shape=(
            jax.ShapeDtypeStruct((3, 256, 1024), BF16),
            jax.ShapeDtypeStruct((1, 1024), F32),
            jax.ShapeDtypeStruct((1, 16), F32),
        ),
        in_specs=[hbm] * 6,
        out_specs=(hbm, vmem, vmem),
        scratch_shapes=[
            V((VOC, D), BF16),
            V((3, 256, 1024), BF16),
            V((8, 3, 16, 256), BF16),
            V((1, 1024), F32),
            V((32, 128), jnp.int32),
            V((2, 16, 16, 256), F32),
            V((16, 16, 256), F32),
            V((16, 16, 256), F32),
            V((16, 16, 256), F32),
            V((2, 8, 16, 16, 256), BF16),
            V((2, 16, 1, 256), F32),
            V((2, 2, 4, 4, 8, 16, 128), BF16),
            V((16, 256), F32),
            V((1, 128), F32),
            V((32, 1, 128), F32),
            V((ROWS, 128), F32),
            V((VOC, 128), F32),
            V((VOC, 128), F32),
            V((VOC, 128), F32),
            V((ROWS, 128), F32),
            *stat,
            *stat,
            V((1, 128), F32), V((16, 1, 128), F32), V((1, 128), F32), V((16, 1, 128), F32),
            V((2, 16, 128, 256), F32),
            V((2, 16, 128, 256), BF16),
            V((16, 128, 256), BF16),
            V((2, 4, 4, 128, 128), BF16),
            V((2, 4, 4, 128, 128), BF16),
            V((2, 4, 128, 128), BF16),
            V((2, 4, 128, 128), BF16),
            V((8, 16, 256), BF16),
            V((8, 16, 256), BF16),
            V((1, 256), F32),
            V((16, 1, 256), F32),
            V((2, 1, 256), F32),
            V((2, 2, 1, 256), F32),
            V((2, 16, 16, 256), BF16),
            V((3, 256, 128), BF16),
            V((3, 256, 1024), BF16),
            pltpu.SemaphoreType.DMA((7,)),
            pltpu.SemaphoreType.DMA((STAGES,)),
            pltpu.SemaphoreType.DMA((STAGES,)),
            pltpu.SemaphoreType.DMA((8,)),
            pltpu.SemaphoreType.DMA,
            pltpu.SemaphoreType.DMA,
            pltpu.SemaphoreType.DMA,
            pltpu.SemaphoreType.DMA((8,)),
            pltpu.SemaphoreType.DMA((2,)),
        ],
        compiler_params=pltpu.CompilerParams(
            collective_id=0, has_side_effects=True, vmem_limit_bytes=60 * 2**20
        ),
        cost_estimate=pl.CostEstimate(flops=3_600_000_000, bytes_accessed=12_000_000, transcendentals=200_000),
    )(features, fc_weight, head, draft_gain.reshape(1, 1024), target_gain.reshape(1, 256), teacher_index.T)
    return (weight_grad, gain_grad.reshape(1024), loss.reshape(16))


def solution(mesh):
    return jax.shard_map(
        shards,
        mesh=mesh,
        in_specs=(
            P(None, "dp", ("section", "mp")),
            P(None, ("section", "mp"), "dp"),
            P(("dp", "section", "mp"), None),
            P("dp"),
            P(("section", "mp")),
            P(),
        ),
        out_specs=(P(None, ("section", "mp"), "dp"), P("dp"), P("dp")),
        check_vma=False,
    )
```

```python
import jax
import jax.numpy as jnp
from jax import lax
from jax.experimental import pallas as pl
from jax.experimental.pallas import tpu as pltpu
from jax.sharding import PartitionSpec as P

D = 8192
EPS = 1e-05
VOC = 501
ROWS = 512
LOW = -1e30
F32 = jnp.float32
BF16 = jnp.bfloat16
MESH = pl.DeviceIdType.MESH

(A1, T1, TG, TY, TX, TX2, T3, TGS, B0, B1, S1, C1, U1, U2, V1, V2, W1, W2, RY, RX, RYX, RXY, R2, GM, GS, JM, JS, LX, LY, LXY, LYX, T3B) = range(32)
STAGES = 32


def kernel(
    feat, fc_hbm, head_hbm, dgain_hbm, tgain_hbm, index_hbm,
    grad_out, gain_out, loss_out,
    head, fc, featg, dgain, index, part, brecv0, bsum, brecv1, xr, tg, xd, joined,
    sq_s, sq_r, mask, lt, ld, placed, grad,
    us1, ur1, us2, ur2, vs1, vr1, vs2, vr2, ws1, wr1, ws2, wr2,
    hf, hb, r0, r1s, ra, rb_s, rb_r, r2s, r2r, gp_s, gp_r, gs_s, gs_r, jg, feat_t, wg,
    load_sem, ssem, rsem, c2r, c3s, c3r, r0s, r0r, out_sem,
):
    d = lax.axis_index("dp")
    c = lax.axis_index("section")
    m = lax.axis_index("mp")
    z = m // 2
    yh = m % 2
    p = d * 2 + yh
    px = d // 2
    py = d % 2 * 2 + yh
    sib = (d, 1 - c, m)

    loads = [
        pltpu.make_async_copy(src, dst, load_sem.at[k])
        for k, (src, dst) in enumerate((
            (feat, featg.at[d]), (feat.at[2], xr.at[c, d, m]), (tgain_hbm, tg.at[c, m]), (index_hbm, index),
            (dgain_hbm, dgain), (fc_hbm, fc), (head_hbm, head),
        ))
    ]
    for load in loads:
        load.start()
    load_feat, load_high, load_tg, load_index, load_dg, load_fc, load_head = loads

    barrier = pltpu.get_barrier_semaphore()

    @pl.loop(1, 16)
    def _(i):
        pl.semaphore_signal(barrier, inc=1, device_id=(d, c, (m + i) % 16), device_id_type=MESH)

    @pl.loop(1, 32)
    def _(i):
        k = (p * 2 + c + i) % 32
        pl.semaphore_signal(
            barrier, inc=1, device_id=(k // 4, k % 2, z * 2 + k // 2 % 2), device_id_type=MESH
        )

    other = d + 1 - 2 * (d % 2)

    @pl.loop(0, 16)
    def _(i):
        pl.semaphore_signal(barrier, inc=1, device_id=(other, c, (m + i) % 16), device_id_type=MESH)

    pl.semaphore_wait(barrier, 62)

    def send(src, dst, stage, dev):
        pltpu.make_async_remote_copy(
            src_ref=src, dst_ref=dst, send_sem=ssem.at[stage], recv_sem=rsem.at[stage],
            device_id=dev, device_id_type=MESH,
        ).start()

    volume = {
        A1: featg.at[pl.ds(0, 7)], T1: xr.at[c, d, pl.ds(0, 15)], TG: tg.at[c, pl.ds(0, 15)], TY: xr.at[c, d],
        TX: xr.at[c, pl.ds(0, 6), pl.ds(0, 10)],
        TX2: xr.at[c, pl.ds(0, 6), pl.ds(0, 6)], T3: xr.at[c, :, pl.ds(0, 10)], T3B: xr.at[c, :, pl.ds(10, 6)], TGS: tg.at[c], B0: brecv0, B1: bsum.at[pl.ds(0, 15)],
        S1: sq_r.at[pl.ds(0, 31)], C1: xd.at[:, c, px, py, pl.ds(0, 7)],
        LX: xd.at[0, c, pl.ds(0, 3), py], LY: xd.at[1, c, px, pl.ds(0, 3)], LXY: xd.at[0, c, pl.ds(0, 3)], LYX: xd.at[1, c, pl.ds(0, 3)],
        U1: ur1.at[pl.ds(0, 7)], U2: ur2.at[pl.ds(0, 31)],
        W1: wr1.at[pl.ds(0, 15)], W2: wr2.at[pl.ds(0, 15)], V1: vr1.at[pl.ds(0, 7)], V2: vr2.at[pl.ds(0, 31)], RY: ra.at[0, pl.ds(0, 3)], RX: ra.at[1, pl.ds(0, 3)],
        RYX: rb_r.at[0, pl.ds(0, 3)], RXY: rb_r.at[1, pl.ds(0, 3)], R2: r2r.at[pl.ds(0, 7)],
        GM: gp_r.at[pl.ds(0, 15)], GS: gs_s, JM: jg.at[c, pl.ds(0, 15)], JS: jg.at[c],
    }

    def arrived(stage):
        pltpu.make_async_copy(volume[stage], volume[stage], rsem.at[stage]).wait()

    def sent(stage):
        pltpu.make_async_copy(volume[stage], volume[stage], ssem.at[stage]).wait()

    def step(i, n):
        return i % 2 * ((i + 1) // 2) + (1 - i % 2) * (n - i // 2)

    def to_mp(src, dst, stage):
        @pl.loop(1, 16)
        def _(i):
            send(src, dst, stage, (d, c, (m + step(i, 16)) % 16))

    def to_dp(src, dst, stage):
        @pl.loop(1, 8)
        def _(i):
            send(src, dst, stage, ((d + step(i, 8)) % 8, c, m))

    def to_dp_both(src, dst, stage):
        @pl.loop(1, 16)
        def _(i):
            k = (d * 2 + c + step(i, 16)) % 16
            send(src, dst, stage, (k // 2, k % 2, m))

    def to_z(src, dst, stage):
        @pl.loop(1, 8)
        def _(i):
            send(src, dst, stage, (d, c, ((z + step(i, 8)) % 8) * 2 + yh))

    def to_plane_both(src, dst, stage):
        @pl.loop(1, 32)
        def _(i):
            k = (p * 2 + c + step(i, 32)) % 32
            send(src, dst, stage, (k // 4, k % 2, z * 2 + k // 2 % 2))

    to_dp(feat, featg.at[d], A1)
    to_mp(feat.at[2], xr.at[c, d, m], T1)

    @pl.loop(0, 16)
    def _(i):
        send(feat.at[2], xr.at[c, d, m], TY, (other, c, (m + step(i, 16)) % 16))

    to_mp(tgain_hbm, tg.at[c, m], TG)

    start = ((d * 2 + c) * 16 + m) * VOC
    load_index.wait()

    @pl.loop(0, ROWS // 64)
    def _(i):
        rows = lax.broadcasted_iota(jnp.int32, (64, 128), 0) + (i * 64 + start)
        hit = rows == index[0:1, :]
        for k in range(1, 32):
            hit = hit | (rows == index[k : k + 1, :])
        hit = hit & (rows < start + VOC)
        mask[pl.ds(pl.multiple_of(i * 64, 64), 64), :] = hit.astype(F32)

    load_fc.wait()
    load_feat.wait()
    arrived(A1)
    for half in range(4):
        cols = slice(half * 256, half * 256 + 256)
        acc = jnp.dot(featg[:, 0].reshape(128, 256), fc[0, :, cols], preferred_element_type=F32)
        for j in (1, 2):
            acc += jnp.dot(featg[:, j].reshape(128, 256), fc[j, :, cols], preferred_element_type=F32)
        for zz in range(8):
            part[half // 2, zz * 2 + half % 2] = acc[zz * 16 : zz * 16 + 16]
    send(part.at[1 - c], brecv0, B0, sib)

    arrived(B0)
    bsum[...] = part[c] + brecv0[...]

    @pl.loop(1, 16)
    def _(i):
        k = (m + step(i, 16)) % 16
        send(bsum.at[k], brecv1.at[m], B1, (d, c, k))

    brecv1[m] = bsum[m]

    load_high.wait()
    arrived(T1)
    arrived(TY)

    def along_x(first, count, stage):
        pair = xr.at[c, pl.ds(d - d % 2, 2), pl.ds(first, count)]

        @pl.loop(1, 4)
        def _(i):
            send(pair, pair, stage, ((d + 2 * i) % 8, c, m))

    along_x(0, 10, TX)
    arrived(B1)
    js = brecv1[0]
    for k in range(1, 16):
        js += brecv1[k]
    joined[...] = js

    eye = lax.broadcasted_iota(jnp.int32, (16, 128), 0) == lax.broadcasted_iota(jnp.int32, (16, 128), 1)

    def as_row(x):
        return jnp.sum(jnp.where(eye, jnp.sum(x, axis=1, keepdims=True), 0.0), axis=0, keepdims=True)

    def as_column(ref):
        return jnp.sum(jnp.where(eye, jnp.sum(ref[...], axis=0), 0.0), axis=1, keepdims=True)

    sq_s[...] = as_row(js * js)
    to_plane_both(sq_s, sq_r.at[p * 2 + c], S1)
    sq_r[p * 2 + c] = sq_s[...]
    along_x(10, 6, TX2)
    arrived(S1)
    dscale = lax.rsqrt(as_column(sq_r) / D + EPS)
    load_dg.wait()
    own_cols = pl.multiple_of((c * 2 + yh) * 256, 256)
    gain = dgain[:, pl.ds(own_cols, 256)]
    normed = (js * dscale * gain).astype(BF16)
    xd[0, c, px, py, z] = normed[:, :128]
    xd[1, c, px, py, z] = normed[:, 128:]
    to_z(xd.at[:, c, px, py, z], xd.at[:, c, px, py, z], C1)

    load_tg.wait()
    arrived(TG)
    send(tg.at[c], tg.at[c], TGS, sib)
    arrived(TX)
    send(xr.at[c, :, pl.ds(0, 10)], xr.at[c, :, pl.ds(0, 10)], T3, sib)

    arrived(C1)

    def at_x(i):
        return ((px + i) % 4 * 2 + d % 2, c, m)

    def at_y(i):
        k = (py + i) % 4
        return (px * 2 + k // 2, c, z * 2 + k % 2)

    for i in (1, 3, 2):
        send(xd.at[0, c, px, py], xd.at[0, c, px, py], LX, at_x(i))
        send(xd.at[1, c, px, py], xd.at[1, c, px, py], LY, at_y(i))

    def line(half, k):
        return xd.at[0, c, :, k] if half == 0 else xd.at[1, c, k]

    def second(half, i):
        own = line(half, (py, px)[half])
        return pltpu.make_async_remote_copy(
            src_ref=own, dst_ref=own, send_sem=ssem.at[(LXY, LYX)[half]], recv_sem=c2r.at[half * 4 + (py, px)[half]],
            device_id=(at_y, at_x)[half](i), device_id_type=MESH,
        )

    def c3(half, k):
        return pltpu.make_async_remote_copy(
            src_ref=line(half, k), dst_ref=line(half, k), send_sem=c3s, recv_sem=c3r,
            device_id=sib, device_id_type=MESH,
        )

    arrived(TX2)
    send(xr.at[c, :, pl.ds(10, 6)], xr.at[c, :, pl.ds(10, 6)], T3B, sib)
    for half in range(2):
        arrived((LX, LY)[half])
        for i in (1, 3, 2):
            second(half, i).start()
    for half in range(2):
        c3(half, (py, px)[half]).start()

    arrived(T3)
    arrived(T3B)
    arrived(TGS)

    def add_squares(i, acc):
        x = xr[i // 16, :, i % 16].reshape(128, 256).astype(F32)
        x = x * x
        return acc + x[:, :128] + x[:, 128:]

    squares = lax.fori_loop(0, 32, add_squares, jnp.zeros((128, 128), F32))
    tscale = lax.rsqrt(jnp.sum(squares, axis=1, keepdims=True) / D + EPS)

    load_head.wait()
    lt[...] = jnp.zeros_like(lt)

    @pl.loop(0, 8)
    def _(i):
        cc = i // 4
        mm = (i % 4) * 4
        x = jnp.concatenate(
            [
                (xr[cc, :, mm + k].reshape(128, 256).astype(F32) * tscale * tg[cc, mm + k]).astype(BF16)
                for k in range(4)
            ],
            axis=1,
        )
        cols = pl.ds(pl.multiple_of(i * 1024, 1024), 1024)
        lt[...] += lax.dot_general(head[:, cols], x, (((1,), (1,)), ((), ())), preferred_element_type=F32)

    on = mask[0:VOC, :] > 0.5
    logits = jnp.where(on, lt[...], LOW)
    tmax = jnp.max(logits, axis=0, keepdims=True)
    away = logits - tmax
    e = jnp.where(on, jnp.exp(away), 0.0)
    tz = jnp.sum(e, axis=0, keepdims=True)
    tw = jnp.sum(jnp.where(on, e * away, 0.0), axis=0, keepdims=True)

    def rows_of(a, b, w):
        return jnp.concatenate([a, b, w, jnp.zeros((1, 128), F32)], axis=0)

    def merge(ref):
        a = ref[...]
        top = jnp.max(a[:, 0:1, :], axis=0)
        low = a[:, 0:1, :] - top[None]
        f = jnp.exp(low)
        zz = jnp.sum(f * a[:, 1:2, :], axis=0)
        ww = jnp.sum(f * (a[:, 2:3, :] + jnp.where(a[:, 1:2, :] > 0.0, low, 0.0) * a[:, 1:2, :]), axis=0)
        return top, zz, ww

    us1[...] = rows_of(tmax, tz, tw)
    to_z(us1, ur1.at[z], U1)
    ur1[z] = us1[...]

    for i in (1, 3, 2):
        for half in range(2):
            k = ((py, px)[half] + i) % 4
            pltpu.make_async_copy(line(half, k), line(half, k), c2r.at[half * 4 + k]).wait()
            c3(half, k).start()

    pltpu.make_async_copy(xd.at[:, 1 - c], xd.at[:, 1 - c], c3r).wait()
    ld[...] = jnp.zeros_like(ld)

    @pl.loop(0, 8)
    def _(i):
        x = jnp.concatenate(
            [xd[h, k // 2, i // 2, i % 2 * 2 + k % 2].reshape(128, 128) for k in range(4) for h in range(2)], axis=1
        )
        cols = pl.ds(pl.multiple_of(i * 1024, 1024), 1024)
        ld[...] += lax.dot_general(head[:, cols], x, (((1,), (1,)), ((), ())), preferred_element_type=F32)

    logits = ld[...]
    dmax = jnp.max(logits, axis=0, keepdims=True)
    away = logits - dmax
    e = jnp.exp(away)
    dz = jnp.sum(e, axis=0, keepdims=True)
    ds = jnp.sum(e * away, axis=0, keepdims=True)
    vs1[...] = rows_of(dmax, dz, ds)
    to_z(vs1, vr1.at[z], V1)
    vr1[z] = vs1[...]

    arrived(U1)
    us2[...] = rows_of(*merge(ur1))
    to_plane_both(us2, ur2.at[p * 2 + c], U2)
    ur2[p * 2 + c] = us2[...]

    arrived(V1)
    vs2[...] = rows_of(*merge(vr1))
    to_plane_both(vs2, vr2.at[p * 2 + c], V2)
    vr2[p * 2 + c] = vs2[...]

    arrived(U2)
    tmax, tz, tw = merge(ur2)
    tp = jnp.where(mask[0:VOC, :] > 0.5, jnp.exp(jnp.minimum(lt[...] - tmax, 0.0)) / tz, 0.0)
    placed[...] = tp
    teach = tw / tz - jnp.log(tz)
    ws1[...] = jnp.sum(tp * ld[...], axis=0, keepdims=True)
    to_mp(ws1, wr1.at[m], W1)
    wr1[m] = ws1[...]

    arrived(V2)
    dmax, dz, ds = merge(vr2)
    log_total = dmax + jnp.log(dz)
    g = jnp.exp(ld[...] - log_total) - placed[...]
    grad[...] = jnp.zeros_like(grad)
    grad[0:VOC, :] = g
    grad_rows = jnp.transpose(grad[...])[:, 0:VOC].astype(BF16)

    def r0_copy(dd):
        return pltpu.make_async_remote_copy(
            src_ref=hb.at[1 - c, pl.ds(dd * 2, 2)], dst_ref=r0.at[pl.ds(dd * 2, 2)],
            send_sem=r0s, recv_sem=r0r.at[dd], device_id=sib, device_id_type=MESH,
        )

    def compute(dd):
        for k in range(4):
            cols = pl.ds(pl.multiple_of(dd * 1024 + k * 256, 256), 256)
            h = jnp.dot(grad_rows, head[:, cols], preferred_element_type=F32)
            hf[k // 2, dd * 2 + k % 2] = h
            hb[k // 2, dd * 2 + k % 2] = h.astype(BF16)
        r0_copy(dd).start()

    def add_up(dd):
        pltpu.make_async_copy(r0.at[pl.ds(dd * 2, 2)], r0.at[pl.ds(dd * 2, 2)], r0r.at[dd]).wait()
        for k in range(2):
            q = dd * 2 + k
            total = (hf[c, q] + r0[q].astype(F32)).astype(BF16)
            r1s[0, dd // 2, dd % 2 * 2 + k] = total[:, :128]
            r1s[1, dd // 2, dd % 2 * 2 + k] = total[:, 128:]

    def to_lines(dd):
        x = dd // 2
        for k in range(2):
            y = dd % 2 * 2 + k

            @pl.when(y != py)
            def _():
                send(r1s.at[0, x, y], ra.at[0, py, x], RY, (px * 2 + y // 2, c, z * 2 + k))

            @pl.when(x != px)
            def _():
                send(r1s.at[1, x, y], ra.at[1, px, y], RX, (x * 2 + d % 2, c, m))

    compute((d + 1) % 8)

    @pl.loop(2, 9)
    def _(i):
        compute((d + step(i, 8) * (1 - i // 8)) % 8)
        dd = (d + step(i - 1, 8)) % 8
        add_up(dd)
        to_lines(dd)

    add_up(d)
    to_lines(d)
    ra[0, py] = r1s[0, :, py]
    ra[1, px] = r1s[1, px]
    arrived(W1)
    ws2[...] = jnp.sum(wr1[...], axis=0)
    to_dp_both(ws2, wr2.at[d * 2 + c], W2)
    wr2[d * 2 + c] = ws2[...]
    for half in range(2):
        arrived((RY, RX)[half])
        for k in range(4):
            acc = ra[half, 0, k].astype(F32)
            for i in range(1, 4):
                acc += ra[half, i, k].astype(F32)
            rb_s[half, k] = acc.astype(BF16)
        own = (px, py)[half]
        for i in (1, 3, 2):
            send(rb_s.at[half, (own + i) % 4], rb_r.at[half, own], (RYX, RXY)[half], (at_x, at_y)[half](i))
        rb_r[half, own] = rb_s[half, own]
    for half in range(2):
        arrived((RYX, RXY)[half])
        for zz in range(8):
            rows = slice(zz * 16, zz * 16 + 16)
            acc = rb_r[half, 0, rows].astype(F32)
            for i in range(1, 4):
                acc += rb_r[half, i, rows].astype(F32)
            r2s[zz, :, half * 128 : half * 128 + 128] = acc.astype(BF16)

    @pl.loop(1, 8)
    def _(i):
        zz = (z + step(i, 8)) % 8
        send(r2s.at[zz], r2r.at[z], R2, (d, c, zz * 2 + yh))

    r2r[z] = r2s[z]
    arrived(W2)
    dw = jnp.sum(wr2[...], axis=0)
    loss = teach - dw + log_total
    moment = ds / dz + (dmax - dw)
    loss_out[...] = pltpu.roll(jnp.broadcast_to(loss, (8, 128)), (128 - d * 16) % 128, 1)[0:1, 0:16]

    arrived(R2)
    hidden = r2r[0].astype(F32)
    for k in range(1, 8):
        hidden += r2r[k].astype(F32)

    js = joined[...]
    weighted = hidden * gain
    own_tokens = lax.broadcasted_iota(jnp.int32, (16, 128), 0) + z * 16 == lax.broadcasted_iota(jnp.int32, (16, 128), 1)
    back = jnp.sum(jnp.where(own_tokens, moment, 0.0), axis=1, keepdims=True)
    jg[c, m] = (dscale * weighted - js * (dscale * dscale * back / D)).astype(BF16)
    to_mp(jg.at[c, m], jg.at[c, m], JM)
    gp_s[...] = jnp.sum(hidden * js * dscale, axis=0, keepdims=True)
    to_mp(gp_s, gp_r.at[m], GM)
    gp_r[m] = gp_s[...]
    for j in range(3):
        feat_t[j] = jnp.transpose(featg[:, j].reshape(128, 256).astype(F32)).astype(BF16)
    arrived(JM)
    send(jg.at[c], jg.at[c], JS, sib)

    def weight_grad(cc):
        cols = pl.ds(pl.multiple_of(cc * 512, 512), 512)
        for k in range(2):
            rows = jnp.concatenate([jg[cc, zz * 2 + k] for zz in range(8)], axis=0)
            part_cols = pl.ds(pl.multiple_of(cc * 512 + k * 256, 256), 256)
            for j in range(3):
                wg[j, :, part_cols] = jnp.dot(feat_t[j], rows, preferred_element_type=F32).astype(BF16)
        return pltpu.make_async_copy(wg.at[:, :, cols], grad_out.at[:, :, cols], out_sem.at[cc])

    weight_grad(c).start()
    arrived(GM)
    for k in range(2):
        acc = gp_r[k]
        for zz in range(1, 8):
            acc += gp_r[zz * 2 + k]
        gs_s[k] = acc
    send(gs_s, gs_r.at[c], GS, sib)
    gs_r[c] = gs_s[...]
    arrived(JS)
    weight_grad(1 - c).start()
    arrived(GS)
    for k in range(4):
        gain_out[:, k * 256 : k * 256 + 256] = gs_r[k // 2, k % 2]
    for k in range(2):
        half = slice(k * 512, k * 512 + 512)
        pltpu.make_async_copy(wg.at[:, :, half], grad_out.at[:, :, half], out_sem.at[k]).wait()

    for stage in volume:
        sent(stage)
    pltpu.make_async_copy(xd.at[:, c], xd.at[:, c], c3s).wait()
    pltpu.make_async_copy(r0, r0, r0s).wait()


def shards(features, fc_weight, head, draft_gain, target_gain, teacher_index):
    vmem = pl.BlockSpec(memory_space=pltpu.VMEM)
    hbm = pl.BlockSpec(memory_space=pl.ANY)
    V = pltpu.VMEM
    stat = [V((4, 128), F32), V((8, 4, 128), F32), V((4, 128), F32), V((32, 4, 128), F32)]
    weight_grad, gain_grad, loss = pl.pallas_call(
        kernel,
        out_shape=(
            jax.ShapeDtypeStruct((3, 256, 1024), BF16),
            jax.ShapeDtypeStruct((1, 1024), F32),
            jax.ShapeDtypeStruct((1, 16), F32),
        ),
        in_specs=[hbm] * 6,
        out_specs=(hbm, vmem, vmem),
        scratch_shapes=[
            V((VOC, D), BF16),
            V((3, 256, 1024), BF16),
            V((8, 3, 16, 256), BF16),
            V((1, 1024), F32),
            V((32, 128), jnp.int32),
            V((2, 16, 16, 256), F32),
            V((16, 16, 256), F32),
            V((16, 16, 256), F32),
            V((16, 16, 256), F32),
            V((2, 8, 16, 16, 256), BF16),
            V((2, 16, 1, 256), F32),
            V((2, 2, 4, 4, 8, 16, 128), BF16),
            V((16, 256), F32),
            V((1, 128), F32),
            V((32, 1, 128), F32),
            V((ROWS, 128), F32),
            V((VOC, 128), F32),
            V((VOC, 128), F32),
            V((VOC, 128), F32),
            V((ROWS, 128), F32),
            *stat,
            *stat,
            V((1, 128), F32), V((16, 1, 128), F32), V((1, 128), F32), V((16, 1, 128), F32),
            V((2, 16, 128, 256), F32),
            V((2, 16, 128, 256), BF16),
            V((16, 128, 256), BF16),
            V((2, 4, 4, 128, 128), BF16),
            V((2, 4, 4, 128, 128), BF16),
            V((2, 4, 128, 128), BF16),
            V((2, 4, 128, 128), BF16),
            V((8, 16, 256), BF16),
            V((8, 16, 256), BF16),
            V((1, 256), F32),
            V((16, 1, 256), F32),
            V((2, 1, 256), F32),
            V((2, 2, 1, 256), F32),
            V((2, 16, 16, 256), BF16),
            V((3, 256, 128), BF16),
            V((3, 256, 1024), BF16),
            pltpu.SemaphoreType.DMA((7,)),
            pltpu.SemaphoreType.DMA((STAGES,)),
            pltpu.SemaphoreType.DMA((STAGES,)),
            pltpu.SemaphoreType.DMA((8,)),
            pltpu.SemaphoreType.DMA,
            pltpu.SemaphoreType.DMA,
            pltpu.SemaphoreType.DMA,
            pltpu.SemaphoreType.DMA((8,)),
            pltpu.SemaphoreType.DMA((2,)),
        ],
        compiler_params=pltpu.CompilerParams(
            collective_id=0, has_side_effects=True, vmem_limit_bytes=60 * 2**20
        ),
        cost_estimate=pl.CostEstimate(flops=3_600_000_000, bytes_accessed=12_000_000, transcendentals=200_000),
    )(features, fc_weight, head, draft_gain.reshape(1, 1024), target_gain.reshape(1, 256), teacher_index.T)
    return (weight_grad, gain_grad.reshape(1024), loss.reshape(16))


def solution(mesh):
    return jax.shard_map(
        shards,
        mesh=mesh,
        in_specs=(
            P(None, "dp", ("section", "mp")),
            P(None, ("section", "mp"), "dp"),
            P(("dp", "section", "mp"), None),
            P("dp"),
            P(("section", "mp")),
            P(),
        ),
        out_specs=(P(None, ("section", "mp"), "dp"), P("dp"), P("dp")),
        check_vma=False,
    )
```
